128 devices in a mesh: train: 8 (over y, core), test: 16 (over z, x).
Axes of the slice: x: 4, y: 4, z: 4, core: 2. Of those that a mesh axis runs over, the one named last changes fastest.
Arguments:
- train_features: float32 [16384, 8192], P('train', 'test'), may hold values from -6 to 6
- test_panel: float32 [4096, 1024], P('test', 'train'), may hold values from -6 to 6
- damping: float32 [1024], replicated, may hold values from 0.05 to 1
Outputs:
- scores: float32 [4096, 16384], P('test', 'train')
- panel_factor: float32 [8192, 1024], P('test')
The draws below stay inside these ranges and needn't reach their ends.
All inputs are finite; a program needn't handle non-finite values.
Results may differ from the reference program's by a relative error of at most 0.0002.
Values sent between devices are 32-bit elements; how exact they have to be, the bound alone decides.
No kernel may reach another device: no remote copies, remote signals or barrier semaphores. Data moves between devices by JAX's collectives and lax.ppermute only.
A program may use at most 128 MiB of HBM per device.

```python
import math
import jax
import jax.numpy as jnp
from jax import lax

K = 8192
P_SIZE = 1024
NTR = 16384
NTE = 4096
N_TEST = 16


def shard_levels(stream_key, shape, pieces, low, high):
    level, own = 1.0, jax.random.fold_in(stream_key, 6)
    for position, blocks in pieces:
        steps = jnp.exp(jax.random.uniform(jax.random.fold_in(own, position), (blocks,), jnp.float32, low / len(pieces), high / len(pieces)))
        level = level * jnp.repeat(steps, shape[position] // blocks).reshape([-1 if axis == position else 1 for axis in range(len(shape))])
    return level


def gaussian(own_key, extent, spread, limit, cuts=(), kind=jnp.bfloat16):
    loudness = shard_levels(own_key, extent, cuts, -0.22, 0.18) if cuts else 1.0
    entries = jax.random.normal(own_key, extent, jnp.float32) * spread * loudness
    return jnp.minimum(jnp.maximum(entries, -limit), limit).astype(kind)


def setup_inputs(seed: int = 0) -> dict:
    streams_of = jax.random.split(jax.random.key(seed), 4)
    return {
        "train_features": gaussian(streams_of[0], (NTR, K), 1.0, 6.0, ((0, 8), (1, 16)), jnp.float32),
        "test_panel": gaussian(streams_of[1], (NTE, P_SIZE), 1.0, 6.0, ((0, 16), (1, 8)), jnp.float32),
        "damping": jnp.clip(jnp.exp(jax.random.uniform(streams_of[2], (P_SIZE,), jnp.float32, math.log(0.05), math.log(1.0))), 0.05, 1.0),
    }


def reference(train_features, test_panel, damping):
    highest = lax.Precision.HIGHEST
    train_count = train_features.shape[0]
    shard_width = K // N_TEST
    share_width = P_SIZE // N_TEST
    panel_columns = train_features.reshape(train_count, N_TEST, shard_width)[:, :, :share_width].reshape(train_count, P_SIZE)
    gram = jnp.dot(train_features.T.astype(jnp.float32), panel_columns.astype(jnp.float32), precision=highest, preferred_element_type=jnp.float32) / train_count
    shaped = gram.reshape(N_TEST, shard_width, P_SIZE)
    shaped = shaped.at[:, :share_width, :].add(jnp.diag(damping).reshape(N_TEST, share_width, P_SIZE))
    damped = shaped.reshape(K, P_SIZE)
    diag_block = shaped[:, :share_width, :].reshape(P_SIZE, P_SIZE)
    lower_factor = jnp.linalg.cholesky(diag_block)
    inverse = lax.linalg.triangular_solve(lower_factor, jnp.eye(P_SIZE, dtype=jnp.float32), left_side=True, lower=True)
    panel_factor = jnp.dot(damped.astype(jnp.float32), inverse.T.astype(jnp.float32), precision=highest, preferred_element_type=jnp.float32)
    train_solved = jnp.dot(panel_columns.astype(jnp.float32), inverse.T.astype(jnp.float32), precision=highest, preferred_element_type=jnp.float32)
    test_solved = jnp.dot(test_panel.astype(jnp.float32), inverse.T.astype(jnp.float32), precision=highest, preferred_element_type=jnp.float32)
    scores = jnp.dot(test_solved.astype(jnp.float32), train_solved.T.astype(jnp.float32), precision=highest, preferred_element_type=jnp.float32) / math.sqrt(P_SIZE)
    return (scores, panel_factor)
```

```python
import functools
import math

import jax
import jax.numpy as jnp
from jax import lax
from jax.experimental import pallas as pl
from jax.experimental.pallas import tpu as pltpu
from jax.sharding import PartitionSpec as P

P_SIZE = 1024
BLOCK = 128
F32 = jnp.float32
HIGH = lax.Precision.HIGH
HIGHEST = lax.Precision.HIGHEST


def factor_block(tiles):
    tiles = list(tiles)
    count = len(tiles)
    lane = lax.broadcasted_iota(jnp.int32, (8, BLOCK), 1)
    row = lax.broadcasted_iota(jnp.int32, (8, BLOCK), 0)

    def spread(value):
        return jnp.broadcast_to(value, (8, BLOCK))

    for group in range(count):
        first = 8 * group
        own = tiles[group]
        below = range(group + 1, count)
        columns = [spread(own[:, first + j : first + j + 1]) for j in range(8)]
        pivots = [[spread(columns[j][i : i + 1, :]) for j in range(i + 1)] for i in range(8)]
        inside = (lane >= first) & (lane < first + 8)
        own = jnp.where(inside, (lane - first == row).astype(F32), own)
        lines = [spread(own[i : i + 1, :]) for i in range(8)]
        factors = {m: [spread(tiles[m][:, first + j : first + j + 1]) for j in range(8)] for m in below}
        for m in below:
            tiles[m] = jnp.where(inside, 0.0, tiles[m])
        done = None
        for k in range(8):
            scale = lax.rsqrt(pivots[k][k])
            line = lines[k] * scale
            ratios = {i: pivots[i][k] * scale for i in range(k + 1, 8)}
            for i in range(k + 1, 8):
                for j in range(k + 1, i + 1):
                    pivots[i][j] = pivots[i][j] - ratios[i] * ratios[j]
                lines[i] = lines[i] - ratios[i] * line
            done = line if done is None else jnp.where(row == k, line, done)
            for m in below:
                factor = factors[m][k] * scale
                tiles[m] = tiles[m] - factor * line
                for i in range(k + 1, 8):
                    factors[m][i] = factors[m][i] - factor * ratios[i]
        tiles[group] = done
    return [jnp.where(lane < 8 * group + 8, tiles[group], 0.0) for group in range(count)]


def inverse_factor_kernel(size, core_ref, mine_ref, other_ref, x_ref, inv_ref):
    blocks = size // BLOCK
    strips, half, _ = mine_ref.shape
    core = core_ref[0]
    for strip in range(strips):
        start = 2 * half * strip
        x_ref[pl.ds(pl.multiple_of(start + half * core, half), half), :] = mine_ref[strip]
        x_ref[pl.ds(pl.multiple_of(start + half * (1 - core), half), half), :] = other_ref[strip]

    def step(k, _):
        first = pl.multiple_of(k * BLOCK, BLOCK)
        rows = pl.ds(first, BLOCK)
        tiles = [x_ref[pl.ds(pl.multiple_of(first + 8 * m, 8), 8), rows] for m in range(BLOCK // 8)]
        for m, tile in enumerate(factor_block(tiles)):
            inv_ref[8 * m : 8 * m + 8, :] = tile
        inverse = inv_ref[...]
        x_ref[rows, :] = jnp.dot(inverse, x_ref[rows, :], precision=HIGHEST, preferred_element_type=F32)
        x_ref[rows, rows] = inverse

        def update(i, _):
            lower = pl.ds(pl.multiple_of(i * BLOCK, BLOCK), BLOCK)
            panel = lax.dot_general(
                x_ref[lower, rows], inverse, (((1,), (1,)), ((), ())), precision=HIGHEST, preferred_element_type=F32
            )
            x_ref[lower, rows] = jnp.zeros((BLOCK, BLOCK), F32)
            x_ref[lower, :] -= jnp.dot(panel, x_ref[rows, :], precision=HIGHEST, preferred_element_type=F32)
            return 0

        lax.fori_loop(k + 1, blocks, update, 0)
        return 0

    lax.fori_loop(0, blocks, step, 0)
    for k in range(blocks - 1):
        x_ref[BLOCK * k : BLOCK * (k + 1), BLOCK * (k + 1) :] = jnp.zeros((BLOCK, size - BLOCK * (k + 1)), F32)


def inverse_factor(mine, other, core):
    size = mine.shape[2]
    return pl.pallas_call(
        functools.partial(inverse_factor_kernel, size),
        out_shape=jax.ShapeDtypeStruct((size, size), F32),
        in_specs=[pl.BlockSpec(memory_space=pltpu.SMEM)] + [pl.BlockSpec(memory_space=pltpu.VMEM)] * 2,
        out_specs=pl.BlockSpec(memory_space=pltpu.VMEM),
        scratch_shapes=[pltpu.VMEM((BLOCK, BLOCK), F32)],
        compiler_params=pltpu.CompilerParams(vmem_limit_bytes=32 * 1024 * 1024),
        cost_estimate=pl.CostEstimate(flops=size**3 * 40, bytes_accessed=8 * size * size, transcendentals=size),
    )(core.reshape(1), mine, other)


def matmul(a, b, contract, precision):
    return lax.dot_general(a, b, ((contract[:1], contract[1:]), ((), ())), precision=precision, preferred_element_type=F32)


def hop(axis, move):
    size = {"test": 16, "train": 8}[axis]
    return lambda value: lax.ppermute(value, axis, [(i, move(i)) for i in range(size)])


TO_X = {d: hop("test", lambda s, d=d: s // 4 * 4 + (s + d) % 4) for d in (1, -1)}
TO_Z = {d: hop("test", lambda s, d=d: (s + 4 * d) % 16) for d in (1, -1)}
SWAP_CORE = hop("train", lambda t: t ^ 1)
SWAP_Y1 = hop("train", lambda t: t ^ 2)
SWAP_Y2 = hop("train", lambda t: t ^ 4)


def ring_gather(value, to):
    ahead = to[-1](value)
    behind = to[1](value)
    half = value.shape[0] // 2
    across = jnp.concatenate([to[-1](ahead[:half]), to[1](behind[half:])], axis=0)
    return ahead, across, behind


def place(parts, axis, here):
    shape = list(parts[0].shape)
    shape.insert(axis, 4)
    whole = jnp.zeros(shape, parts[0].dtype)
    for distance, part in enumerate(parts):
        whole = lax.dynamic_update_index_in_dim(whole, part, (here + distance) % 4, axis)
    return whole


def plane_gather(first, second, x, z):
    row = place((first,) + ring_gather(first, TO_X), 0, x)
    column = place((second,) + ring_gather(second, TO_Z), 0, z)
    rows = (row,) + ring_gather(row, TO_Z)
    columns = (column,) + ring_gather(column, TO_X)
    whole = jnp.zeros((4, 4, 2) + first.shape, first.dtype)
    rest = (0,) * first.ndim
    for distance in (0, 1, 3, 2):
        whole = lax.dynamic_update_slice(whole, rows[distance][None, :, None], ((z + distance) % 4, 0, 0) + rest)
        whole = lax.dynamic_update_slice(whole, columns[distance][:, None, None], (0, (x + distance) % 4, 1) + rest)
    return whole


def per_device(train_features, test_panel, damping):
    test, train = lax.axis_index("test"), lax.axis_index("train")
    x, z, core = test % 4, test // 4, train % 2
    share = P_SIZE // lax.axis_size("test")
    half = share // 2
    train_total = train_features.shape[0] * lax.axis_size("train")
    own_t = train_features[:, :share].T
    panel_t = plane_gather(own_t[:half], own_t[half:], x, z).reshape(P_SIZE, -1)
    tests = lax.all_gather(test_panel, "train", axis=1, tiled=True)

    top = matmul(own_t, panel_t, (1, 1), HIGHEST).reshape(2, half, P_SIZE) / train_total
    strip = lax.dynamic_index_in_dim(top, core, 0, False) + SWAP_CORE(lax.dynamic_index_in_dim(top, 1 - core, 0, False))
    strip = strip + SWAP_Y1(strip)
    strip = strip + SWAP_Y2(strip)
    row = lax.broadcasted_iota(jnp.int32, strip.shape, 0)
    column = lax.broadcasted_iota(jnp.int32, strip.shape, 1)
    strip = strip + jnp.where(column == test * share + core * half + row, damping[None, :], 0.0)
    mine = plane_gather(strip[: half // 2], strip[half // 2 :], x, z).reshape(16, half, P_SIZE)
    inverse = inverse_factor(mine, SWAP_CORE(mine), core)

    gram_t = lax.psum(matmul(panel_t, train_features, (1, 0), HIGH) / train_total, "train")
    row = lax.broadcasted_iota(jnp.int32, gram_t.shape, 0)
    column = lax.broadcasted_iota(jnp.int32, gram_t.shape, 1)
    damped_t = gram_t + jnp.where((column < share) & (row == test * share + column), damping[:, None], 0.0)
    panel_factor = matmul(damped_t, inverse, (0, 1), HIGH)
    test_solved = matmul(tests, inverse, (1, 1), HIGH)
    scores = matmul(matmul(test_solved, inverse, (1, 0), HIGH), panel_t, (1, 0), HIGH) / math.sqrt(P_SIZE)
    return (scores, panel_factor)


def solution(mesh):
    in_specs = (P("train", "test"), P("test", "train"), P())
    out_specs = (P("test", "train"), P("test", None))
    return jax.shard_map(
        per_device, mesh=mesh, in_specs=in_specs, out_specs=out_specs, check_vma=False
    )
```

```python
import functools
import math

import jax
import jax.numpy as jnp
from jax import lax
from jax.experimental import pallas as pl
from jax.experimental.pallas import tpu as pltpu
from jax.sharding import PartitionSpec as P

P_SIZE = 1024
BLOCK = 128
SHARE = 64
F32 = jnp.float32
BF16 = jnp.bfloat16
HIGHEST = lax.Precision.HIGHEST
VMEM = pl.BlockSpec(memory_space=pltpu.VMEM)
SMEM = pl.BlockSpec(memory_space=pltpu.SMEM)
PARAMS = pltpu.CompilerParams(vmem_limit_bytes=48 * 1024 * 1024)


def dot(a, b, contract=(1, 0), precision=None):
    return lax.dot_general(a, b, ((contract[:1], contract[1:]), ((), ())), precision=precision, preferred_element_type=F32)


def split(value):
    high = value.astype(BF16)
    return high, (value - high.astype(F32)).astype(BF16)


def dot3(a, b, contract=(1, 0)):
    return dot(a[0], b[0], contract) + (dot(a[0], b[1], contract) + dot(a[1], b[0], contract))


def factor_block(tiles, work):
    tiles = list(tiles)
    count = len(tiles)
    lane = lax.broadcasted_iota(jnp.int32, (8, BLOCK), 1)
    row = lax.broadcasted_iota(jnp.int32, (8, BLOCK), 0)
    share = -(-len(work) // count)

    def spread(value):
        return jnp.broadcast_to(value, (8, BLOCK))

    for group in range(count):
        first = 8 * group
        own = tiles[group]
        below = range(group + 1, count)
        columns = [spread(own[:, first + j : first + j + 1]) for j in range(8)]
        pivots = [[spread(columns[j][i : i + 1, :]) for j in range(i + 1)] for i in range(8)]
        inside = (lane >= first) & (lane < first + 8)
        own = jnp.where(inside, (lane - first == row).astype(F32), own)
        lines = [spread(own[i : i + 1, :]) for i in range(8)]
        factors = {m: [spread(tiles[m][:, first + j : first + j + 1]) for j in range(8)] for m in below}
        for m in below:
            tiles[m] = jnp.where(inside, 0.0, tiles[m])
        done = None
        for k in range(8):
            scale = lax.rsqrt(pivots[k][k])
            line = lines[k] * scale
            ratios = {i: pivots[i][k] * scale for i in range(k + 1, 8)}
            for i in range(k + 1, 8):
                for j in range(k + 1, i + 1):
                    pivots[i][j] = pivots[i][j] - ratios[i] * ratios[j]
                lines[i] = lines[i] - ratios[i] * line
            done = line if done is None else jnp.where(row == k, line, done)
            for m in below:
                factor = factors[m][k] * scale
                tiles[m] = tiles[m] - factor * line
                for i in range(k + 1, 8):
                    factors[m][i] = factors[m][i] - factor * ratios[i]
        tiles[group] = done
        for step in work[share * group : share * (group + 1)]:
            step()
    return [jnp.where(lane < 8 * group + 8, tiles[group], 0.0) for group in range(count)]


def inverse_factor_kernel(pos_ref, mine_ref, other_ref, x_ref, panel_ref):
    strips, half, size = mine_ref.shape
    blocks = size // BLOCK
    core = pos_ref[2]
    for strip in range(strips):
        start = 2 * half * strip
        x_ref[pl.ds(pl.multiple_of(start + half * core, half), half), :] = mine_ref[strip]
        x_ref[pl.ds(pl.multiple_of(start + half * (1 - core), half), half), :] = other_ref[strip]

    def at(i):
        return slice(BLOCK * i, BLOCK * (i + 1))

    def finish_rows(k):
        x_ref[at(k), : BLOCK * k] = dot(x_ref[at(k), at(k)], x_ref[at(k), : BLOCK * k], precision=HIGHEST)

    def column_panel(i, k):
        panel_ref[at(i), :] = dot(x_ref[at(i), at(k)], x_ref[at(k), at(k)], (1, 1), HIGHEST)

    def update_right(i, j):
        x_ref[at(i), at(j)] -= dot(panel_ref[at(i), :], panel_ref[at(j), :], (1, 1), HIGHEST)

    def update_left(i, k):
        change = dot(panel_ref[at(i), :], x_ref[at(k), : BLOCK * (k + 1)], precision=HIGHEST)
        if k:
            x_ref[at(i), : BLOCK * k] -= change[:, : BLOCK * k]
        x_ref[at(i), at(k)] = -change[:, BLOCK * k :]

    def later(k):
        work = [functools.partial(finish_rows, k)] if k else []
        work += [functools.partial(column_panel, i, k) for i in range(k + 2, blocks)]
        work += [functools.partial(update_right, i, j) for j in range(k + 1, blocks) for i in range(max(j, k + 2), blocks)]
        work += [functools.partial(update_left, i, k) for i in range(k + 1, blocks)]
        return work

    for k in range(blocks):
        work = []
        if k:
            column_panel(k, k - 1)
            update_right(k, k)
            work = later(k - 1)
        tiles = [x_ref[BLOCK * k + 8 * m : BLOCK * k + 8 * (m + 1), at(k)] for m in range(BLOCK // 8)]
        for m, tile in enumerate(factor_block(tiles, work)):
            x_ref[BLOCK * k + 8 * m : BLOCK * k + 8 * (m + 1), at(k)] = tile
    finish_rows(blocks - 1)
    for k in range(blocks - 1):
        x_ref[at(k), BLOCK * (k + 1) :] = jnp.zeros((BLOCK, size - BLOCK * (k + 1)), F32)


def inverse_factor(pos, mine, other):
    size = mine.shape[2]
    return pl.pallas_call(
        inverse_factor_kernel,
        out_shape=jax.ShapeDtypeStruct((size, size), F32),
        in_specs=[SMEM, VMEM, VMEM],
        out_specs=VMEM,
        scratch_shapes=[pltpu.VMEM((size, BLOCK), F32)],
        compiler_params=PARAMS,
        cost_estimate=pl.CostEstimate(flops=size**3 * 40, bytes_accessed=8 * size * size, transcendentals=size),
    )(pos, mine, other)


def arrange_kernel(pos_ref, *refs):
    for ring in range(2):
        for distance in range(4):
            place = (pos_ref[ring] + distance) % 4
            for half in range(2):

                @pl.when(place // 2 == half)
                def _(ring=ring, distance=distance, half=half, place=place):
                    refs[8 + 2 * ring + half][place % 2] = refs[4 * ring + distance][...]


def arrange(pos, blocks):
    half = jax.ShapeDtypeStruct((2,) + blocks[0].shape, F32)
    return pl.pallas_call(
        arrange_kernel,
        out_shape=[half] * 4,
        in_specs=[SMEM] + [VMEM] * 8,
        out_specs=[VMEM] * 4,
        compiler_params=PARAMS,
        cost_estimate=pl.CostEstimate(flops=0, bytes_accessed=16 * half.size, transcendentals=0),
    )(pos, *blocks)


def gram_kernel(distances, first, last, pos_ref, f_ref, *refs):
    pieces, refs = refs[: 4 * len(distances)], refs[4 * len(distances) :]
    if first:
        out_ref = refs[0]
        out_ref[...] = jnp.zeros_like(out_ref)
    else:
        out_ref = refs[1]
        out_ref[...] = refs[0][...]
    rows = f_ref.shape[0] // 2
    for ring in range(2):
        features = split(f_ref[rows * ring : rows * (ring + 1), :])
        for n, distance in enumerate(distances):
            halves = pieces[4 * n + 2 * ring : 4 * n + 2 * ring + 2]
            piece = jnp.concatenate([half[...].reshape(2 * SHARE, rows) for half in halves], axis=0)
            product = dot3(split(piece), features)
            place = (pos_ref[1 - ring] + distance) % 4
            if ring == 0:
                out_ref[pl.ds(pl.multiple_of(place * 4 * SHARE, 4 * SHARE), 4 * SHARE), :] += product
            else:
                for z in range(4):
                    to = pl.ds(pl.multiple_of((4 * z + place) * SHARE, SHARE), SHARE)
                    out_ref[to, :] += product[SHARE * z : SHARE * (z + 1), :]
    if last:
        strip_ref = refs[2]
        for i in range(out_ref.shape[0] // BLOCK):
            at = slice(BLOCK * i, BLOCK * (i + 1))
            strip_ref[:, at] = out_ref[at, :BLOCK].T[:SHARE]


def gram(pos, features, distances, pieces, before=None, last=False):
    columns = features.shape[1]
    total = jax.ShapeDtypeStruct((P_SIZE, columns), F32)
    strip = jax.ShapeDtypeStruct((SHARE, P_SIZE), F32)
    operands = (pos, features, *pieces) + (() if before is None else (before,))
    return pl.pallas_call(
        functools.partial(gram_kernel, distances, before is None, last),
        out_shape=[total, strip] if last else total,
        in_specs=[SMEM] + [VMEM] * (len(operands) - 1),
        out_specs=[VMEM, VMEM] if last else VMEM,
        compiler_params=PARAMS,
        cost_estimate=pl.CostEstimate(
            flops=6 * features.size * 4 * SHARE * len(distances), bytes_accessed=4 * features.size, transcendentals=0
        ),
    )(*operands)


def outputs_kernel(distances, pos_ref, tests_ref, inverse_ref, damped_ref, *refs):
    pieces, (scores_ref, factor_ref, solved_ref, weights_ref, mixed_ref) = refs[: 4 * len(distances)], refs[4 * len(distances) :]
    size = inverse_ref.shape[0]
    wide = 4 * SHARE
    rows = scores_ref.shape[1] // 2
    for k in range(size // wide):
        at, upto = slice(wide * k, wide * (k + 1)), slice(0, wide * (k + 1))
        inverse = split(inverse_ref[at, upto])
        solved_ref[:, at] = dot3(split(tests_ref[:, upto]), inverse, (1, 1))
        factor_ref[:, at] = dot3(split(damped_ref[:, upto]), inverse, (1, 1))
    for k in range(size // wide):
        at, after = slice(wide * k, wide * (k + 1)), slice(wide * k, size)
        weights_ref[:, at] = dot3(split(solved_ref[:, after]), split(inverse_ref[after, at])) * (1.0 / math.sqrt(size))
    weights = weights_ref[...]
    for x in range(4):
        parts = [weights[:, wide * z + SHARE * x : wide * z + SHARE * (x + 1)] for z in range(4)]
        mixed_ref[:, wide * x : wide * (x + 1)] = jnp.concatenate(parts, axis=1)
    for ring, source in enumerate((weights_ref, mixed_ref)):
        total = None
        for n, distance in enumerate(distances):
            halves = pieces[4 * n + 2 * ring : 4 * n + 2 * ring + 2]
            piece = jnp.concatenate([half[...].reshape(2 * SHARE, rows) for half in halves], axis=0)
            place = (pos_ref[1 - ring] + distance) % 4
            part = dot3(split(source[:, pl.ds(pl.multiple_of(place * wide, wide), wide)]), split(piece))
            total = part if total is None else total + part
        scores_ref[:, rows * ring : rows * (ring + 1)] = total


def outputs(pos, tests, inverse, damped, distances, pieces):
    count, size = tests.shape
    scores = jax.ShapeDtypeStruct((count, 2 * pieces[0].shape[2]), F32)
    factor = jax.ShapeDtypeStruct(damped.shape, F32)
    return pl.pallas_call(
        functools.partial(outputs_kernel, distances),
        out_shape=[scores, factor],
        in_specs=[SMEM] + [VMEM] * (3 + len(pieces)),
        out_specs=[VMEM, VMEM],
        scratch_shapes=[pltpu.VMEM((count, size), F32)] * 3,
        compiler_params=PARAMS,
        cost_estimate=pl.CostEstimate(flops=6 * size * size * 1400, bytes_accessed=20 * size * size, transcendentals=0),
    )(pos, tests, inverse, damped, *pieces)


def hop(axis, move):
    size = {"test": 16, "train": 8}[axis]
    return lambda value: lax.ppermute(value, axis, [(i, move(i)) for i in range(size)])


TO_X = {d: hop("test", lambda s, d=d: s // 4 * 4 + (s + d) % 4) for d in (1, 2, 3)}
TO_Z = {d: hop("test", lambda s, d=d: (s + 4 * d) % 16) for d in (1, 2, 3)}
SWAP_CORE = hop("train", lambda t: t ^ 1)
SWAP_Y1 = hop("train", lambda t: t ^ 2)
SWAP_Y2 = hop("train", lambda t: t ^ 4)


def ring(value, to):
    return [value, to[3](value), to[2](value), to[1](value)]


def ring_relayed(halves, to):
    ahead, behind = [to[3](halves[0])], [None, to[1](halves[1])]
    ahead.append(to[3](halves[1]))
    behind[0] = to[1](halves[0])
    across = [to[3](ahead[0]), to[1](behind[1])]
    return [list(halves), ahead, across, behind]


def place(parts, axis, here):
    shape = list(parts[0].shape)
    shape.insert(axis, 4)
    whole = jnp.zeros(shape, parts[0].dtype)
    for distance, part in enumerate(parts):
        whole = lax.dynamic_update_index_in_dim(whole, part, (here + distance) % 4, axis)
    return whole


def strips_gather(first, second, x, z):
    rows = ring(place(ring(first, TO_X), 0, x), TO_Z)
    columns = ring(place(ring(second, TO_Z), 0, z), TO_X)
    whole = jnp.zeros((4, 4, 2) + first.shape, first.dtype)
    rest = (0,) * first.ndim
    for distance in (0, 1, 3, 2):
        whole = lax.dynamic_update_slice(whole, rows[distance][None, :, None], ((z + distance) % 4, 0, 0) + rest)
        whole = lax.dynamic_update_slice(whole, columns[distance][:, None, None], (0, (x + distance) % 4, 1) + rest)
    return whole


def per_device(train_features, test_panel, damping):
    test, train = lax.axis_index("test"), lax.axis_index("train")
    x, z, core = test % 4, test // 4, train % 2
    pos = jnp.stack([x, z, core]).astype(jnp.int32)
    rows_dev = train_features.shape[0]
    train_total = rows_dev * lax.axis_size("train")
    half = SHARE // 2

    own_t = train_features[:, :SHARE].T
    blocks = ring(own_t[:, : rows_dev // 2], TO_X) + ring(own_t[:, rows_dev // 2 :], TO_Z)
    halves = arrange(pos, blocks)
    rows, columns = ring_relayed(halves[:2], TO_Z), ring_relayed(halves[2:], TO_X)
    pieces = [rows[d] + columns[d] for d in range(4)]
    tests = lax.all_gather(test_panel, "train", axis=1, tiled=True)
    total = gram(pos, train_features, (0,), pieces[0])
    total, tests = lax.optimization_barrier((total, tests))
    total = gram(pos, train_features, (1, 3), pieces[1] + pieces[3], total)
    total, strip = gram(pos, train_features, (2,), pieces[2], total, last=True)

    strip = strip.reshape(2, half, P_SIZE) / train_total
    strip = lax.dynamic_index_in_dim(strip, core, 0, False) + SWAP_CORE(lax.dynamic_index_in_dim(strip, 1 - core, 0, False))
    strip = strip + SWAP_Y1(strip)
    strip = strip + SWAP_Y2(strip)
    row = lax.broadcasted_iota(jnp.int32, strip.shape, 0)
    column = lax.broadcasted_iota(jnp.int32, strip.shape, 1)
    strip = strip + jnp.where(column == test * SHARE + core * half + row, damping[None, :], 0.0)

    part = total.T / train_total
    row = lax.broadcasted_iota(jnp.int32, part.shape, 0)
    column = lax.broadcasted_iota(jnp.int32, part.shape, 1)
    on_diagonal = (train == 0) & (row < SHARE) & (column == test * SHARE + row)
    damped = lax.psum(part + jnp.where(on_diagonal, damping[None, :], 0.0), "train")

    mine = strips_gather(strip[: half // 2], strip[half // 2 :], x, z).reshape(16, half, P_SIZE)
    inverse = inverse_factor(pos, mine, SWAP_CORE(mine))
    distances = (0, 1, 3, 2)
    return tuple(outputs(pos, tests, inverse, damped, distances, sum((pieces[d] for d in distances), [])))


def solution(mesh):
    in_specs = (P("train", "test"), P("test", "train"), P())
    out_specs = (P("test", "train"), P("test", None))
    return jax.shard_map(
        per_device, mesh=mesh, in_specs=in_specs, out_specs=out_specs, check_vma=False
    )
```

```python
import functools
import math

import jax
import jax.numpy as jnp
from jax import lax
from jax.experimental import pallas as pl
from jax.experimental.pallas import tpu as pltpu
from jax.sharding import PartitionSpec as P

P_SIZE = 1024
BLOCK = 128
SHARE = 64
F32 = jnp.float32
BF16 = jnp.bfloat16
HIGHEST = lax.Precision.HIGHEST
VMEM = pl.BlockSpec(memory_space=pltpu.VMEM)
SMEM = pl.BlockSpec(memory_space=pltpu.SMEM)
SPREAD = pltpu.VMEM((2, 64, BLOCK), F32)


def params(mebibytes):
    return pltpu.CompilerParams(vmem_limit_bytes=mebibytes * 1024 * 1024)


def dot(a, b, contract=(1, 0), precision=None):
    return lax.dot_general(a, b, ((contract[:1], contract[1:]), ((), ())), precision=precision, preferred_element_type=F32)


def split(value):
    high = value.astype(BF16)
    return high, (value - high.astype(F32)).astype(BF16)


def dot3(a, b, contract=(1, 0)):
    return dot(a[0], b[0], contract) + (dot(a[0], b[1], contract) + dot(a[1], b[0], contract))


def factor_block(tiles, work, spread_ref):
    tiles = list(tiles)
    count = len(tiles)
    lane = lax.broadcasted_iota(jnp.int32, (8, BLOCK), 1)
    row = lax.broadcasted_iota(jnp.int32, (8, BLOCK), 0)
    share = -(-len(work) // count)

    def spread(value):
        return jnp.broadcast_to(value, (8, BLOCK))

    for group in range(count):
        first = 8 * group
        own = tiles[group]
        below = range(group + 1, count)
        columns = [spread(own[:, first + j : first + j + 1]) for j in range(8)]
        for j in range(8):
            spread_ref[group % 2, 8 * j : 8 * (j + 1), :] = columns[j]
        pivots = [[spread(spread_ref[group % 2, 8 * j + i : 8 * j + i + 1, :]) for j in range(i + 1)] for i in range(8)]
        inside = (lane >= first) & (lane < first + 8)
        own = jnp.where(inside, (lane - first == row).astype(F32), own)
        lines = [spread(own[i : i + 1, :]) for i in range(8)]
        factors = {m: [spread(tiles[m][:, first + j : first + j + 1]) for j in range(8)] for m in below}
        for m in below:
            tiles[m] = jnp.where(inside, 0.0, tiles[m])
        done = None
        for k in range(8):
            scale = lax.rsqrt(pivots[k][k])
            line = lines[k] * scale
            ratios = {i: pivots[i][k] * scale for i in range(k + 1, 8)}
            for i in range(k + 1, 8):
                for j in range(k + 1, i + 1):
                    pivots[i][j] = pivots[i][j] - ratios[i] * ratios[j]
                lines[i] = lines[i] - ratios[i] * line
            done = line if done is None else jnp.where(row == k, line, done)
            for m in below:
                factor = factors[m][k] * scale
                tiles[m] = tiles[m] - factor * line
                for i in range(k + 1, 8):
                    factors[m][i] = factors[m][i] - factor * ratios[i]
        tiles[group] = done
        for step in work[share * group : share * (group + 1)]:
            step()
    return [jnp.where(lane < 8 * group + 8, tiles[group], 0.0) for group in range(count)]


def factor_in_place(x_ref, panel_ref, spread_ref, extra=()):
    size = x_ref.shape[0]
    blocks = size // BLOCK

    def at(i):
        return slice(BLOCK * i, BLOCK * (i + 1))

    def finish_rows(k):
        x_ref[at(k), : BLOCK * k] = dot(x_ref[at(k), at(k)], x_ref[at(k), : BLOCK * k], precision=HIGHEST)

    def column_panel(i, k):
        panel_ref[at(i), :] = dot(x_ref[at(i), at(k)], x_ref[at(k), at(k)], (1, 1), HIGHEST)

    def update_right(i, j):
        x_ref[at(i), at(j)] -= dot(panel_ref[at(i), :], panel_ref[at(j), :], (1, 1), HIGHEST)

    def update_left(i, k):
        change = dot(panel_ref[at(i), :], x_ref[at(k), : BLOCK * (k + 1)], precision=HIGHEST)
        if k:
            x_ref[at(i), : BLOCK * k] -= change[:, : BLOCK * k]
        x_ref[at(i), at(k)] = -change[:, BLOCK * k :]

    def later(k):
        work = [functools.partial(finish_rows, k)] if k else []
        work += [functools.partial(column_panel, i, k) for i in range(k + 2, blocks)]
        work += [functools.partial(update_right, i, j) for j in range(k + 1, blocks) for i in range(max(j, k + 2), blocks)]
        work += [functools.partial(update_left, i, k) for i in range(k + 1, blocks)]
        return work

    for k in range(blocks):
        work = list(extra)
        if k:
            column_panel(k, k - 1)
            update_right(k, k)
            work = later(k - 1)
        tiles = [x_ref[BLOCK * k + 8 * m : BLOCK * k + 8 * (m + 1), at(k)] for m in range(BLOCK // 8)]
        for m, tile in enumerate(factor_block(tiles, work, spread_ref)):
            x_ref[BLOCK * k + 8 * m : BLOCK * k + 8 * (m + 1), at(k)] = tile
    finish_rows(blocks - 1)
    for k in range(blocks - 1):
        x_ref[at(k), BLOCK * (k + 1) :] = jnp.zeros((BLOCK, size - BLOCK * (k + 1)), F32)


def place_strips(pos_ref, mine_ref, other_ref, to_ref):
    for distance in range(mine_ref.shape[0]):
        x = (pos_ref[0] + distance) % 4
        for z in range(mine_ref.shape[1]):
            for source, core in ((mine_ref, pos_ref[2]), (other_ref, 1 - pos_ref[2])):
                start = pl.multiple_of((4 * z + x) * SHARE + core * (SHARE // 2), SHARE // 2)
                to_ref[pl.ds(start, SHARE // 2), :] = source[distance, z]


def first_factor_kernel(pos_ref, mine_ref, other_ref, x_ref, panel_ref, spread_ref):
    place_strips(pos_ref, mine_ref, other_ref, x_ref)
    factor_in_place(x_ref, panel_ref, spread_ref)


def second_factor_kernel(pos_ref, mine_ref, other_ref, first_ref, out_ref, a_ref, x_ref, l_ref, r_ref, panel_ref, spread_ref):
    size = first_ref.shape[0]
    place_strips(pos_ref, mine_ref, other_ref, a_ref)
    step = 256
    for k in range(size // step):
        at, upto = slice(step * k, step * (k + 1)), slice(0, step * (k + 1))
        l_ref[:, at] = dot(a_ref[:, upto], first_ref[at, upto], (1, 1), HIGHEST)
    for k in range(size // step):
        at, below = slice(step * k, step * (k + 1)), slice(step * k, size)
        x_ref[below, at] = a_ref[below, size + step * k : size + step * (k + 1)] - dot(
            l_ref[below, :], l_ref[at, :], (1, 1), HIGHEST
        )

    def right(i, k):
        at, after = slice(step * k, step * (k + 1)), slice(step * k, size)
        rows = slice(BLOCK * i, BLOCK * (i + 1))
        r_ref[rows, at] = dot(l_ref[rows, after], first_ref[after, at], precision=HIGHEST)

    products = [functools.partial(right, i, k) for k in range(size // step) for i in range(size // BLOCK)]
    factor_in_place(x_ref, panel_ref, spread_ref, products)
    out_ref[:size, :size] = first_ref[...]
    out_ref[:size, size:] = jnp.zeros((size, size), F32)
    out_ref[size:, size:] = x_ref[...]
    for k in range(size // step):
        at, upto = slice(step * k, step * (k + 1)), slice(0, step * (k + 1))
        out_ref[size + step * k : size + step * (k + 1), :size] = -dot(x_ref[at, upto], r_ref[upto, :], precision=HIGHEST)


def first_factor(pos, mine, other):
    size = mine.shape[3]
    return pl.pallas_call(
        first_factor_kernel,
        out_shape=jax.ShapeDtypeStruct((size, size), F32),
        in_specs=[SMEM, VMEM, VMEM],
        out_specs=VMEM,
        scratch_shapes=[pltpu.VMEM((size, BLOCK), F32), SPREAD],
        compiler_params=params(16),
        cost_estimate=pl.CostEstimate(flops=size * size, bytes_accessed=8 * size * size, transcendentals=size),
    )(pos, mine, other)


def second_factor(pos, mine, other, first):
    size = first.shape[0]
    square = pltpu.VMEM((size, size), F32)
    return pl.pallas_call(
        second_factor_kernel,
        out_shape=jax.ShapeDtypeStruct((2 * size, 2 * size), F32),
        in_specs=[SMEM, VMEM, VMEM, VMEM],
        out_specs=VMEM,
        scratch_shapes=[pltpu.VMEM((size, 2 * size), F32), square, square, square, pltpu.VMEM((size, BLOCK), F32), SPREAD],
        compiler_params=params(24),
        cost_estimate=pl.CostEstimate(flops=size * size, bytes_accessed=8 * size * size, transcendentals=size),
    )(pos, mine, other, first)


def arrange_kernel(axis, pos_ref, *refs):
    for distance in range(4):
        refs[4][(pos_ref[axis] + distance) % 4] = refs[distance][...]


def arrange(pos, axis, blocks):
    block = blocks[0]
    return pl.pallas_call(
        functools.partial(arrange_kernel, axis),
        out_shape=jax.ShapeDtypeStruct((4,) + block.shape, F32),
        in_specs=[SMEM] + [VMEM] * 4,
        out_specs=VMEM,
        compiler_params=params(4),
        cost_estimate=pl.CostEstimate(flops=0, bytes_accessed=32 * block.size, transcendentals=0),
    )(pos, *blocks)


def cut_kernel(first_ref, second_ref, upper_ref, lower_ref):
    half = upper_ref.shape[0]
    upper_ref[...] = first_ref[:half]
    lower_ref[...] = second_ref[half:]


def cut(first, second):
    half = jax.ShapeDtypeStruct((first.shape[0] // 2,) + first.shape[1:], F32)
    return pl.pallas_call(
        cut_kernel,
        out_shape=[half] * 2,
        in_specs=[VMEM] * 2,
        out_specs=[VMEM] * 2,
        compiler_params=params(4),
        cost_estimate=pl.CostEstimate(flops=0, bytes_accessed=8 * first.size, transcendentals=0),
    )(first, second)


def order_strips_kernel(pos_ref, *refs):
    left_ref, rest_ref = refs[4:]
    left = left_ref.shape[2]
    for distance in range(4):
        z = (pos_ref[1] + distance) % 4

        @pl.when(z < 2)
        def _(distance=distance, z=z):
            left_ref[z % 2] = refs[distance][:, :left]

        @pl.when(z >= 2)
        def _(distance=distance, z=z):
            rest_ref[z % 2] = refs[distance][...]


def order_strips(pos, strips):
    rows, columns = strips[0].shape
    return pl.pallas_call(
        order_strips_kernel,
        out_shape=[jax.ShapeDtypeStruct((2, rows, columns // 2), F32), jax.ShapeDtypeStruct((2, rows, columns), F32)],
        in_specs=[SMEM] + [VMEM] * 4,
        out_specs=[VMEM] * 2,
        compiler_params=params(4),
        cost_estimate=pl.CostEstimate(flops=0, bytes_accessed=32 * rows * columns, transcendentals=0),
    )(pos, *strips)


def piece_rows(ring, place, z):
    if ring == 0:
        return pl.ds(pl.multiple_of(place * 4 * SHARE, 4 * SHARE), 4 * SHARE)
    return pl.ds(pl.multiple_of((4 * z + place) * SHARE, SHARE), SHARE)


def add_product(ring, place, product, to_ref):
    if ring == 0:
        to_ref[piece_rows(0, place, 0), :] += product
    else:
        for z in range(4):
            to_ref[piece_rows(1, place, z), :] += product[SHARE * z : SHARE * (z + 1), :]


def early_gram_kernel(distances, first, pos_ref, f_ref, *refs):
    count = 2 * len(distances)
    pieces, refs = refs[:count], refs[count:]
    examples = f_ref.shape[0] // 2
    if first:
        out_ref = refs[0]
        out_ref[...] = jnp.zeros_like(out_ref)
    else:
        before_ref, out_ref, strip_ref = refs
        out_ref[...] = before_ref[...]
    for ring in range(2):
        features = split(f_ref[examples * ring : examples * (ring + 1), :])
        for n, distance in enumerate(distances):
            product = dot3(split(pieces[2 * n + ring][...].reshape(4 * SHARE, examples)), features)
            add_product(ring, (pos_ref[1 - ring] + distance) % 4, product, out_ref)
    if not first:
        for i in range(out_ref.shape[0] // BLOCK):
            at = slice(BLOCK * i, BLOCK * (i + 1))
            strip_ref[:, at] = out_ref[at, :BLOCK].T[:SHARE]


def early_gram(pos, features, distances, pieces, before=None):
    columns = features.shape[1]
    total = jax.ShapeDtypeStruct((P_SIZE, columns), F32)
    strip = jax.ShapeDtypeStruct((SHARE, P_SIZE), F32)
    extra = () if before is None else (before,)
    return pl.pallas_call(
        functools.partial(early_gram_kernel, distances, before is None),
        out_shape=total if before is None else [total, strip],
        in_specs=[SMEM] + [VMEM] * (1 + len(pieces) + len(extra)),
        out_specs=VMEM if before is None else [VMEM, VMEM],
        compiler_params=params(16),
        cost_estimate=pl.CostEstimate(
            flops=6 * features.size * 4 * SHARE * len(distances), bytes_accessed=4 * features.size, transcendentals=0
        ),
    )(pos, features, *pieces, *extra)


def strip_kernel(total, pos_ref, damping_ref, own_ref, early_ref, *refs):
    halves, (mine_ref, other_ref, strip_ref) = refs[:4], refs[4:]
    wide = 4 * SHARE
    examples = own_ref.shape[1] // 2
    strip_ref[...] = early_ref[...]
    for ring in range(2):
        own = split(own_ref[:, examples * ring : examples * (ring + 1)])
        parts = [half[...].reshape(wide // 2, examples) for half in halves[2 * ring : 2 * ring + 2]]
        product = jnp.concatenate([dot3(own, split(part), (1, 1)) for part in parts], axis=1)
        place = (pos_ref[1 - ring] + 2) % 4
        if ring == 0:
            strip_ref[:, piece_rows(0, place, 0)] += product
        else:
            lane = lax.broadcasted_iota(jnp.int32, (SHARE, wide), 1)
            for z in range(4):
                part = jnp.concatenate([product[:, SHARE * z : SHARE * (z + 1)]] * 4, axis=1)
                strip_ref[:, wide * z : wide * (z + 1)] += jnp.where(lane // SHARE == place, part, 0.0)
    half = mine_ref.shape[0]
    start = pl.multiple_of(pos_ref[2] * half, half)
    row = lax.broadcasted_iota(jnp.int32, mine_ref.shape, 0) + (4 * pos_ref[1] + pos_ref[0]) * SHARE + start
    column = lax.broadcasted_iota(jnp.int32, mine_ref.shape, 1)
    damping = jnp.where((row == column) & (pos_ref[3] < 2), damping_ref[...], 0.0)
    mine_ref[...] = strip_ref[pl.ds(start, half), :] * (1.0 / total) + damping
    other_ref[...] = strip_ref[pl.ds(half - start, half), :] * (1.0 / total)


def strip_product(total, pos, damping, own_t, early, halves):
    return pl.pallas_call(
        functools.partial(strip_kernel, total),
        out_shape=[jax.ShapeDtypeStruct((SHARE // 2, P_SIZE), F32)] * 2,
        in_specs=[SMEM] + [VMEM] * 7,
        out_specs=[VMEM] * 2,
        scratch_shapes=[pltpu.VMEM(early.shape, F32)],
        compiler_params=params(12),
        cost_estimate=pl.CostEstimate(flops=24 * own_t.size * 256, bytes_accessed=16 * own_t.size, transcendentals=0),
    )(pos, damping[None, :], own_t, early, *halves)


def add_kernel(a_ref, b_ref, sum_ref):
    sum_ref[...] = a_ref[...] + b_ref[...]


def add(a, b):
    return pl.pallas_call(
        add_kernel,
        out_shape=jax.ShapeDtypeStruct(a.shape, F32),
        in_specs=[VMEM] * 2,
        out_specs=VMEM,
        compiler_params=params(4),
        cost_estimate=pl.CostEstimate(flops=a.size, bytes_accessed=12 * a.size, transcendentals=0),
    )(a, b)


def stack_kernel(*refs):
    for i, ref in enumerate(refs[:-1]):
        refs[-1][i] = ref[...]


def stack(arrays):
    return pl.pallas_call(
        stack_kernel,
        out_shape=jax.ShapeDtypeStruct((len(arrays),) + arrays[0].shape, F32),
        in_specs=[VMEM] * len(arrays),
        out_specs=VMEM,
        compiler_params=params(4),
        cost_estimate=pl.CostEstimate(flops=0, bytes_accessed=32 * arrays[0].size, transcendentals=0),
    )(*arrays)


def late_gram_kernel(total, pos_ref, damping_ref, early_ref, f_ref, *refs):
    halves, (mine_ref, other_ref, sum_ref) = refs[:4], refs[4:]
    wide = 4 * SHARE
    examples = f_ref.shape[0] // 2
    half = mine_ref.shape[0]
    sum_ref[...] = early_ref[...]
    for ring in range(2):
        parts = [part[...].reshape(wide // 2, examples) for part in halves[2 * ring : 2 * ring + 2]]
        features = split(f_ref[examples * ring : examples * (ring + 1), :])
        product = dot3(split(jnp.concatenate(parts, axis=0)), features)
        add_product(ring, (pos_ref[1 - ring] + 2) % 4, product, sum_ref)
    for to_ref, core in ((mine_ref, pos_ref[2]), (other_ref, 1 - pos_ref[2])):
        columns = pl.ds(pl.multiple_of(core * half, half), half)
        for i in range(sum_ref.shape[0] // BLOCK):
            at = slice(BLOCK * i, BLOCK * (i + 1))
            to_ref[:, at] = sum_ref[at, columns].T * (1.0 / total)

    @pl.when(pos_ref[3] == 0)
    def _():
        shape = (SHARE, mine_ref.shape[1])
        row = lax.broadcasted_iota(jnp.int32, shape, 0) + (4 * pos_ref[1] + pos_ref[0]) * SHARE
        column = lax.broadcasted_iota(jnp.int32, shape, 1)
        mine_ref[:SHARE, :] += jnp.where(row == column, damping_ref[...], 0.0)


def late_gram(total, pos, damping, early, features, halves):
    rows, columns = features.shape
    return pl.pallas_call(
        functools.partial(late_gram_kernel, total),
        out_shape=[jax.ShapeDtypeStruct((columns // 2, P_SIZE), F32)] * 2,
        in_specs=[SMEM] + [VMEM] * 7,
        out_specs=[VMEM] * 2,
        scratch_shapes=[pltpu.VMEM(early.shape, F32)],
        compiler_params=params(16),
        cost_estimate=pl.CostEstimate(flops=6 * features.size * 256, bytes_accessed=8 * features.size, transcendentals=0),
    )(pos, damping[None, :], early, features, *halves)


def factor_kernel(damped_ref, last_ref, inverse_ref, factor_ref):
    size = inverse_ref.shape[0]
    wide = 4 * SHARE
    damped = split(damped_ref[...] + last_ref[...])
    for k in range(size // wide):
        at, upto = slice(wide * k, wide * (k + 1)), slice(0, wide * (k + 1))
        factor_ref[:, at] = dot3(tuple(part[:, upto] for part in damped), split(inverse_ref[at, upto]), (1, 1))


def factor_product(damped, last, inverse):
    return pl.pallas_call(
        factor_kernel,
        out_shape=jax.ShapeDtypeStruct(damped.shape, F32),
        in_specs=[VMEM] * 3,
        out_specs=VMEM,
        compiler_params=params(16),
        cost_estimate=pl.CostEstimate(flops=4 * damped.size * P_SIZE, bytes_accessed=12 * damped.size, transcendentals=0),
    )(damped, last, inverse)


def scores_kernel(distances, pos_ref, inverse_ref, *refs):
    tests, refs = refs[:4], refs[4:]
    count = 2 * len(distances) + 4
    pieces, (scores_ref, tests_ref, solved_ref, weights_ref, mixed_ref) = refs[:count], refs[count:]
    size = inverse_ref.shape[0]
    wide = 4 * SHARE
    blocks = size // wide
    for distance, block in enumerate(tests):
        first = (pos_ref[3] + 2 * distance) % 8
        columns = block.shape[2]
        for i, place in enumerate((first, first + 1 - 2 * pos_ref[2])):
            tests_ref[:, pl.ds(pl.multiple_of(place * columns, columns), columns)] = block[i]
    for k in range(blocks):
        at, upto = slice(wide * k, wide * (k + 1)), slice(0, wide * (k + 1))
        solved_ref[:, at] = dot3(split(tests_ref[:, upto]), split(inverse_ref[at, upto]), (1, 1))
    for k in range(blocks):
        at, after = slice(wide * k, wide * (k + 1)), slice(wide * k, size)
        weights_ref[:, at] = dot3(split(solved_ref[:, after]), split(inverse_ref[after, at])) * (1.0 / math.sqrt(size))
    weights = weights_ref[...]
    for x in range(4):
        parts = [weights[:, wide * z + SHARE * x : wide * z + SHARE * (x + 1)] for z in range(4)]
        mixed_ref[:, wide * x : wide * (x + 1)] = jnp.concatenate(parts, axis=1)
    for ring, source in enumerate((weights_ref, mixed_ref)):
        whole = [pieces[2 * n + ring][...] for n in range(len(distances))]
        whole.append(jnp.concatenate([part[...] for part in pieces[count - 4 + 2 * ring : count - 2 + 2 * ring]], axis=0))
        total = None
        for piece, distance in zip(whole, distances + (2,)):
            place = pl.multiple_of((pos_ref[1 - ring] + distance) % 4 * wide, wide)
            part = dot3(split(source[:, pl.ds(place, wide)]), split(piece.reshape(wide, piece.shape[2])))
            total = part if total is None else total + part
        examples = total.shape[1]
        scores_ref[:, examples * ring : examples * (ring + 1)] = total


def scores_product(pos, inverse, tests, distances, pieces):
    size = inverse.shape[0]
    count = tests[0].shape[1]
    return pl.pallas_call(
        functools.partial(scores_kernel, distances),
        out_shape=jax.ShapeDtypeStruct((count, 2 * pieces[0].shape[2]), F32),
        in_specs=[SMEM] + [VMEM] * (5 + len(pieces)),
        out_specs=VMEM,
        scratch_shapes=[pltpu.VMEM((count, size), F32)] * 4,
        compiler_params=params(24),
        cost_estimate=pl.CostEstimate(flops=6 * size * size * 1000, bytes_accessed=20 * size * size, transcendentals=0),
    )(pos, inverse, *tests, *pieces)


def join_kernel(pos_ref, mine_ref, other_ref, whole_ref):
    half = mine_ref.shape[0]
    whole_ref[pl.ds(pl.multiple_of(pos_ref[2] * half, half), half), :] = mine_ref[...]
    whole_ref[pl.ds(pl.multiple_of((1 - pos_ref[2]) * half, half), half), :] = other_ref[...]


def join(pos, mine, other):
    rows, columns = mine.shape
    return pl.pallas_call(
        join_kernel,
        out_shape=jax.ShapeDtypeStruct((2 * rows, columns), F32),
        in_specs=[SMEM, VMEM, VMEM],
        out_specs=VMEM,
        compiler_params=params(4),
        cost_estimate=pl.CostEstimate(flops=0, bytes_accessed=16 * mine.size, transcendentals=0),
    )(pos, mine, other)


def hop(axis, move):
    size = {"test": 16, "train": 8}[axis]
    return lambda value: lax.ppermute(value, axis, [(i, move(i)) for i in range(size)])


TO_X = {d: hop("test", lambda s, d=d: s // 4 * 4 + (s + d) % 4) for d in (1, 2, 3)}
TO_Z = {d: hop("test", lambda s, d=d: (s + 4 * d) % 16) for d in (1, 2, 3)}
TO_Y = {d: hop("train", lambda t, d=d: (t + 2 * d) % 8) for d in (1, 2, 3)}
SWAP_CORE = hop("train", lambda t: t ^ 1)
SWAP_Y1 = hop("train", lambda t: t ^ 2)
SWAP_Y2 = hop("train", lambda t: t ^ 4)


def ring(value, to):
    return [value, to[3](value), to[2](value), to[1](value)]


def relay(ahead, behind, to):
    upper, lower = cut(ahead, behind)
    return to[3](upper), to[1](lower)


def per_device(train_features, test_panel, damping):
    test, train = lax.axis_index("test"), lax.axis_index("train")
    pos = jnp.stack([test % 4, test // 4, train % 2, train]).astype(jnp.int32)
    rows_dev = train_features.shape[0]
    train_total = rows_dev * lax.axis_size("train")

    own_t = train_features[:, :SHARE].T
    first, second = own_t[:, : rows_dev // 2], own_t[:, rows_dev // 2 :]
    pos, first, second = lax.optimization_barrier((pos, first, second))
    own_row = arrange(pos, 0, ring(first, TO_X))
    own_column = arrange(pos, 1, ring(second, TO_Z))
    near = [TO_Z[3](own_row), TO_X[3](own_column), TO_Z[1](own_row), TO_X[1](own_column)]
    early = early_gram(pos, train_features, (0,), [own_row, own_column])
    early, test_panel = lax.optimization_barrier((early, test_panel))
    tests = ring(stack([test_panel, SWAP_CORE(test_panel)]), TO_Y)
    early, near = lax.optimization_barrier((early, near))
    far = [*relay(near[0], near[2], TO_Z), *relay(near[1], near[3], TO_X)]
    early, strip = early_gram(pos, train_features, (1, 3), near, early)
    strip, tests = lax.optimization_barrier((strip, tests))

    strip, other_strip = strip_product(train_total, pos, damping, own_t, strip, far)
    strip = add(strip, SWAP_CORE(other_strip))
    strip = add(strip, SWAP_Y1(strip))
    term, other_term = late_gram(train_total, pos, damping, early, train_features, far)
    strip, term, other_term = lax.optimization_barrier((strip, term, other_term))
    strip = add(strip, SWAP_Y2(strip))

    strip, damped = lax.optimization_barrier((strip, add(term, SWAP_CORE(other_term))))
    damped_y1 = SWAP_Y1(damped)
    left, rest = order_strips(pos, ring(strip, TO_Z))
    mine = stack(ring(left, TO_X))
    mine, rest = lax.optimization_barrier((mine, rest))
    later = ring(rest, TO_X)
    first = first_factor(pos, mine, SWAP_CORE(mine))
    first, later, damped_y1 = lax.optimization_barrier((first, later, damped_y1))
    damped = add(damped, damped_y1)
    later = stack(later)
    later_other = SWAP_CORE(later)
    later, damped = lax.optimization_barrier((later, damped))
    damped_y2 = SWAP_Y2(damped)
    inverse = second_factor(pos, later, later_other, first)
    inverse, damped, damped_y2 = lax.optimization_barrier((inverse, damped, damped_y2))
    factor = factor_product(damped, damped_y2, inverse)
    other_factor = SWAP_CORE(factor)
    inverse, factor = lax.optimization_barrier((inverse, factor))
    scores = scores_product(pos, inverse, tests, (0, 1, 3), [own_row, own_column] + near + far)
    scores, other_factor = lax.optimization_barrier((scores, other_factor))
    return scores, join(pos, factor, other_factor)


def solution(mesh):
    in_specs = (P("train", "test"), P("test", "train"), P())
    out_specs = (P("test", "train"), P("test", None))
    return jax.shard_map(
        per_device, mesh=mesh, in_specs=in_specs, out_specs=out_specs, check_vma=False
    )
```

```python
import functools
import math

import jax
import jax.numpy as jnp
from jax import lax
from jax.experimental import pallas as pl
from jax.experimental.pallas import tpu as pltpu
from jax.sharding import PartitionSpec as P

P_SIZE = 1024
BLOCK = 128
SHARE = 64
F32 = jnp.float32
BF16 = jnp.bfloat16
HIGHEST = lax.Precision.HIGHEST
VMEM = pl.BlockSpec(memory_space=pltpu.VMEM)
SMEM = pl.BlockSpec(memory_space=pltpu.SMEM)
ANY = pl.BlockSpec(memory_space=pl.ANY)
SPREAD = pltpu.VMEM((2, 64, BLOCK), F32)


def params(mebibytes):
    return pltpu.CompilerParams(vmem_limit_bytes=mebibytes * 1024 * 1024)


def dot(a, b, contract=(1, 0), precision=None):
    return lax.dot_general(a, b, ((contract[:1], contract[1:]), ((), ())), precision=precision, preferred_element_type=F32)


def split(value):
    high = value.astype(BF16)
    return high, (value - high.astype(F32)).astype(BF16)


def dot3(a, b, contract=(1, 0)):
    return dot(a[0], b[0], contract) + (dot(a[0], b[1], contract) + dot(a[1], b[0], contract))


def factor_block(tiles, work, spread_ref):
    tiles = list(tiles)
    count = len(tiles)
    lane = lax.broadcasted_iota(jnp.int32, (8, BLOCK), 1)
    row = lax.broadcasted_iota(jnp.int32, (8, BLOCK), 0)
    share = -(-len(work) // count)

    def spread(value):
        return jnp.broadcast_to(value, (8, BLOCK))

    for group in range(count):
        first = 8 * group
        own = tiles[group]
        below = range(group + 1, count)
        columns = [spread(own[:, first + j : first + j + 1]) for j in range(8)]
        for j in range(8):
            spread_ref[group % 2, 8 * j : 8 * (j + 1), :] = columns[j]
        pivots = [[spread(spread_ref[group % 2, 8 * j + i : 8 * j + i + 1, :]) for j in range(i + 1)] for i in range(8)]
        inside = (lane >= first) & (lane < first + 8)
        own = jnp.where(inside, (lane - first == row).astype(F32), own)
        lines = [spread(own[i : i + 1, :]) for i in range(8)]
        factors = {m: [spread(tiles[m][:, first + j : first + j + 1]) for j in range(8)] for m in below}
        for m in below:
            tiles[m] = jnp.where(inside, 0.0, tiles[m])
        done = None
        for k in range(8):
            scale = lax.rsqrt(pivots[k][k])
            line = lines[k] * scale
            ratios = {i: pivots[i][k] * scale for i in range(k + 1, 8)}
            for i in range(k + 1, 8):
                for j in range(k + 1, i + 1):
                    pivots[i][j] = pivots[i][j] - ratios[i] * ratios[j]
                lines[i] = lines[i] - ratios[i] * line
            done = line if done is None else jnp.where(row == k, line, done)
            for m in below:
                factor = factors[m][k] * scale
                tiles[m] = tiles[m] - factor * line
                for i in range(k + 1, 8):
                    factors[m][i] = factors[m][i] - factor * ratios[i]
        tiles[group] = done
        for step in work[share * group : share * (group + 1)]:
            step()
    return [jnp.where(lane < 8 * group + 8, tiles[group], 0.0) for group in range(count)]


def blocks_at(i):
    return slice(BLOCK * i, BLOCK * (i + 1))


def factor_in_place(x_ref, panel_ref, spread_ref, extra):
    size = x_ref.shape[0]
    blocks = size // BLOCK
    at = blocks_at

    def finish_rows(k):
        x_ref[at(k), : BLOCK * k] = dot(x_ref[at(k), at(k)], x_ref[at(k), : BLOCK * k], precision=HIGHEST)

    def column_panel(i, k):
        panel_ref[at(i), :] = dot(x_ref[at(i), at(k)], x_ref[at(k), at(k)], (1, 1), HIGHEST)

    def update_right(i, j):
        x_ref[at(i), at(j)] -= dot(panel_ref[at(i), :], panel_ref[at(j), :], (1, 1), HIGHEST)

    def update_left(i, k):
        change = dot(panel_ref[at(i), :], x_ref[at(k), : BLOCK * (k + 1)], precision=HIGHEST)
        if k:
            x_ref[at(i), : BLOCK * k] -= change[:, : BLOCK * k]
        x_ref[at(i), at(k)] = -change[:, BLOCK * k :]

    def clear_right(k):
        x_ref[at(k), BLOCK * (k + 1) :] = jnp.zeros((BLOCK, size - BLOCK * (k + 1)), F32)

    def later(k):
        work = [functools.partial(finish_rows, k)] if k else []
        work += [functools.partial(column_panel, i, k) for i in range(k + 2, blocks)]
        work += [functools.partial(update_right, i, j) for j in range(k + 1, blocks) for i in range(max(j, k + 2), blocks)]
        work += [functools.partial(update_left, i, k) for i in range(k + 1, blocks)]
        return work + [functools.partial(clear_right, k)]

    for k in range(blocks):
        work = []
        if k:
            column_panel(k, k - 1)
            update_right(k, k)
            work = later(k - 1)
        tiles = [x_ref[BLOCK * k + 8 * m : BLOCK * k + 8 * (m + 1), at(k)] for m in range(BLOCK // 8)]
        for m, tile in enumerate(factor_block(tiles, work + extra(k), spread_ref)):
            x_ref[BLOCK * k + 8 * m : BLOCK * k + 8 * (m + 1), at(k)] = tile
    finish_rows(blocks - 1)


def place_strips(pos_ref, mine_ref, other_ref, to_ref):
    for distance in range(mine_ref.shape[0]):
        x = (pos_ref[0] + distance) % 4
        for z in range(mine_ref.shape[1]):
            for source, core in ((mine_ref, pos_ref[2]), (other_ref, 1 - pos_ref[2])):
                start = pl.multiple_of((4 * z + x) * SHARE + core * (SHARE // 2), SHARE // 2)
                to_ref[pl.ds(start, SHARE // 2), :] = source[distance, z]


def first_factor_kernel(pos_ref, mine_ref, other_ref, x_ref, panel_ref, spread_ref):
    place_strips(pos_ref, mine_ref, other_ref, x_ref)
    factor_in_place(x_ref, panel_ref, spread_ref, lambda k: [])


def second_factor_kernel(pos_ref, mine_ref, other_ref, first_ref, out_ref, a_ref, x_ref, l_ref, r_ref, panel_ref, spread_ref):
    size = first_ref.shape[0]
    blocks = size // BLOCK
    place_strips(pos_ref, mine_ref, other_ref, a_ref)
    at = blocks_at
    wide = 2 * BLOCK

    def left(i):
        for k in range(size // wide):
            columns, upto = slice(wide * k, wide * (k + 1)), slice(0, wide * (k + 1))
            l_ref[at(i), columns] = dot(a_ref[at(i), upto], first_ref[columns, upto], (1, 1), HIGHEST)

    def remainder(i, j):
        whole = a_ref[at(i), size + BLOCK * j : size + BLOCK * (j + 1)]
        x_ref[at(i), at(j)] = whole - dot(l_ref[at(i), :], l_ref[at(j), :], (1, 1), HIGHEST)

    def product(i, k):
        columns, after = slice(wide * k, wide * (k + 1)), slice(wide * k, size)
        r_ref[at(i), columns] = dot3(split(l_ref[at(i), after]), split(first_ref[after, columns]))

    def lower_left(i):
        upto = slice(0, BLOCK * (i + 1))
        out_ref[size + BLOCK * i : size + BLOCK * (i + 1), :size] = -dot3(split(x_ref[at(i), upto]), split(r_ref[upto, :]))

    def upper(i):
        out_ref[at(i), :size] = first_ref[at(i), :]
        out_ref[at(i), size:] = jnp.zeros((BLOCK, size), F32)

    def extra(k):
        work = []
        if k == 0:
            work += [functools.partial(left, i) for i in range(1, blocks)]
            work += [functools.partial(remainder, i, j) for j in range(blocks) for i in range(max(j, 1), blocks)]
        else:
            work += [functools.partial(lower_left, k - 1)]
        work += [functools.partial(product, k, i) for i in range(size // wide)]
        return work + [functools.partial(upper, k)]

    left(0)
    remainder(0, 0)
    factor_in_place(x_ref, panel_ref, spread_ref, extra)
    lower_left(blocks - 1)
    out_ref[size:, size:] = x_ref[...]


def first_factor(pos, mine, other):
    size = mine.shape[3]
    return pl.pallas_call(
        first_factor_kernel,
        out_shape=jax.ShapeDtypeStruct((size, size), F32),
        in_specs=[SMEM, VMEM, VMEM],
        out_specs=VMEM,
        scratch_shapes=[pltpu.VMEM((size, BLOCK), F32), SPREAD],
        compiler_params=params(16),
        cost_estimate=pl.CostEstimate(flops=size * size, bytes_accessed=8 * size * size, transcendentals=size),
    )(pos, mine, other)


def second_factor(pos, mine, other, first):
    size = first.shape[0]
    square = pltpu.VMEM((size, size), F32)
    return pl.pallas_call(
        second_factor_kernel,
        out_shape=jax.ShapeDtypeStruct((2 * size, 2 * size), F32),
        in_specs=[SMEM, VMEM, VMEM, VMEM],
        out_specs=VMEM,
        scratch_shapes=[pltpu.VMEM((size, 2 * size), F32), square, square, square, pltpu.VMEM((size, BLOCK), F32), SPREAD],
        compiler_params=params(24),
        cost_estimate=pl.CostEstimate(flops=size * size, bytes_accessed=8 * size * size, transcendentals=size),
    )(pos, mine, other, first)


def arrange_kernel(axis, pos_ref, *refs):
    for distance in range(4):
        refs[4][(pos_ref[axis] + distance) % 4] = refs[distance][...]


def arrange(pos, axis, blocks):
    block = blocks[0]
    return pl.pallas_call(
        functools.partial(arrange_kernel, axis),
        out_shape=jax.ShapeDtypeStruct((4,) + block.shape, F32),
        in_specs=[SMEM] + [VMEM] * 4,
        out_specs=VMEM,
        compiler_params=params(4),
        cost_estimate=pl.CostEstimate(flops=0, bytes_accessed=32 * block.size, transcendentals=0),
    )(pos, *blocks)


def cut_kernel(first_ref, second_ref, upper_ref, lower_ref):
    half = upper_ref.shape[0]
    upper_ref[...] = first_ref[:half]
    lower_ref[...] = second_ref[half:]


def cut(first, second):
    half = jax.ShapeDtypeStruct((first.shape[0] // 2,) + first.shape[1:], F32)
    return pl.pallas_call(
        cut_kernel,
        out_shape=[half] * 2,
        in_specs=[VMEM] * 2,
        out_specs=[VMEM] * 2,
        compiler_params=params(4),
        cost_estimate=pl.CostEstimate(flops=0, bytes_accessed=8 * first.size, transcendentals=0),
    )(first, second)


def order_strips_kernel(pos_ref, *refs):
    left_ref, rest_ref = refs[4:]
    left = left_ref.shape[2]
    for distance in range(4):
        z = (pos_ref[1] + distance) % 4

        @pl.when(z < 2)
        def _(distance=distance, z=z):
            left_ref[z % 2] = refs[distance][:, :left]

        @pl.when(z >= 2)
        def _(distance=distance, z=z):
            rest_ref[z % 2] = refs[distance][...]


def order_strips(pos, strips):
    rows, columns = strips[0].shape
    return pl.pallas_call(
        order_strips_kernel,
        out_shape=[jax.ShapeDtypeStruct((2, rows, columns // 2), F32), jax.ShapeDtypeStruct((2, rows, columns), F32)],
        in_specs=[SMEM] + [VMEM] * 4,
        out_specs=[VMEM] * 2,
        compiler_params=params(4),
        cost_estimate=pl.CostEstimate(flops=0, bytes_accessed=32 * rows * columns, transcendentals=0),
    )(pos, *strips)


def piece_rows(ring, place, z):
    if ring == 0:
        return pl.ds(pl.multiple_of(place * 4 * SHARE, 4 * SHARE), 4 * SHARE)
    return pl.ds(pl.multiple_of((4 * z + place) * SHARE, SHARE), SHARE)


def add_product(ring, place, product, to_ref):
    if ring == 0:
        to_ref[piece_rows(0, place, 0), :] += product
    else:
        for z in range(4):
            to_ref[piece_rows(1, place, z), :] += product[SHARE * z : SHARE * (z + 1), :]


def early_gram_kernel(distances, first, pos_ref, f_ref, *refs):
    count = 2 * len(distances)
    pieces, refs = refs[:count], refs[count:]
    examples = f_ref.shape[0] // 2
    if first:
        out_ref = refs[0]
        out_ref[...] = jnp.zeros_like(out_ref)
    else:
        before_ref, out_ref, strip_ref = refs
        out_ref[...] = before_ref[...]
    for ring in range(2):
        features = split(f_ref[examples * ring : examples * (ring + 1), :])
        for n, distance in enumerate(distances):
            product = dot3(split(pieces[2 * n + ring][...].reshape(4 * SHARE, examples)), features)
            add_product(ring, (pos_ref[1 - ring] + distance) % 4, product, out_ref)
    if not first:
        for i in range(out_ref.shape[0] // BLOCK):
            at = slice(BLOCK * i, BLOCK * (i + 1))
            strip_ref[:, at] = out_ref[at, :BLOCK].T[:SHARE]


def early_gram(pos, features, distances, pieces, before=None):
    columns = features.shape[1]
    total = jax.ShapeDtypeStruct((P_SIZE, columns), F32)
    strip = jax.ShapeDtypeStruct((SHARE, P_SIZE), F32)
    extra = () if before is None else (before,)
    return pl.pallas_call(
        functools.partial(early_gram_kernel, distances, before is None),
        out_shape=total if before is None else [total, strip],
        in_specs=[SMEM] + [VMEM] * (1 + len(pieces) + len(extra)),
        out_specs=VMEM if before is None else [VMEM, VMEM],
        compiler_params=params(16),
        cost_estimate=pl.CostEstimate(
            flops=6 * features.size * 4 * SHARE * len(distances), bytes_accessed=4 * features.size, transcendentals=0
        ),
    )(pos, features, *pieces, *extra)


def strip_kernel(total, pos_ref, damping_ref, own_ref, early_ref, *refs):
    halves, (mine_ref, other_ref, strip_ref) = refs[:4], refs[4:]
    wide = 4 * SHARE
    examples = own_ref.shape[1] // 2
    strip_ref[...] = early_ref[...]
    for ring in range(2):
        own = split(own_ref[:, examples * ring : examples * (ring + 1)])
        parts = [half[...].reshape(wide // 2, examples) for half in halves[2 * ring : 2 * ring + 2]]
        product = jnp.concatenate([dot3(own, split(part), (1, 1)) for part in parts], axis=1)
        place = (pos_ref[1 - ring] + 2) % 4
        if ring == 0:
            strip_ref[:, piece_rows(0, place, 0)] += product
        else:
            lane = lax.broadcasted_iota(jnp.int32, (SHARE, wide), 1)
            for z in range(4):
                part = jnp.concatenate([product[:, SHARE * z : SHARE * (z + 1)]] * 4, axis=1)
                strip_ref[:, wide * z : wide * (z + 1)] += jnp.where(lane // SHARE == place, part, 0.0)
    half = mine_ref.shape[0]
    start = pl.multiple_of(pos_ref[2] * half, half)
    row = lax.broadcasted_iota(jnp.int32, mine_ref.shape, 0) + (4 * pos_ref[1] + pos_ref[0]) * SHARE + start
    column = lax.broadcasted_iota(jnp.int32, mine_ref.shape, 1)
    damping = jnp.where((row == column) & (pos_ref[3] < 2), damping_ref[...], 0.0)
    mine_ref[...] = strip_ref[pl.ds(start, half), :] * (1.0 / total) + damping
    other_ref[...] = strip_ref[pl.ds(half - start, half), :] * (1.0 / total)


def strip_product(total, pos, damping, own_t, early, halves):
    return pl.pallas_call(
        functools.partial(strip_kernel, total),
        out_shape=[jax.ShapeDtypeStruct((SHARE // 2, P_SIZE), F32)] * 2,
        in_specs=[SMEM] + [VMEM] * 7,
        out_specs=[VMEM] * 2,
        scratch_shapes=[pltpu.VMEM(early.shape, F32)],
        compiler_params=params(12),
        cost_estimate=pl.CostEstimate(flops=24 * own_t.size * 256, bytes_accessed=16 * own_t.size, transcendentals=0),
    )(pos, damping[None, :], own_t, early, *halves)


def add_kernel(a_ref, b_ref, sum_ref):
    sum_ref[...] = a_ref[...] + b_ref[...]


def add(a, b):
    return pl.pallas_call(
        add_kernel,
        out_shape=jax.ShapeDtypeStruct(a.shape, F32),
        in_specs=[VMEM] * 2,
        out_specs=VMEM,
        compiler_params=params(4),
        cost_estimate=pl.CostEstimate(flops=a.size, bytes_accessed=12 * a.size, transcendentals=0),
    )(a, b)


def sum_in_order_kernel(pos_ref, *refs):
    parts_ref = refs[5]
    for distance in range(4):
        parts_ref[(pos_ref[3] // 2 + distance) % 4] = refs[distance][...]
    refs[4][...] = (parts_ref[0] + parts_ref[1]) + (parts_ref[2] + parts_ref[3])


def sum_in_order(pos, parts):
    shape = parts[0].shape
    return pl.pallas_call(
        sum_in_order_kernel,
        out_shape=jax.ShapeDtypeStruct(shape, F32),
        in_specs=[SMEM] + [VMEM] * 4,
        out_specs=VMEM,
        scratch_shapes=[pltpu.VMEM((4,) + shape, F32)],
        compiler_params=params(4),
        cost_estimate=pl.CostEstimate(flops=3 * parts[0].size, bytes_accessed=20 * parts[0].size, transcendentals=0),
    )(pos, *parts)


def stack_kernel(*refs):
    for i, ref in enumerate(refs[:-1]):
        refs[-1][i] = ref[...]


def stack(arrays):
    return pl.pallas_call(
        stack_kernel,
        out_shape=jax.ShapeDtypeStruct((len(arrays),) + arrays[0].shape, F32),
        in_specs=[VMEM] * len(arrays),
        out_specs=VMEM,
        compiler_params=params(4),
        cost_estimate=pl.CostEstimate(flops=0, bytes_accessed=32 * arrays[0].size, transcendentals=0),
    )(*arrays)


def late_gram_kernel(total, pos_ref, damping_ref, early_ref, f_ref, *refs):
    halves, (mine_ref, other_ref, sum_ref) = refs[:4], refs[4:]
    wide = 4 * SHARE
    examples = f_ref.shape[0] // 2
    half = mine_ref.shape[0]
    sum_ref[...] = early_ref[...]
    for ring in range(2):
        parts = [part[...].reshape(wide // 2, examples) for part in halves[2 * ring : 2 * ring + 2]]
        features = split(f_ref[examples * ring : examples * (ring + 1), :])
        product = dot3(split(jnp.concatenate(parts, axis=0)), features)
        add_product(ring, (pos_ref[1 - ring] + 2) % 4, product, sum_ref)
    for to_ref, core in ((mine_ref, pos_ref[2]), (other_ref, 1 - pos_ref[2])):
        columns = pl.ds(pl.multiple_of(core * half, half), half)
        for i in range(sum_ref.shape[0] // BLOCK):
            at = slice(BLOCK * i, BLOCK * (i + 1))
            to_ref[:, at] = sum_ref[at, columns].T * (1.0 / total)

    @pl.when(pos_ref[3] == 0)
    def _():
        shape = (SHARE, mine_ref.shape[1])
        row = lax.broadcasted_iota(jnp.int32, shape, 0) + (4 * pos_ref[1] + pos_ref[0]) * SHARE
        column = lax.broadcasted_iota(jnp.int32, shape, 1)
        mine_ref[:SHARE, :] += jnp.where(row == column, damping_ref[...], 0.0)


def late_gram(total, pos, damping, early, features, halves):
    rows, columns = features.shape
    return pl.pallas_call(
        functools.partial(late_gram_kernel, total),
        out_shape=[jax.ShapeDtypeStruct((columns // 2, P_SIZE), F32)] * 2,
        in_specs=[SMEM] + [VMEM] * 7,
        out_specs=[VMEM] * 2,
        scratch_shapes=[pltpu.VMEM(early.shape, F32)],
        compiler_params=params(16),
        cost_estimate=pl.CostEstimate(flops=6 * features.size * 256, bytes_accessed=8 * features.size, transcendentals=0),
    )(pos, damping[None, :], early, features, *halves)


def factor_kernel(damped_ref, last_ref, inverse_ref, factor_ref):
    size = inverse_ref.shape[0]
    wide = 4 * SHARE
    damped = split(damped_ref[...] + last_ref[...])
    for k in range(size // wide):
        at, upto = slice(wide * k, wide * (k + 1)), slice(0, wide * (k + 1))
        factor_ref[:, at] = dot3(tuple(part[:, upto] for part in damped), split(inverse_ref[at, upto]), (1, 1))


def factor_product(damped, last, inverse):
    return pl.pallas_call(
        factor_kernel,
        out_shape=jax.ShapeDtypeStruct(damped.shape, F32),
        in_specs=[VMEM] * 3,
        out_specs=VMEM,
        compiler_params=params(16),
        cost_estimate=pl.CostEstimate(flops=4 * damped.size * P_SIZE, bytes_accessed=12 * damped.size, transcendentals=0),
    )(damped, last, inverse)


def weights_kernel(pos_ref, inverse_ref, *refs):
    tests, (weights_ref, mixed_ref, tests_ref, solved_ref) = refs[:4], refs[4:]
    size = inverse_ref.shape[0]
    wide = 4 * SHARE
    blocks = size // wide
    for distance, block in enumerate(tests):
        first = (pos_ref[3] + 2 * distance) % 8
        columns = block.shape[2]
        for i, place in enumerate((first, first + 1 - 2 * pos_ref[2])):
            tests_ref[:, pl.ds(pl.multiple_of(place * columns, columns), columns)] = block[i]
    for k in range(blocks):
        at, upto = slice(wide * k, wide * (k + 1)), slice(0, wide * (k + 1))
        solved_ref[:, at] = dot3(split(tests_ref[:, upto]), split(inverse_ref[at, upto]), (1, 1))
    for k in range(blocks):
        at, after = slice(wide * k, wide * (k + 1)), slice(wide * k, size)
        weights_ref[:, at] = dot3(split(solved_ref[:, after]), split(inverse_ref[after, at])) * (1.0 / math.sqrt(size))
    weights = weights_ref[...]
    for x in range(4):
        parts = [weights[:, wide * z + SHARE * x : wide * z + SHARE * (x + 1)] for z in range(4)]
        mixed_ref[:, wide * x : wide * (x + 1)] = jnp.concatenate(parts, axis=1)


def weights_product(pos, inverse, tests):
    size = inverse.shape[0]
    count = tests[0].shape[1]
    weights = jax.ShapeDtypeStruct((count, size), F32)
    return pl.pallas_call(
        weights_kernel,
        out_shape=[weights] * 2,
        in_specs=[SMEM] + [VMEM] * 5,
        out_specs=[VMEM] * 2,
        scratch_shapes=[pltpu.VMEM((count, size), F32)] * 2,
        compiler_params=params(16),
        cost_estimate=pl.CostEstimate(flops=6 * size * size * count, bytes_accessed=8 * size * size, transcendentals=0),
    )(pos, inverse, *tests)


def scores_columns(ring, distances, pos_ref, weights_ref, pieces, scores_ref, total_ref, sems):
    wide = 4 * SHARE
    examples = pieces[0].shape[2]
    whole = [piece[...].reshape(wide, examples) for piece in pieces[: len(distances)]]
    whole.append(jnp.concatenate([part[...] for part in pieces[len(distances) :]], axis=0).reshape(wide, examples))
    places = [pl.multiple_of((pos_ref[1 - ring] + distance) % 4 * wide, wide) for distance in distances + (2,)]
    weights = [split(weights_ref[:, pl.ds(place, wide)]) for place in places]
    copies = []
    for k in range(examples // wide):
        at = slice(wide * k, wide * (k + 1))
        total = None
        for weight, piece in zip(weights, whole):
            part = dot3(weight, split(piece[:, at]))
            total = part if total is None else total + part
        total_ref[:, at] = total
        target = scores_ref.at[:, examples * ring + wide * k : examples * ring + wide * (k + 1)]
        copies.append(pltpu.make_async_copy(total_ref.at[:, at], target, sems.at[k]))
        copies[-1].start()
    return copies


def first_scores_kernel(distances, pos_ref, weights_ref, *refs):
    pieces, (scores_ref, total_ref, sems) = refs[: len(distances) + 2], refs[len(distances) + 2 :]
    for copy in scores_columns(0, distances, pos_ref, weights_ref, pieces, scores_ref, total_ref, sems):
        copy.wait()


def second_scores_kernel(distances, pos_ref, weights_ref, mine_ref, other_ref, before_ref, *refs):
    del before_ref
    pieces, refs = refs[: len(distances) + 2], refs[len(distances) + 2 :]
    scores_ref, factor_ref, total_ref, sems, factor_sems = refs
    half = mine_ref.shape[0]
    copies = []
    for i, (source, core) in enumerate(((mine_ref, pos_ref[2]), (other_ref, 1 - pos_ref[2]))):
        target = factor_ref.at[pl.ds(pl.multiple_of(core * half, half), half)]
        copies.append(pltpu.make_async_copy(source, target, factor_sems.at[i]))
        copies[-1].start()
    copies += scores_columns(1, distances, pos_ref, weights_ref, pieces, scores_ref, total_ref, sems)
    for copy in copies:
        copy.wait()


def scores_scratch(weights, pieces):
    examples = pieces[0].shape[2]
    return [pltpu.VMEM((weights.shape[0], examples), F32), pltpu.SemaphoreType.DMA((examples // (4 * SHARE),))]


def first_scores(pos, weights, distances, pieces):
    return pl.pallas_call(
        functools.partial(first_scores_kernel, distances),
        out_shape=jax.ShapeDtypeStruct((weights.shape[0], 2 * pieces[0].shape[2]), F32),
        in_specs=[SMEM] + [VMEM] * (1 + len(pieces)),
        out_specs=ANY,
        scratch_shapes=scores_scratch(weights, pieces),
        compiler_params=params(16),
        cost_estimate=pl.CostEstimate(flops=6 * P_SIZE * P_SIZE * 256, bytes_accessed=4 * P_SIZE * P_SIZE, transcendentals=0),
    )(pos, weights, *pieces)


def second_scores(pos, weights, mine, other, before, distances, pieces):
    return pl.pallas_call(
        functools.partial(second_scores_kernel, distances),
        out_shape=[
            jax.ShapeDtypeStruct(before.shape, F32),
            jax.ShapeDtypeStruct((2 * mine.shape[0], mine.shape[1]), F32),
        ],
        in_specs=[SMEM] + [VMEM] * 3 + [ANY] + [VMEM] * len(pieces),
        out_specs=[ANY] * 2,
        input_output_aliases={4: 0},
        scratch_shapes=scores_scratch(weights, pieces) + [pltpu.SemaphoreType.DMA((2,))],
        compiler_params=params(16),
        cost_estimate=pl.CostEstimate(flops=6 * P_SIZE * P_SIZE * 256, bytes_accessed=4 * P_SIZE * P_SIZE, transcendentals=0),
    )(pos, weights, mine, other, before, *pieces)


def hop(axis, move):
    size = {"test": 16, "train": 8}[axis]
    return lambda value: lax.ppermute(value, axis, [(i, move(i)) for i in range(size)])


TO_X = {d: hop("test", lambda s, d=d: s // 4 * 4 + (s + d) % 4) for d in (1, 2, 3)}
TO_Z = {d: hop("test", lambda s, d=d: (s + 4 * d) % 16) for d in (1, 2, 3)}
TO_Y = {d: hop("train", lambda t, d=d: (t + 2 * d) % 8) for d in (1, 2, 3)}
SWAP_CORE = hop("train", lambda t: t ^ 1)
SWAP_Y1 = hop("train", lambda t: t ^ 2)
SWAP_Y2 = hop("train", lambda t: t ^ 4)


def ring(value, to):
    return [value, to[3](value), to[2](value), to[1](value)]


def relay(ahead, behind, to):
    upper, lower = cut(ahead, behind)
    return to[3](upper), to[1](lower)


def per_device(train_features, test_panel, damping):
    test, train = lax.axis_index("test"), lax.axis_index("train")
    pos = jnp.stack([test % 4, test // 4, train % 2, train]).astype(jnp.int32)
    rows_dev = train_features.shape[0]
    train_total = rows_dev * lax.axis_size("train")

    own_t = train_features[:, :SHARE].T
    first, second = own_t[:, : rows_dev // 2], own_t[:, rows_dev // 2 :]
    pos, first, second = lax.optimization_barrier((pos, first, second))
    own_row = arrange(pos, 0, ring(first, TO_X))
    own_column = arrange(pos, 1, ring(second, TO_Z))
    near_rows, near_columns = [TO_Z[3](own_row), TO_Z[1](own_row)], [TO_X[3](own_column), TO_X[1](own_column)]
    early = early_gram(pos, train_features, (0,), [own_row, own_column])
    early, test_panel = lax.optimization_barrier((early, test_panel))
    tests = ring(stack([test_panel, SWAP_CORE(test_panel)]), TO_Y)
    early, near_columns = lax.optimization_barrier((early, near_columns))
    far_rows, far_columns = relay(*near_rows, TO_Z), relay(*near_columns, TO_X)
    near = [near_rows[0], near_columns[0], near_rows[1], near_columns[1]]
    far = [*far_rows, *far_columns]
    early, strip = early_gram(pos, train_features, (1, 3), near, early)
    strip, tests = lax.optimization_barrier((strip, tests))

    strip, other_strip = strip_product(train_total, pos, damping, own_t, strip, far)
    strip = add(strip, SWAP_CORE(other_strip))
    strips = ring(strip, TO_Y)
    term, other_term = late_gram(train_total, pos, damping, early, train_features, far)
    strips, term, other_term = lax.optimization_barrier((strips, term, other_term))
    strip = sum_in_order(pos, strips)

    damped = add(term, SWAP_CORE(other_term))
    left, rest = order_strips(pos, ring(strip, TO_Z))
    left, damped = lax.optimization_barrier((left, damped))
    damped_y1 = SWAP_Y1(damped)
    mine = stack(ring(left, TO_X))
    mine, rest = lax.optimization_barrier((mine, rest))
    later = ring(rest, TO_X)
    first = first_factor(pos, mine, SWAP_CORE(mine))
    first, later, damped_y1 = lax.optimization_barrier((first, later, damped_y1))
    damped = add(damped, damped_y1)
    later = stack(later)
    later_other = SWAP_CORE(later)
    later, damped = lax.optimization_barrier((later, damped))
    damped_y2 = SWAP_Y2(damped)
    inverse = second_factor(pos, later, later_other, first)
    weights, mixed = weights_product(pos, inverse, tests)
    weights, damped, damped_y2 = lax.optimization_barrier((weights, damped, damped_y2))
    factor = factor_product(damped, damped_y2, inverse)
    other_factor = SWAP_CORE(factor)
    weights, factor = lax.optimization_barrier((weights, factor))
    scores = first_scores(pos, weights, (0, 1, 3), [own_row, *near_rows, *far_rows])
    scores, other_factor = lax.optimization_barrier((scores, other_factor))
    columns = [own_column, *near_columns, *far_columns]
    return tuple(second_scores(pos, mixed, factor, other_factor, scores, (0, 1, 3), columns))


def solution(mesh):
    in_specs = (P("train", "test"), P("test", "train"), P())
    out_specs = (P("test", "train"), P("test", None))
    return jax.shard_map(
        per_device, mesh=mesh, in_specs=in_specs, out_specs=out_specs, check_vma=False
    )
```

```python
import functools
import math

import jax
import jax.numpy as jnp
from jax import lax
from jax.experimental import pallas as pl
from jax.experimental.pallas import tpu as pltpu
from jax.sharding import PartitionSpec as P

P_SIZE = 1024
BLOCK = 128
SHARE = 64
F32 = jnp.float32
BF16 = jnp.bfloat16
VMEM = pl.BlockSpec(memory_space=pltpu.VMEM)
SMEM = pl.BlockSpec(memory_space=pltpu.SMEM)
ANY = pl.BlockSpec(memory_space=pl.ANY)
SPREAD = pltpu.VMEM((2, 64, BLOCK), F32)


def params(mebibytes):
    return pltpu.CompilerParams(vmem_limit_bytes=mebibytes * 1024 * 1024)


def dot(a, b, contract=(1, 0)):
    return lax.dot_general(a, b, ((contract[:1], contract[1:]), ((), ())), preferred_element_type=F32)


def split(value):
    high = value.astype(BF16)
    return high, (value - high.astype(F32)).astype(BF16)


def dot3(a, b, contract=(1, 0)):
    return dot(a[0], b[0], contract) + (dot(a[0], b[1], contract) + dot(a[1], b[0], contract))


def split3(value):
    high, rest = split(value)
    return high, rest, (value - high.astype(F32) - rest.astype(F32)).astype(BF16)


def dot6(a, b, contract=(1, 0)):
    ca, cb = contract
    wide = jnp.concatenate([jnp.concatenate(b[:2], axis=cb), jnp.concatenate(b[1::-1], axis=cb)], axis=1 - cb)
    both = dot(jnp.concatenate(a[:2], axis=ca), wide, contract)
    small = dot(jnp.concatenate(a[::2], axis=ca), jnp.concatenate(b[2::-2], axis=cb), contract)
    half = both.shape[1] // 2
    return both[:, :half] + (both[:, half:] + small)


def factor_block(tiles, work, spread_ref):
    tiles = list(tiles)
    count = len(tiles)
    lane = lax.broadcasted_iota(jnp.int32, (8, BLOCK), 1)
    row = lax.broadcasted_iota(jnp.int32, (8, BLOCK), 0)
    share = -(-len(work) // count)

    def spread(value):
        return jnp.broadcast_to(value, (8, BLOCK))

    for group in range(count):
        first = 8 * group
        own = tiles[group]
        below = range(group + 1, count)
        columns = [spread(own[:, first + j : first + j + 1]) for j in range(8)]
        for j in range(8):
            spread_ref[group % 2, 8 * j : 8 * (j + 1), :] = columns[j]
        pivots = [[spread(spread_ref[group % 2, 8 * j + i : 8 * j + i + 1, :]) for j in range(i + 1)] for i in range(8)]
        inside = (lane >= first) & (lane < first + 8)
        own = jnp.where(inside, (lane - first == row).astype(F32), own)
        lines = [spread(own[i : i + 1, :]) for i in range(8)]
        factors = {m: [spread(tiles[m][:, first + j : first + j + 1]) for j in range(8)] for m in below}
        for m in below:
            tiles[m] = jnp.where(inside, 0.0, tiles[m])
        done = None
        for k in range(8):
            scale = lax.rsqrt(pivots[k][k])
            line = lines[k] * scale
            ratios = {i: pivots[i][k] * scale for i in range(k + 1, 8)}
            for i in range(k + 1, 8):
                for j in range(k + 1, i + 1):
                    pivots[i][j] = pivots[i][j] - ratios[i] * ratios[j]
                lines[i] = lines[i] - ratios[i] * line
            done = line if done is None else jnp.where(row == k, line, done)
            for m in below:
                factor = factors[m][k] * scale
                tiles[m] = tiles[m] - factor * line
                for i in range(k + 1, 8):
                    factors[m][i] = factors[m][i] - factor * ratios[i]
        tiles[group] = done
        for step in work[share * group : share * (group + 1)]:
            step()
    return [jnp.where(lane < 8 * group + 8, tiles[group], 0.0) for group in range(count)]


def blocks_at(i):
    return slice(BLOCK * i, BLOCK * (i + 1))


def factor_in_place(x_ref, spread_ref, extra):
    size = x_ref.shape[0]
    blocks = size // BLOCK
    at = blocks_at

    inverses, panels, rows = {}, {}, {}

    def inverse(k):
        if k not in inverses:
            inverses[k] = split3(x_ref[at(k), at(k)])
        return inverses[k]

    def finish_rows(k):
        left = x_ref[at(k), : BLOCK * k]
        left = dot6(inverse(k), split3(left))
        x_ref[at(k), : BLOCK * k] = left
        rows[k] = tuple(jnp.concatenate(parts, axis=1) for parts in zip(split3(left), inverse(k)))

    def column_panel(i, k):
        panels[i, k] = split3(dot6(split3(x_ref[at(i), at(k)]), inverse(k), (1, 1)))

    def update_right(i, j, k):
        x_ref[at(i), at(j)] -= dot6(panels[i, k], panels[j, k], (1, 1))

    def update_left(i, k):
        change = dot6(panels[i, k], rows[k] if k else inverse(k))
        if k:
            x_ref[at(i), : BLOCK * k] -= change[:, : BLOCK * k]
        x_ref[at(i), at(k)] = -change[:, BLOCK * k :]

    def clear_right(k):
        x_ref[at(k), BLOCK * (k + 1) :] = jnp.zeros((BLOCK, size - BLOCK * (k + 1)), F32)

    def later(k):
        work = [functools.partial(finish_rows, k)] if k else []
        work += [functools.partial(column_panel, i, k) for i in range(k + 2, blocks)]
        work += [functools.partial(update_right, i, j, k) for j in range(k + 1, blocks) for i in range(max(j, k + 2), blocks)]
        work += [functools.partial(update_left, i, k) for i in range(k + 1, blocks)]
        return work + [functools.partial(clear_right, k)]

    for k in range(blocks):
        work = []
        if k:
            column_panel(k, k - 1)
            update_right(k, k, k - 1)
            work = later(k - 1)
        tiles = [x_ref[BLOCK * k + 8 * m : BLOCK * k + 8 * (m + 1), at(k)] for m in range(BLOCK // 8)]
        for m, tile in enumerate(factor_block(tiles, work + extra(k), spread_ref)):
            x_ref[BLOCK * k + 8 * m : BLOCK * k + 8 * (m + 1), at(k)] = tile
    finish_rows(blocks - 1)


def place_strips(pos_ref, mine_ref, other_ref, to_ref):
    for distance in range(mine_ref.shape[0]):
        x = (pos_ref[0] + distance) % 4
        for z in range(mine_ref.shape[1]):
            for source, core in ((mine_ref, pos_ref[2]), (other_ref, 1 - pos_ref[2])):
                start = pl.multiple_of((4 * z + x) * SHARE + core * (SHARE // 2), SHARE // 2)
                to_ref[pl.ds(start, SHARE // 2), :] = source[distance, z]


def first_factor_kernel(pos_ref, mine_ref, other_ref, x_ref, spread_ref):
    place_strips(pos_ref, mine_ref, other_ref, x_ref)
    factor_in_place(x_ref, spread_ref, lambda k: [])


def second_factor_kernel(pos_ref, mine_ref, other_ref, first_ref, out_ref, a_ref, x_ref, spread_ref):
    size = first_ref.shape[0]
    blocks = size // BLOCK
    place_strips(pos_ref, mine_ref, other_ref, a_ref)
    at = blocks_at
    wide = 2 * BLOCK

    chunks = range(size // wide)
    lefts, products, columns, factors = {}, {}, {}, {}

    def left(i):
        parts = []
        for k in chunks:
            upto = slice(0, wide * (k + 1))
            if k not in factors:
                factors[k] = split3(first_ref[wide * k : wide * (k + 1), upto])
            parts.append(dot6(split3(a_ref[at(i), upto]), factors[k], (1, 1)))
        lefts[i] = split3(jnp.concatenate(parts, axis=1))

    def remainder(i, j):
        whole = a_ref[at(i), size + BLOCK * j : size + BLOCK * (j + 1)]
        x_ref[at(i), at(j)] = whole - dot6(lefts[i], lefts[j], (1, 1))

    def product(i):
        parts = []
        for k in chunks:
            after = slice(wide * k, size)
            if k not in columns:
                columns[k] = split(first_ref[after, wide * k : wide * (k + 1)])
            parts.append(dot3(tuple(part[:, after] for part in lefts[i][:2]), columns[k]))
        products[i] = split(jnp.concatenate(parts, axis=1))

    def lower_left(i):
        done = tuple(jnp.concatenate([products[j][part] for j in range(i + 1)], axis=0) for part in range(2))
        lower = dot3(split(x_ref[at(i), : BLOCK * (i + 1)]), done)
        out_ref[size + BLOCK * i : size + BLOCK * (i + 1), :size] = -lower

    def upper(i):
        out_ref[at(i), :size] = first_ref[at(i), :]
        out_ref[at(i), size:] = jnp.zeros((BLOCK, size), F32)

    def extra(k):
        work = []
        if k == 0:
            work += [functools.partial(left, i) for i in range(1, blocks)]
            work += [functools.partial(remainder, i, j) for j in range(blocks) for i in range(max(j, 1), blocks)]
        else:
            work += [functools.partial(lower_left, k - 1)]
        work += [functools.partial(product, k)]
        return work + [functools.partial(upper, k)]

    left(0)
    remainder(0, 0)
    factor_in_place(x_ref, spread_ref, extra)
    lower_left(blocks - 1)
    out_ref[size:, size:] = x_ref[...]


def first_factor(pos, mine, other):
    size = mine.shape[3]
    return pl.pallas_call(
        first_factor_kernel,
        out_shape=jax.ShapeDtypeStruct((size, size), F32),
        in_specs=[SMEM, VMEM, VMEM],
        out_specs=VMEM,
        scratch_shapes=[SPREAD],
        compiler_params=params(16),
        cost_estimate=pl.CostEstimate(flops=size * size, bytes_accessed=8 * size * size, transcendentals=size),
    )(pos, mine, other)


def second_factor(pos, mine, other, first):
    size = first.shape[0]
    return pl.pallas_call(
        second_factor_kernel,
        out_shape=jax.ShapeDtypeStruct((2 * size, 2 * size), F32),
        in_specs=[SMEM, VMEM, VMEM, VMEM],
        out_specs=VMEM,
        scratch_shapes=[pltpu.VMEM((size, 2 * size), F32), pltpu.VMEM((size, size), F32), SPREAD],
        compiler_params=params(24),
        cost_estimate=pl.CostEstimate(flops=size * size, bytes_accessed=8 * size * size, transcendentals=size),
    )(pos, mine, other, first)


def arrange_kernel(axis, pos_ref, *refs):
    for distance in range(4):
        refs[4][(pos_ref[axis] + distance) % 4] = refs[distance][...]


def arrange(pos, axis, blocks):
    block = blocks[0]
    return pl.pallas_call(
        functools.partial(arrange_kernel, axis),
        out_shape=jax.ShapeDtypeStruct((4,) + block.shape, F32),
        in_specs=[SMEM] + [VMEM] * 4,
        out_specs=VMEM,
        compiler_params=params(4),
        cost_estimate=pl.CostEstimate(flops=0, bytes_accessed=32 * block.size, transcendentals=0),
    )(pos, *blocks)


def cut_kernel(first_ref, second_ref, upper_ref, lower_ref):
    half = upper_ref.shape[0]
    upper_ref[...] = first_ref[:half]
    lower_ref[...] = second_ref[half:]


def cut(first, second):
    half = jax.ShapeDtypeStruct((first.shape[0] // 2,) + first.shape[1:], F32)
    return pl.pallas_call(
        cut_kernel,
        out_shape=[half] * 2,
        in_specs=[VMEM] * 2,
        out_specs=[VMEM] * 2,
        compiler_params=params(4),
        cost_estimate=pl.CostEstimate(flops=0, bytes_accessed=8 * first.size, transcendentals=0),
    )(first, second)


def order_strips_kernel(pos_ref, *refs):
    left_ref, rest_ref = refs[4:]
    left = left_ref.shape[2]
    for distance in range(4):
        z = (pos_ref[1] + distance) % 4

        @pl.when(z < 2)
        def _(distance=distance, z=z):
            left_ref[z % 2] = refs[distance][:, :left]

        @pl.when(z >= 2)
        def _(distance=distance, z=z):
            rest_ref[z % 2] = refs[distance][...]


def order_strips(pos, strips):
    rows, columns = strips[0].shape
    return pl.pallas_call(
        order_strips_kernel,
        out_shape=[jax.ShapeDtypeStruct((2, rows, columns // 2), F32), jax.ShapeDtypeStruct((2, rows, columns), F32)],
        in_specs=[SMEM] + [VMEM] * 4,
        out_specs=[VMEM] * 2,
        compiler_params=params(4),
        cost_estimate=pl.CostEstimate(flops=0, bytes_accessed=32 * rows * columns, transcendentals=0),
    )(pos, *strips)


def piece_rows(ring, place, z):
    if ring == 0:
        return pl.ds(pl.multiple_of(place * 4 * SHARE, 4 * SHARE), 4 * SHARE)
    return pl.ds(pl.multiple_of((4 * z + place) * SHARE, SHARE), SHARE)


def add_product(ring, place, product, to_ref):
    if ring == 0:
        to_ref[piece_rows(0, place, 0), :] += product
    else:
        for z in range(4):
            to_ref[piece_rows(1, place, z), :] += product[SHARE * z : SHARE * (z + 1), :]


def early_gram_kernel(distances, first, pos_ref, f_ref, *refs):
    count = 2 * len(distances)
    pieces, refs = refs[:count], refs[count:]
    examples = f_ref.shape[0] // 2
    if first:
        out_ref = refs[0]
        out_ref[...] = jnp.zeros_like(out_ref)
    else:
        before_ref, out_ref, strip_ref = refs
        out_ref[...] = before_ref[...]
    for ring in range(2):
        features = split(f_ref[examples * ring : examples * (ring + 1), :])
        for n, distance in enumerate(distances):
            product = dot3(split(pieces[2 * n + ring][...].reshape(4 * SHARE, examples)), features)
            add_product(ring, (pos_ref[1 - ring] + distance) % 4, product, out_ref)
    if not first:
        for i in range(out_ref.shape[0] // BLOCK):
            at = slice(BLOCK * i, BLOCK * (i + 1))
            strip_ref[:, at] = out_ref[at, :BLOCK].T[:SHARE]


def early_gram(pos, features, distances, pieces, before=None):
    columns = features.shape[1]
    total = jax.ShapeDtypeStruct((P_SIZE, columns), F32)
    strip = jax.ShapeDtypeStruct((SHARE, P_SIZE), F32)
    extra = () if before is None else (before,)
    return pl.pallas_call(
        functools.partial(early_gram_kernel, distances, before is None),
        out_shape=total if before is None else [total, strip],
        in_specs=[SMEM] + [VMEM] * (1 + len(pieces) + len(extra)),
        out_specs=VMEM if before is None else [VMEM, VMEM],
        compiler_params=params(16),
        cost_estimate=pl.CostEstimate(
            flops=6 * features.size * 4 * SHARE * len(distances), bytes_accessed=4 * features.size, transcendentals=0
        ),
    )(pos, features, *pieces, *extra)


def strip_kernel(total, pos_ref, damping_ref, own_ref, early_ref, *refs):
    halves, (mine_ref, other_ref, strip_ref) = refs[:4], refs[4:]
    wide = 4 * SHARE
    examples = own_ref.shape[1] // 2
    strip_ref[...] = early_ref[...]
    for ring in range(2):
        own = split(own_ref[:, examples * ring : examples * (ring + 1)])
        parts = [half[...].reshape(wide // 2, examples) for half in halves[2 * ring : 2 * ring + 2]]
        product = jnp.concatenate([dot3(own, split(part), (1, 1)) for part in parts], axis=1)
        place = (pos_ref[1 - ring] + 2) % 4
        if ring == 0:
            strip_ref[:, piece_rows(0, place, 0)] += product
        else:
            lane = lax.broadcasted_iota(jnp.int32, (SHARE, wide), 1)
            for z in range(4):
                part = jnp.concatenate([product[:, SHARE * z : SHARE * (z + 1)]] * 4, axis=1)
                strip_ref[:, wide * z : wide * (z + 1)] += jnp.where(lane // SHARE == place, part, 0.0)
    half = mine_ref.shape[0]
    start = pl.multiple_of(pos_ref[2] * half, half)
    row = lax.broadcasted_iota(jnp.int32, mine_ref.shape, 0) + (4 * pos_ref[1] + pos_ref[0]) * SHARE + start
    column = lax.broadcasted_iota(jnp.int32, mine_ref.shape, 1)
    damping = jnp.where((row == column) & (pos_ref[3] < 2), damping_ref[...], 0.0)
    mine_ref[...] = strip_ref[pl.ds(start, half), :] * (1.0 / total) + damping
    other_ref[...] = strip_ref[pl.ds(half - start, half), :] * (1.0 / total)


def strip_product(total, pos, damping, own_t, early, halves):
    return pl.pallas_call(
        functools.partial(strip_kernel, total),
        out_shape=[jax.ShapeDtypeStruct((SHARE // 2, P_SIZE), F32)] * 2,
        in_specs=[SMEM] + [VMEM] * 7,
        out_specs=[VMEM] * 2,
        scratch_shapes=[pltpu.VMEM(early.shape, F32)],
        compiler_params=params(12),
        cost_estimate=pl.CostEstimate(flops=24 * own_t.size * 256, bytes_accessed=16 * own_t.size, transcendentals=0),
    )(pos, damping[None, :], own_t, early, *halves)


def add_kernel(a_ref, b_ref, sum_ref):
    sum_ref[...] = a_ref[...] + b_ref[...]


def add(a, b):
    return pl.pallas_call(
        add_kernel,
        out_shape=jax.ShapeDtypeStruct(a.shape, F32),
        in_specs=[VMEM] * 2,
        out_specs=VMEM,
        compiler_params=params(4),
        cost_estimate=pl.CostEstimate(flops=a.size, bytes_accessed=12 * a.size, transcendentals=0),
    )(a, b)


def sum_in_order_kernel(pos_ref, *refs):
    parts_ref = refs[5]
    for distance in range(4):
        parts_ref[(pos_ref[3] // 2 + distance) % 4] = refs[distance][...]
    refs[4][...] = (parts_ref[0] + parts_ref[1]) + (parts_ref[2] + parts_ref[3])


def sum_in_order(pos, parts):
    shape = parts[0].shape
    return pl.pallas_call(
        sum_in_order_kernel,
        out_shape=jax.ShapeDtypeStruct(shape, F32),
        in_specs=[SMEM] + [VMEM] * 4,
        out_specs=VMEM,
        scratch_shapes=[pltpu.VMEM((4,) + shape, F32)],
        compiler_params=params(4),
        cost_estimate=pl.CostEstimate(flops=3 * parts[0].size, bytes_accessed=20 * parts[0].size, transcendentals=0),
    )(pos, *parts)


def stack_kernel(*refs):
    for i, ref in enumerate(refs[:-1]):
        refs[-1][i] = ref[...]


def stack(arrays):
    return pl.pallas_call(
        stack_kernel,
        out_shape=jax.ShapeDtypeStruct((len(arrays),) + arrays[0].shape, F32),
        in_specs=[VMEM] * len(arrays),
        out_specs=VMEM,
        compiler_params=params(4),
        cost_estimate=pl.CostEstimate(flops=0, bytes_accessed=32 * arrays[0].size, transcendentals=0),
    )(*arrays)


def late_gram_kernel(total, pos_ref, damping_ref, early_ref, f_ref, *refs):
    halves, (mine_ref, other_ref, sum_ref) = refs[:4], refs[4:]
    wide = 4 * SHARE
    examples = f_ref.shape[0] // 2
    half = mine_ref.shape[0]
    sum_ref[...] = early_ref[...]
    for ring in range(2):
        parts = [part[...].reshape(wide // 2, examples) for part in halves[2 * ring : 2 * ring + 2]]
        features = split(f_ref[examples * ring : examples * (ring + 1), :])
        product = dot3(split(jnp.concatenate(parts, axis=0)), features)
        add_product(ring, (pos_ref[1 - ring] + 2) % 4, product, sum_ref)
    for to_ref, core in ((mine_ref, pos_ref[2]), (other_ref, 1 - pos_ref[2])):
        columns = pl.ds(pl.multiple_of(core * half, half), half)
        for i in range(sum_ref.shape[0] // BLOCK):
            at = slice(BLOCK * i, BLOCK * (i + 1))
            to_ref[:, at] = sum_ref[at, columns].T * (1.0 / total)

    @pl.when(pos_ref[3] == 0)
    def _():
        shape = (SHARE, mine_ref.shape[1])
        row = lax.broadcasted_iota(jnp.int32, shape, 0) + (4 * pos_ref[1] + pos_ref[0]) * SHARE
        column = lax.broadcasted_iota(jnp.int32, shape, 1)
        mine_ref[:SHARE, :] += jnp.where(row == column, damping_ref[...], 0.0)


def late_gram(total, pos, damping, early, features, halves):
    rows, columns = features.shape
    return pl.pallas_call(
        functools.partial(late_gram_kernel, total),
        out_shape=[jax.ShapeDtypeStruct((columns // 2, P_SIZE), F32)] * 2,
        in_specs=[SMEM] + [VMEM] * 7,
        out_specs=[VMEM] * 2,
        scratch_shapes=[pltpu.VMEM(early.shape, F32)],
        compiler_params=params(16),
        cost_estimate=pl.CostEstimate(flops=6 * features.size * 256, bytes_accessed=8 * features.size, transcendentals=0),
    )(pos, damping[None, :], early, features, *halves)


def factor_kernel(damped_ref, last_ref, inverse_ref, factor_ref):
    size = inverse_ref.shape[0]
    wide = 4 * SHARE
    damped = split(damped_ref[...] + last_ref[...])
    for k in range(size // wide):
        at, upto = slice(wide * k, wide * (k + 1)), slice(0, wide * (k + 1))
        factor_ref[:, at] = dot3(tuple(part[:, upto] for part in damped), split(inverse_ref[at, upto]), (1, 1))


def factor_product(damped, last, inverse):
    return pl.pallas_call(
        factor_kernel,
        out_shape=jax.ShapeDtypeStruct(damped.shape, F32),
        in_specs=[VMEM] * 3,
        out_specs=VMEM,
        compiler_params=params(16),
        cost_estimate=pl.CostEstimate(flops=4 * damped.size * P_SIZE, bytes_accessed=12 * damped.size, transcendentals=0),
    )(damped, last, inverse)


def weights_kernel(pos_ref, inverse_ref, *refs):
    tests, (weights_ref, mixed_ref, tests_ref, solved_ref) = refs[:4], refs[4:]
    size = inverse_ref.shape[0]
    wide = 4 * SHARE
    blocks = size // wide
    for distance, block in enumerate(tests):
        first = (pos_ref[3] + 2 * distance) % 8
        columns = block.shape[2]
        for i, place in enumerate((first, first + 1 - 2 * pos_ref[2])):
            tests_ref[:, pl.ds(pl.multiple_of(place * columns, columns), columns)] = block[i]
    for k in range(blocks):
        at, upto = slice(wide * k, wide * (k + 1)), slice(0, wide * (k + 1))
        solved_ref[:, at] = dot3(split(tests_ref[:, upto]), split(inverse_ref[at, upto]), (1, 1))
    for k in range(blocks):
        at, after = slice(wide * k, wide * (k + 1)), slice(wide * k, size)
        weights_ref[:, at] = dot3(split(solved_ref[:, after]), split(inverse_ref[after, at])) * (1.0 / math.sqrt(size))
    weights = weights_ref[...]
    for x in range(4):
        parts = [weights[:, wide * z + SHARE * x : wide * z + SHARE * (x + 1)] for z in range(4)]
        mixed_ref[:, wide * x : wide * (x + 1)] = jnp.concatenate(parts, axis=1)


def weights_product(pos, inverse, tests):
    size = inverse.shape[0]
    count = tests[0].shape[1]
    weights = jax.ShapeDtypeStruct((count, size), F32)
    return pl.pallas_call(
        weights_kernel,
        out_shape=[weights] * 2,
        in_specs=[SMEM] + [VMEM] * 5,
        out_specs=[VMEM] * 2,
        scratch_shapes=[pltpu.VMEM((count, size), F32)] * 2,
        compiler_params=params(16),
        cost_estimate=pl.CostEstimate(flops=6 * size * size * count, bytes_accessed=8 * size * size, transcendentals=0),
    )(pos, inverse, *tests)


def scores_columns(ring, distances, pos_ref, weights_ref, pieces, scores_ref, total_ref, sems):
    wide = 4 * SHARE
    examples = pieces[0].shape[2]
    whole = [piece[...].reshape(wide, examples) for piece in pieces[: len(distances)]]
    whole.append(jnp.concatenate([part[...] for part in pieces[len(distances) :]], axis=0).reshape(wide, examples))
    places = [pl.multiple_of((pos_ref[1 - ring] + distance) % 4 * wide, wide) for distance in distances + (2,)]
    weights = [split(weights_ref[:, pl.ds(place, wide)]) for place in places]
    copies = []
    for k in range(examples // wide):
        at = slice(wide * k, wide * (k + 1))
        total = None
        for weight, piece in zip(weights, whole):
            part = dot3(weight, split(piece[:, at]))
            total = part if total is None else total + part
        total_ref[:, at] = total
        target = scores_ref.at[:, examples * ring + wide * k : examples * ring + wide * (k + 1)]
        copies.append(pltpu.make_async_copy(total_ref.at[:, at], target, sems.at[k]))
        copies[-1].start()
    return copies


def first_scores_kernel(distances, pos_ref, weights_ref, *refs):
    pieces, (scores_ref, total_ref, sems) = refs[: len(distances) + 2], refs[len(distances) + 2 :]
    for copy in scores_columns(0, distances, pos_ref, weights_ref, pieces, scores_ref, total_ref, sems):
        copy.wait()


def second_scores_kernel(distances, pos_ref, weights_ref, mine_ref, other_ref, before_ref, *refs):
    del before_ref
    pieces, refs = refs[: len(distances) + 2], refs[len(distances) + 2 :]
    scores_ref, factor_ref, total_ref, sems, factor_sems = refs
    half = mine_ref.shape[0]
    copies = []
    for i, (source, core) in enumerate(((mine_ref, pos_ref[2]), (other_ref, 1 - pos_ref[2]))):
        target = factor_ref.at[pl.ds(pl.multiple_of(core * half, half), half)]
        copies.append(pltpu.make_async_copy(source, target, factor_sems.at[i]))
        copies[-1].start()
    copies += scores_columns(1, distances, pos_ref, weights_ref, pieces, scores_ref, total_ref, sems)
    for copy in copies:
        copy.wait()


def scores_scratch(weights, pieces):
    examples = pieces[0].shape[2]
    return [pltpu.VMEM((weights.shape[0], examples), F32), pltpu.SemaphoreType.DMA((examples // (4 * SHARE),))]


def first_scores(pos, weights, distances, pieces):
    return pl.pallas_call(
        functools.partial(first_scores_kernel, distances),
        out_shape=jax.ShapeDtypeStruct((weights.shape[0], 2 * pieces[0].shape[2]), F32),
        in_specs=[SMEM] + [VMEM] * (1 + len(pieces)),
        out_specs=ANY,
        scratch_shapes=scores_scratch(weights, pieces),
        compiler_params=params(16),
        cost_estimate=pl.CostEstimate(flops=6 * P_SIZE * P_SIZE * 256, bytes_accessed=4 * P_SIZE * P_SIZE, transcendentals=0),
    )(pos, weights, *pieces)


def second_scores(pos, weights, mine, other, before, distances, pieces):
    return pl.pallas_call(
        functools.partial(second_scores_kernel, distances),
        out_shape=[
            jax.ShapeDtypeStruct(before.shape, F32),
            jax.ShapeDtypeStruct((2 * mine.shape[0], mine.shape[1]), F32),
        ],
        in_specs=[SMEM] + [VMEM] * 3 + [ANY] + [VMEM] * len(pieces),
        out_specs=[ANY] * 2,
        input_output_aliases={4: 0},
        scratch_shapes=scores_scratch(weights, pieces) + [pltpu.SemaphoreType.DMA((2,))],
        compiler_params=params(16),
        cost_estimate=pl.CostEstimate(flops=6 * P_SIZE * P_SIZE * 256, bytes_accessed=4 * P_SIZE * P_SIZE, transcendentals=0),
    )(pos, weights, mine, other, before, *pieces)


def hop(axis, move):
    size = {"test": 16, "train": 8}[axis]
    return lambda value: lax.ppermute(value, axis, [(i, move(i)) for i in range(size)])


TO_X = {d: hop("test", lambda s, d=d: s // 4 * 4 + (s + d) % 4) for d in (1, 2, 3)}
TO_Z = {d: hop("test", lambda s, d=d: (s + 4 * d) % 16) for d in (1, 2, 3)}
TO_Y = {d: hop("train", lambda t, d=d: (t + 2 * d) % 8) for d in (1, 2, 3)}
SWAP_CORE = hop("train", lambda t: t ^ 1)
SWAP_Y1 = hop("train", lambda t: t ^ 2)
SWAP_Y2 = hop("train", lambda t: t ^ 4)


def ring(value, to):
    return [value, to[3](value), to[2](value), to[1](value)]


def relay(ahead, behind, to):
    upper, lower = cut(ahead, behind)
    return to[3](upper), to[1](lower)


def per_device(train_features, test_panel, damping):
    test, train = lax.axis_index("test"), lax.axis_index("train")
    pos = jnp.stack([test % 4, test // 4, train % 2, train]).astype(jnp.int32)
    rows_dev = train_features.shape[0]
    train_total = rows_dev * lax.axis_size("train")

    own_t = train_features[:, :SHARE].T
    first, second = own_t[:, : rows_dev // 2], own_t[:, rows_dev // 2 :]
    pos, first, second = lax.optimization_barrier((pos, first, second))
    own_row = arrange(pos, 0, ring(first, TO_X))
    own_column = arrange(pos, 1, ring(second, TO_Z))
    near_rows, near_columns = [TO_Z[3](own_row), TO_Z[1](own_row)], [TO_X[3](own_column), TO_X[1](own_column)]
    early = early_gram(pos, train_features, (0,), [own_row, own_column])
    early, test_panel = lax.optimization_barrier((early, test_panel))
    tests = ring(stack([test_panel, SWAP_CORE(test_panel)]), TO_Y)
    early, near_columns = lax.optimization_barrier((early, near_columns))
    far_rows, far_columns = relay(*near_rows, TO_Z), relay(*near_columns, TO_X)
    near = [near_rows[0], near_columns[0], near_rows[1], near_columns[1]]
    far = [*far_rows, *far_columns]
    early, strip = early_gram(pos, train_features, (1, 3), near, early)
    strip, tests = lax.optimization_barrier((strip, tests))

    strip, other_strip = strip_product(train_total, pos, damping, own_t, strip, far)
    strip = add(strip, SWAP_CORE(other_strip))
    strips = ring(strip, TO_Y)
    term, other_term = late_gram(train_total, pos, damping, early, train_features, far)
    strips, term, other_term = lax.optimization_barrier((strips, term, other_term))
    strip = sum_in_order(pos, strips)

    damped = add(term, SWAP_CORE(other_term))
    left, rest = order_strips(pos, ring(strip, TO_Z))
    left, damped = lax.optimization_barrier((left, damped))
    damped_y1 = SWAP_Y1(damped)
    mine = stack(ring(left, TO_X))
    mine, rest = lax.optimization_barrier((mine, rest))
    later = ring(rest, TO_X)
    first = first_factor(pos, mine, SWAP_CORE(mine))
    first, later, damped_y1 = lax.optimization_barrier((first, later, damped_y1))
    damped = add(damped, damped_y1)
    later = stack(later)
    later_other = SWAP_CORE(later)
    later, damped = lax.optimization_barrier((later, damped))
    damped_y2 = SWAP_Y2(damped)
    inverse = second_factor(pos, later, later_other, first)
    weights, mixed = weights_product(pos, inverse, tests)
    weights, damped, damped_y2 = lax.optimization_barrier((weights, damped, damped_y2))
    factor = factor_product(damped, damped_y2, inverse)
    other_factor = SWAP_CORE(factor)
    weights, factor = lax.optimization_barrier((weights, factor))
    scores = first_scores(pos, weights, (0, 1, 3), [own_row, *near_rows, *far_rows])
    scores, other_factor = lax.optimization_barrier((scores, other_factor))
    columns = [own_column, *near_columns, *far_columns]
    return tuple(second_scores(pos, mixed, factor, other_factor, scores, (0, 1, 3), columns))


def solution(mesh):
    in_specs = (P("train", "test"), P("test", "train"), P())
    out_specs = (P("test", "train"), P("test", None))
    return jax.shard_map(
        per_device, mesh=mesh, in_specs=in_specs, out_specs=out_specs, check_vma=False
    )
```

```python
import functools
import math

import jax
import jax.numpy as jnp
from jax import lax
from jax.experimental import pallas as pl
from jax.experimental.pallas import tpu as pltpu
from jax.sharding import PartitionSpec as P

P_SIZE = 1024
BLOCK = 128
SHARE = 64
F32 = jnp.float32
BF16 = jnp.bfloat16
VMEM = pl.BlockSpec(memory_space=pltpu.VMEM)
SMEM = pl.BlockSpec(memory_space=pltpu.SMEM)
ANY = pl.BlockSpec(memory_space=pl.ANY)
SPREAD = pltpu.VMEM((2, 64, BLOCK), F32)


def params(mebibytes):
    return pltpu.CompilerParams(vmem_limit_bytes=mebibytes * 1024 * 1024)


def dot(a, b, contract=(1, 0)):
    return lax.dot_general(a, b, ((contract[:1], contract[1:]), ((), ())), preferred_element_type=F32)


def split(value):
    high = value.astype(BF16)
    return high, (value - high.astype(F32)).astype(BF16)


def dot3(a, b, contract=(1, 0)):
    return dot(a[0], b[0], contract) + (dot(a[0], b[1], contract) + dot(a[1], b[0], contract))


def split3(value):
    high, rest = split(value)
    return high, rest, (value - high.astype(F32) - rest.astype(F32)).astype(BF16)


def dot6(a, b, contract=(1, 0)):
    ca, cb = contract
    wide = jnp.concatenate([jnp.concatenate(b[:2], axis=cb), jnp.concatenate(b[1::-1], axis=cb)], axis=1 - cb)
    both = dot(jnp.concatenate(a[:2], axis=ca), wide, contract)
    small = dot(jnp.concatenate(a[::2], axis=ca), jnp.concatenate(b[2::-2], axis=cb), contract)
    half = both.shape[1] // 2
    return both[:, :half] + (both[:, half:] + small)


def factor_block(tiles, work, spread_ref):
    tiles = list(tiles)
    count = len(tiles)
    lane = lax.broadcasted_iota(jnp.int32, (8, BLOCK), 1)
    row = lax.broadcasted_iota(jnp.int32, (8, BLOCK), 0)
    share = -(-len(work) // count)

    def spread(value):
        return jnp.broadcast_to(value, (8, BLOCK))

    for group in range(count):
        first = 8 * group
        own = tiles[group]
        below = range(group + 1, count)
        columns = [spread(own[:, first + j : first + j + 1]) for j in range(8)]
        for j in range(8):
            spread_ref[group % 2, 8 * j : 8 * (j + 1), :] = columns[j]
        pivots = [[spread(spread_ref[group % 2, 8 * j + i : 8 * j + i + 1, :]) for j in range(i + 1)] for i in range(8)]
        inside = (lane >= first) & (lane < first + 8)
        own = jnp.where(inside, (lane - first == row).astype(F32), own)
        lines = [spread(own[i : i + 1, :]) for i in range(8)]
        factors = {m: [spread(tiles[m][:, first + j : first + j + 1]) for j in range(8)] for m in below}
        for m in below:
            tiles[m] = jnp.where(inside, 0.0, tiles[m])
        done = None
        for k in range(8):
            scale = lax.rsqrt(pivots[k][k])
            line = lines[k] * scale
            ratios = {i: pivots[i][k] * scale for i in range(k + 1, 8)}
            for i in range(k + 1, 8):
                for j in range(k + 1, i + 1):
                    pivots[i][j] = pivots[i][j] - ratios[i] * ratios[j]
                lines[i] = lines[i] - ratios[i] * line
            done = line if done is None else jnp.where(row == k, line, done)
            for m in below:
                factor = factors[m][k] * scale
                tiles[m] = tiles[m] - factor * line
                for i in range(k + 1, 8):
                    factors[m][i] = factors[m][i] - factor * ratios[i]
        tiles[group] = done
        for step in work[share * group : share * (group + 1)]:
            step()
    return [jnp.where(lane < 8 * group + 8, tiles[group], 0.0) for group in range(count)]


def blocks_at(i):
    return slice(BLOCK * i, BLOCK * (i + 1))


def factor_in_place(x_ref, spread_ref, extra):
    size = x_ref.shape[0]
    blocks = size // BLOCK
    at = blocks_at

    inverses, panels, rows = {}, {}, {}

    def inverse(k):
        if k not in inverses:
            inverses[k] = split3(x_ref[at(k), at(k)])
        return inverses[k]

    def finish_rows(k):
        left = x_ref[at(k), : BLOCK * k]
        left = dot6(inverse(k), split3(left))
        x_ref[at(k), : BLOCK * k] = left
        rows[k] = tuple(jnp.concatenate(parts, axis=1) for parts in zip(split3(left), inverse(k)))

    def column_panel(i, k):
        panels[i, k] = split3(dot6(split3(x_ref[at(i), at(k)]), inverse(k), (1, 1)))

    def update_right(i, j, k):
        x_ref[at(i), at(j)] -= dot6(panels[i, k], panels[j, k], (1, 1))

    def update_left(i, k):
        change = dot6(panels[i, k], rows[k] if k else inverse(k))
        if k:
            x_ref[at(i), : BLOCK * k] -= change[:, : BLOCK * k]
        x_ref[at(i), at(k)] = -change[:, BLOCK * k :]

    def clear_right(k):
        x_ref[at(k), BLOCK * (k + 1) :] = jnp.zeros((BLOCK, size - BLOCK * (k + 1)), F32)

    def later(k):
        work = [functools.partial(finish_rows, k)] if k else []
        work += [functools.partial(column_panel, i, k) for i in range(k + 2, blocks)]
        work += [functools.partial(update_right, i, j, k) for j in range(k + 1, blocks) for i in range(max(j, k + 2), blocks)]
        work += [functools.partial(update_left, i, k) for i in range(k + 1, blocks)]
        return work + [functools.partial(clear_right, k)]

    for k in range(blocks):
        work = []
        if k:
            column_panel(k, k - 1)
            update_right(k, k, k - 1)
            work = later(k - 1)
        tiles = [x_ref[BLOCK * k + 8 * m : BLOCK * k + 8 * (m + 1), at(k)] for m in range(BLOCK // 8)]
        for m, tile in enumerate(factor_block(tiles, work + extra(k), spread_ref)):
            x_ref[BLOCK * k + 8 * m : BLOCK * k + 8 * (m + 1), at(k)] = tile
    finish_rows(blocks - 1)


def place_strips(pos_ref, mine_ref, other_ref, to_ref):
    for distance in range(mine_ref.shape[0]):
        x = (pos_ref[0] + distance) % 4
        for z in range(mine_ref.shape[1]):
            for source, core in ((mine_ref, pos_ref[2]), (other_ref, 1 - pos_ref[2])):
                start = pl.multiple_of((4 * z + x) * SHARE + core * (SHARE // 2), SHARE // 2)
                to_ref[pl.ds(start, SHARE // 2), :] = source[distance, z]


def first_factor_kernel(pos_ref, mine_ref, other_ref, x_ref, spread_ref):
    place_strips(pos_ref, mine_ref, other_ref, x_ref)
    factor_in_place(x_ref, spread_ref, lambda k: [])


def second_factor_kernel(pos_ref, mine_ref, other_ref, first_ref, out_ref, a_ref, x_ref, spread_ref):
    size = first_ref.shape[0]
    blocks = size // BLOCK
    place_strips(pos_ref, mine_ref, other_ref, a_ref)
    at = blocks_at
    wide = 2 * BLOCK

    chunks = range(size // wide)
    lefts, products, columns, factors = {}, {}, {}, {}

    def left(i):
        parts = []
        for k in chunks:
            upto = slice(0, wide * (k + 1))
            if k not in factors:
                factors[k] = split3(first_ref[wide * k : wide * (k + 1), upto])
            parts.append(dot6(split3(a_ref[at(i), upto]), factors[k], (1, 1)))
        lefts[i] = split3(jnp.concatenate(parts, axis=1))

    def remainder(i, j):
        whole = a_ref[at(i), size + BLOCK * j : size + BLOCK * (j + 1)]
        x_ref[at(i), at(j)] = whole - dot6(lefts[i], lefts[j], (1, 1))

    def product(i):
        parts = []
        for k in chunks:
            after = slice(wide * k, size)
            if k not in columns:
                columns[k] = split(first_ref[after, wide * k : wide * (k + 1)])
            parts.append(dot3(tuple(part[:, after] for part in lefts[i][:2]), columns[k]))
        products[i] = split(jnp.concatenate(parts, axis=1))

    def lower_left(i):
        done = tuple(jnp.concatenate([products[j][part] for j in range(i + 1)], axis=0) for part in range(2))
        lower = dot3(split(x_ref[at(i), : BLOCK * (i + 1)]), done)
        out_ref[size + BLOCK * i : size + BLOCK * (i + 1), :size] = -lower

    def upper(i):
        out_ref[at(i), :size] = first_ref[at(i), :]
        out_ref[at(i), size:] = jnp.zeros((BLOCK, size), F32)

    def extra(k):
        work = []
        if k == 0:
            work += [functools.partial(left, i) for i in range(1, blocks)]
            work += [functools.partial(remainder, i, j) for j in range(blocks) for i in range(max(j, 1), blocks)]
        else:
            work += [functools.partial(lower_left, k - 1)]
        work += [functools.partial(product, k)]
        return work + [functools.partial(upper, k)]

    left(0)
    remainder(0, 0)
    factor_in_place(x_ref, spread_ref, extra)
    lower_left(blocks - 1)
    out_ref[size:, size:] = x_ref[...]


def first_factor(pos, mine, other):
    size = mine.shape[3]
    return pl.pallas_call(
        first_factor_kernel,
        out_shape=jax.ShapeDtypeStruct((size, size), F32),
        in_specs=[SMEM, VMEM, VMEM],
        out_specs=VMEM,
        scratch_shapes=[SPREAD],
        compiler_params=params(16),
        cost_estimate=pl.CostEstimate(flops=size * size, bytes_accessed=8 * size * size, transcendentals=size),
    )(pos, mine, other)


def second_factor(pos, mine, other, first):
    size = first.shape[0]
    return pl.pallas_call(
        second_factor_kernel,
        out_shape=jax.ShapeDtypeStruct((2 * size, 2 * size), F32),
        in_specs=[SMEM, VMEM, VMEM, VMEM],
        out_specs=VMEM,
        scratch_shapes=[pltpu.VMEM((size, 2 * size), F32), pltpu.VMEM((size, size), F32), SPREAD],
        compiler_params=params(24),
        cost_estimate=pl.CostEstimate(flops=size * size, bytes_accessed=8 * size * size, transcendentals=size),
    )(pos, mine, other, first)


def arrange_kernel(axis, pos_ref, *refs):
    for distance in range(4):
        refs[4][(pos_ref[axis] + distance) % 4] = refs[distance][...]


def arrange(pos, axis, blocks):
    block = blocks[0]
    return pl.pallas_call(
        functools.partial(arrange_kernel, axis),
        out_shape=jax.ShapeDtypeStruct((4,) + block.shape, F32),
        in_specs=[SMEM] + [VMEM] * 4,
        out_specs=VMEM,
        compiler_params=params(4),
        cost_estimate=pl.CostEstimate(flops=0, bytes_accessed=32 * block.size, transcendentals=0),
    )(pos, *blocks)


def cut_kernel(first_ref, second_ref, upper_ref, lower_ref):
    half = upper_ref.shape[0]
    upper_ref[...] = first_ref[:half]
    lower_ref[...] = second_ref[half:]


def cut(first, second):
    half = jax.ShapeDtypeStruct((first.shape[0] // 2,) + first.shape[1:], F32)
    return pl.pallas_call(
        cut_kernel,
        out_shape=[half] * 2,
        in_specs=[VMEM] * 2,
        out_specs=[VMEM] * 2,
        compiler_params=params(4),
        cost_estimate=pl.CostEstimate(flops=0, bytes_accessed=8 * first.size, transcendentals=0),
    )(first, second)


def order_strips_kernel(pos_ref, *refs):
    left_ref, rest_ref = refs[4:]
    left = left_ref.shape[2]
    for distance in range(4):
        z = (pos_ref[1] + distance) % 4

        @pl.when(z < 2)
        def _(distance=distance, z=z):
            left_ref[z % 2] = refs[distance][:, :left]

        @pl.when(z >= 2)
        def _(distance=distance, z=z):
            rest_ref[z % 2] = refs[distance][...]


def order_strips(pos, strips):
    rows, columns = strips[0].shape
    return pl.pallas_call(
        order_strips_kernel,
        out_shape=[jax.ShapeDtypeStruct((2, rows, columns // 2), F32), jax.ShapeDtypeStruct((2, rows, columns), F32)],
        in_specs=[SMEM] + [VMEM] * 4,
        out_specs=[VMEM] * 2,
        compiler_params=params(4),
        cost_estimate=pl.CostEstimate(flops=0, bytes_accessed=32 * rows * columns, transcendentals=0),
    )(pos, *strips)


def piece_rows(ring, place, z):
    if ring == 0:
        return pl.ds(pl.multiple_of(place * 4 * SHARE, 4 * SHARE), 4 * SHARE)
    return pl.ds(pl.multiple_of((4 * z + place) * SHARE, SHARE), SHARE)


def add_product(ring, place, product, to_ref):
    if ring == 0:
        to_ref[piece_rows(0, place, 0), :] += product
    else:
        for z in range(4):
            to_ref[piece_rows(1, place, z), :] += product[SHARE * z : SHARE * (z + 1), :]


def early_gram_kernel(distances, first, pos_ref, f_ref, *refs):
    count = 2 * len(distances)
    pieces, refs = refs[:count], refs[count:]
    examples = f_ref.shape[0] // 2
    if first:
        out_ref = refs[0]
        out_ref[...] = jnp.zeros_like(out_ref)
    else:
        before_ref, out_ref, strip_ref = refs
        out_ref[...] = before_ref[...]
    for ring in range(2):
        features = split(f_ref[examples * ring : examples * (ring + 1), :])
        for n, distance in enumerate(distances):
            product = dot3(split(pieces[2 * n + ring][...].reshape(4 * SHARE, examples)), features)
            add_product(ring, (pos_ref[1 - ring] + distance) % 4, product, out_ref)
    if not first:
        for i in range(out_ref.shape[0] // BLOCK):
            at = slice(BLOCK * i, BLOCK * (i + 1))
            strip_ref[:, at] = out_ref[at, :BLOCK].T[:SHARE]


def early_gram(pos, features, distances, pieces, before=None):
    columns = features.shape[1]
    total = jax.ShapeDtypeStruct((P_SIZE, columns), F32)
    strip = jax.ShapeDtypeStruct((SHARE, P_SIZE), F32)
    extra = () if before is None else (before,)
    return pl.pallas_call(
        functools.partial(early_gram_kernel, distances, before is None),
        out_shape=total if before is None else [total, strip],
        in_specs=[SMEM] + [VMEM] * (1 + len(pieces) + len(extra)),
        out_specs=VMEM if before is None else [VMEM, VMEM],
        compiler_params=params(16),
        cost_estimate=pl.CostEstimate(
            flops=6 * features.size * 4 * SHARE * len(distances), bytes_accessed=4 * features.size, transcendentals=0
        ),
    )(pos, features, *pieces, *extra)


def strip_kernel(total, pos_ref, damping_ref, own_ref, early_ref, *refs):
    halves, (mine_ref, other_ref, strip_ref) = refs[:4], refs[4:]
    wide = 4 * SHARE
    examples = own_ref.shape[1] // 2
    strip_ref[...] = early_ref[...]
    for ring in range(2):
        own = split(own_ref[:, examples * ring : examples * (ring + 1)])
        parts = [half[...].reshape(wide // 2, examples) for half in halves[2 * ring : 2 * ring + 2]]
        product = jnp.concatenate([dot3(own, split(part), (1, 1)) for part in parts], axis=1)
        place = (pos_ref[1 - ring] + 2) % 4
        if ring == 0:
            strip_ref[:, piece_rows(0, place, 0)] += product
        else:
            lane = lax.broadcasted_iota(jnp.int32, (SHARE, wide), 1)
            for z in range(4):
                part = jnp.concatenate([product[:, SHARE * z : SHARE * (z + 1)]] * 4, axis=1)
                strip_ref[:, wide * z : wide * (z + 1)] += jnp.where(lane // SHARE == place, part, 0.0)
    half = mine_ref.shape[0]
    start = pl.multiple_of(pos_ref[2] * half, half)
    row = lax.broadcasted_iota(jnp.int32, mine_ref.shape, 0) + (4 * pos_ref[1] + pos_ref[0]) * SHARE + start
    column = lax.broadcasted_iota(jnp.int32, mine_ref.shape, 1)
    damping = jnp.where((row == column) & (pos_ref[3] < 2), damping_ref[...], 0.0)
    mine_ref[...] = strip_ref[pl.ds(start, half), :] * (1.0 / total) + damping
    other_ref[...] = strip_ref[pl.ds(half - start, half), :] * (1.0 / total)


def strip_product(total, pos, damping, own_t, early, halves):
    return pl.pallas_call(
        functools.partial(strip_kernel, total),
        out_shape=[jax.ShapeDtypeStruct((SHARE // 2, P_SIZE), F32)] * 2,
        in_specs=[SMEM] + [VMEM] * 7,
        out_specs=[VMEM] * 2,
        scratch_shapes=[pltpu.VMEM(early.shape, F32)],
        compiler_params=params(12),
        cost_estimate=pl.CostEstimate(flops=24 * own_t.size * 256, bytes_accessed=16 * own_t.size, transcendentals=0),
    )(pos, damping[None, :], own_t, early, *halves)


def add_kernel(a_ref, b_ref, sum_ref):
    sum_ref[...] = a_ref[...] + b_ref[...]


def add(a, b):
    return pl.pallas_call(
        add_kernel,
        out_shape=jax.ShapeDtypeStruct(a.shape, F32),
        in_specs=[VMEM] * 2,
        out_specs=VMEM,
        compiler_params=params(4),
        cost_estimate=pl.CostEstimate(flops=a.size, bytes_accessed=12 * a.size, transcendentals=0),
    )(a, b)


def sum_in_order_kernel(pos_ref, *refs):
    parts_ref = refs[5]
    for distance in range(4):
        parts_ref[(pos_ref[3] // 2 + distance) % 4] = refs[distance][...]
    refs[4][...] = (parts_ref[0] + parts_ref[1]) + (parts_ref[2] + parts_ref[3])


def sum_in_order(pos, parts):
    shape = parts[0].shape
    return pl.pallas_call(
        sum_in_order_kernel,
        out_shape=jax.ShapeDtypeStruct(shape, F32),
        in_specs=[SMEM] + [VMEM] * 4,
        out_specs=VMEM,
        scratch_shapes=[pltpu.VMEM((4,) + shape, F32)],
        compiler_params=params(4),
        cost_estimate=pl.CostEstimate(flops=3 * parts[0].size, bytes_accessed=20 * parts[0].size, transcendentals=0),
    )(pos, *parts)


def stack_kernel(*refs):
    for i, ref in enumerate(refs[:-1]):
        refs[-1][i] = ref[...]


def stack(arrays):
    return pl.pallas_call(
        stack_kernel,
        out_shape=jax.ShapeDtypeStruct((len(arrays),) + arrays[0].shape, F32),
        in_specs=[VMEM] * len(arrays),
        out_specs=VMEM,
        compiler_params=params(4),
        cost_estimate=pl.CostEstimate(flops=0, bytes_accessed=32 * arrays[0].size, transcendentals=0),
    )(*arrays)


def late_gram_kernel(total, pos_ref, damping_ref, early_ref, f_ref, *refs):
    halves, (mine_ref, other_ref, sum_ref) = refs[:4], refs[4:]
    wide = 4 * SHARE
    examples = f_ref.shape[0] // 2
    half = mine_ref.shape[0]
    sum_ref[...] = early_ref[...]
    for ring in range(2):
        parts = [part[...].reshape(wide // 2, examples) for part in halves[2 * ring : 2 * ring + 2]]
        features = split(f_ref[examples * ring : examples * (ring + 1), :])
        product = dot3(split(jnp.concatenate(parts, axis=0)), features)
        add_product(ring, (pos_ref[1 - ring] + 2) % 4, product, sum_ref)
    for to_ref, core in ((mine_ref, pos_ref[2]), (other_ref, 1 - pos_ref[2])):
        columns = pl.ds(pl.multiple_of(core * half, half), half)
        for i in range(sum_ref.shape[0] // BLOCK):
            at = slice(BLOCK * i, BLOCK * (i + 1))
            to_ref[:, at] = sum_ref[at, columns].T * (1.0 / total)

    @pl.when(pos_ref[3] == 0)
    def _():
        shape = (SHARE, mine_ref.shape[1])
        row = lax.broadcasted_iota(jnp.int32, shape, 0) + (4 * pos_ref[1] + pos_ref[0]) * SHARE
        column = lax.broadcasted_iota(jnp.int32, shape, 1)
        mine_ref[:SHARE, :] += jnp.where(row == column, damping_ref[...], 0.0)


def late_gram(total, pos, damping, early, features, halves):
    rows, columns = features.shape
    return pl.pallas_call(
        functools.partial(late_gram_kernel, total),
        out_shape=[jax.ShapeDtypeStruct((columns // 2, P_SIZE), F32)] * 2,
        in_specs=[SMEM] + [VMEM] * 7,
        out_specs=[VMEM] * 2,
        scratch_shapes=[pltpu.VMEM(early.shape, F32)],
        compiler_params=params(16),
        cost_estimate=pl.CostEstimate(flops=6 * features.size * 256, bytes_accessed=8 * features.size, transcendentals=0),
    )(pos, damping[None, :], early, features, *halves)


def factor_kernel(damped_ref, last_ref, inverse_ref, factor_ref):
    size = inverse_ref.shape[0]
    wide = 4 * SHARE
    damped = split(damped_ref[...] + last_ref[...])
    for k in range(size // wide):
        at, upto = slice(wide * k, wide * (k + 1)), slice(0, wide * (k + 1))
        factor_ref[:, at] = dot3(tuple(part[:, upto] for part in damped), split(inverse_ref[at, upto]), (1, 1))


def factor_product(damped, last, inverse):
    return pl.pallas_call(
        factor_kernel,
        out_shape=jax.ShapeDtypeStruct(damped.shape, F32),
        in_specs=[VMEM] * 3,
        out_specs=VMEM,
        compiler_params=params(16),
        cost_estimate=pl.CostEstimate(flops=4 * damped.size * P_SIZE, bytes_accessed=12 * damped.size, transcendentals=0),
    )(damped, last, inverse)


def weights_kernel(pos_ref, inverse_ref, *refs):
    tests, (weights_ref, mixed_ref, tests_ref, solved_ref) = refs[:4], refs[4:]
    size = inverse_ref.shape[0]
    wide = 4 * SHARE
    blocks = size // wide
    for distance, block in enumerate(tests):
        first = (pos_ref[3] + 2 * distance) % 8
        columns = block.shape[2]
        for i, place in enumerate((first, first + 1 - 2 * pos_ref[2])):
            tests_ref[:, pl.ds(pl.multiple_of(place * columns, columns), columns)] = block[i]
    for k in range(blocks):
        at, upto = slice(wide * k, wide * (k + 1)), slice(0, wide * (k + 1))
        solved_ref[:, at] = dot3(split(tests_ref[:, upto]), split(inverse_ref[at, upto]), (1, 1))
    for k in range(blocks):
        at, after = slice(wide * k, wide * (k + 1)), slice(wide * k, size)
        weights_ref[:, at] = dot3(split(solved_ref[:, after]), split(inverse_ref[after, at])) * (1.0 / math.sqrt(size))
    weights = weights_ref[...]
    for x in range(4):
        parts = [weights[:, wide * z + SHARE * x : wide * z + SHARE * (x + 1)] for z in range(4)]
        mixed_ref[:, wide * x : wide * (x + 1)] = jnp.concatenate(parts, axis=1)


def weights_product(pos, inverse, tests):
    size = inverse.shape[0]
    count = tests[0].shape[1]
    weights = jax.ShapeDtypeStruct((count, size), F32)
    return pl.pallas_call(
        weights_kernel,
        out_shape=[weights] * 2,
        in_specs=[SMEM] + [VMEM] * 5,
        out_specs=[VMEM] * 2,
        scratch_shapes=[pltpu.VMEM((count, size), F32)] * 2,
        compiler_params=params(16),
        cost_estimate=pl.CostEstimate(flops=6 * size * size * count, bytes_accessed=8 * size * size, transcendentals=0),
    )(pos, inverse, *tests)


def scores_columns(ring, distances, pos_ref, weights_ref, pieces, scores_ref, total_ref, sems):
    wide = 4 * SHARE
    examples = pieces[0].shape[2]
    whole = [piece[...].reshape(wide, examples) for piece in pieces[: len(distances)]]
    whole.append(jnp.concatenate([part[...] for part in pieces[len(distances) :]], axis=0).reshape(wide, examples))
    places = [pl.multiple_of((pos_ref[1 - ring] + distance) % 4 * wide, wide) for distance in distances + (2,)]
    weights = [split(weights_ref[:, pl.ds(place, wide)]) for place in places]
    copies = []
    for k in range(examples // wide):
        at = slice(wide * k, wide * (k + 1))
        total = None
        for weight, piece in zip(weights, whole):
            part = dot3(weight, split(piece[:, at]))
            total = part if total is None else total + part
        total_ref[:, at] = total
        target = scores_ref.at[:, examples * ring + wide * k : examples * ring + wide * (k + 1)]
        copies.append(pltpu.make_async_copy(total_ref.at[:, at], target, sems.at[k]))
        copies[-1].start()
    return copies


def first_scores_kernel(distances, pos_ref, weights_ref, *refs):
    pieces, (scores_ref, total_ref, sems) = refs[: len(distances) + 2], refs[len(distances) + 2 :]
    for copy in scores_columns(0, distances, pos_ref, weights_ref, pieces, scores_ref, total_ref, sems):
        copy.wait()


def copy_rows(pos_ref, source_ref, core, to_ref, sems):
    half, parts = source_ref.shape[0], sems.shape[0]
    size = half // parts
    copies = []
    for i in range(parts):
        target = to_ref.at[pl.ds(pl.multiple_of(core * half + size * i, size), size)]
        copies.append(pltpu.make_async_copy(source_ref.at[size * i : size * (i + 1)], target, sems.at[i]))
        copies[-1].start()
    return copies


def second_scores_kernel(distances, pos_ref, weights_ref, mine_ref, before_ref, *refs):
    del before_ref
    pieces, refs = refs[: len(distances) + 2], refs[len(distances) + 2 :]
    scores_ref, factor_ref, total_ref, sems, factor_sems = refs
    copies = copy_rows(pos_ref, mine_ref, pos_ref[2], factor_ref, factor_sems)
    copies += scores_columns(1, distances, pos_ref, weights_ref, pieces, scores_ref, total_ref, sems)
    for copy in copies:
        copy.wait()


def complete_kernel(pos_ref, other_ref, before_ref, factor_ref, sems):
    del before_ref
    for copy in copy_rows(pos_ref, other_ref, 1 - pos_ref[2], factor_ref, sems):
        copy.wait()


def complete(pos, other, before):
    return pl.pallas_call(
        complete_kernel,
        out_shape=jax.ShapeDtypeStruct(before.shape, F32),
        in_specs=[SMEM, VMEM, ANY],
        out_specs=ANY,
        input_output_aliases={2: 0},
        scratch_shapes=[pltpu.SemaphoreType.DMA((8,))],
        compiler_params=params(4),
        cost_estimate=pl.CostEstimate(flops=0, bytes_accessed=8 * other.size, transcendentals=0),
    )(pos, other, before)


def scores_scratch(weights, pieces):
    examples = pieces[0].shape[2]
    return [pltpu.VMEM((weights.shape[0], examples), F32), pltpu.SemaphoreType.DMA((examples // (4 * SHARE),))]


def first_scores(pos, weights, distances, pieces):
    return pl.pallas_call(
        functools.partial(first_scores_kernel, distances),
        out_shape=jax.ShapeDtypeStruct((weights.shape[0], 2 * pieces[0].shape[2]), F32),
        in_specs=[SMEM] + [VMEM] * (1 + len(pieces)),
        out_specs=ANY,
        scratch_shapes=scores_scratch(weights, pieces),
        compiler_params=params(16),
        cost_estimate=pl.CostEstimate(flops=6 * P_SIZE * P_SIZE * 256, bytes_accessed=4 * P_SIZE * P_SIZE, transcendentals=0),
    )(pos, weights, *pieces)


def second_scores(pos, weights, mine, before, distances, pieces):
    return pl.pallas_call(
        functools.partial(second_scores_kernel, distances),
        out_shape=[
            jax.ShapeDtypeStruct(before.shape, F32),
            jax.ShapeDtypeStruct((2 * mine.shape[0], mine.shape[1]), F32),
        ],
        in_specs=[SMEM] + [VMEM] * 2 + [ANY] + [VMEM] * len(pieces),
        out_specs=[ANY] * 2,
        input_output_aliases={3: 0},
        scratch_shapes=scores_scratch(weights, pieces) + [pltpu.SemaphoreType.DMA((2,))],
        compiler_params=params(16),
        cost_estimate=pl.CostEstimate(flops=6 * P_SIZE * P_SIZE * 256, bytes_accessed=4 * P_SIZE * P_SIZE, transcendentals=0),
    )(pos, weights, mine, before, *pieces)


def hop(axis, move):
    size = {"test": 16, "train": 8}[axis]
    return lambda value: lax.ppermute(value, axis, [(i, move(i)) for i in range(size)])


TO_X = {d: hop("test", lambda s, d=d: s // 4 * 4 + (s + d) % 4) for d in (1, 2, 3)}
TO_Z = {d: hop("test", lambda s, d=d: (s + 4 * d) % 16) for d in (1, 2, 3)}
TO_Y = {d: hop("train", lambda t, d=d: (t + 2 * d) % 8) for d in (1, 2, 3)}
SWAP_CORE = hop("train", lambda t: t ^ 1)
SWAP_Y1 = hop("train", lambda t: t ^ 2)
SWAP_Y2 = hop("train", lambda t: t ^ 4)


def ring(value, to):
    return [value, to[3](value), to[2](value), to[1](value)]


def relay(ahead, behind, to):
    upper, lower = cut(ahead, behind)
    return to[3](upper), to[1](lower)


def per_device(train_features, test_panel, damping):
    test, train = lax.axis_index("test"), lax.axis_index("train")
    pos = jnp.stack([test % 4, test // 4, train % 2, train]).astype(jnp.int32)
    rows_dev = train_features.shape[0]
    train_total = rows_dev * lax.axis_size("train")

    own_t = train_features[:, :SHARE].T
    first, second = own_t[:, : rows_dev // 2], own_t[:, rows_dev // 2 :]
    pos, first, second = lax.optimization_barrier((pos, first, second))
    own_row = arrange(pos, 0, ring(first, TO_X))
    own_column = arrange(pos, 1, ring(second, TO_Z))
    near_rows, near_columns = [TO_Z[3](own_row), TO_Z[1](own_row)], [TO_X[3](own_column), TO_X[1](own_column)]
    early = early_gram(pos, train_features, (0,), [own_row, own_column])
    early, test_panel = lax.optimization_barrier((early, test_panel))
    tests = ring(stack([test_panel, SWAP_CORE(test_panel)]), TO_Y)
    early, near_columns = lax.optimization_barrier((early, near_columns))
    far_rows, far_columns = relay(*near_rows, TO_Z), relay(*near_columns, TO_X)
    near = [near_rows[0], near_columns[0], near_rows[1], near_columns[1]]
    far = [*far_rows, *far_columns]
    early, strip = early_gram(pos, train_features, (1, 3), near, early)
    strip, tests = lax.optimization_barrier((strip, tests))

    strip, other_strip = strip_product(train_total, pos, damping, own_t, strip, far)
    strip = add(strip, SWAP_CORE(other_strip))
    strips = ring(strip, TO_Y)
    term, other_term = late_gram(train_total, pos, damping, early, train_features, far)
    strips, term, other_term = lax.optimization_barrier((strips, term, other_term))
    strip = sum_in_order(pos, strips)

    damped = add(term, SWAP_CORE(other_term))
    left, rest = order_strips(pos, ring(strip, TO_Z))
    left, damped = lax.optimization_barrier((left, damped))
    damped_y1 = SWAP_Y1(damped)
    mine = stack(ring(left, TO_X))
    mine, rest = lax.optimization_barrier((mine, rest))
    later = ring(rest, TO_X)
    first = first_factor(pos, mine, SWAP_CORE(mine))
    first, later, damped_y1 = lax.optimization_barrier((first, later, damped_y1))
    damped = add(damped, damped_y1)
    later = stack(later)
    later_other = SWAP_CORE(later)
    later, damped = lax.optimization_barrier((later, damped))
    damped_y2 = SWAP_Y2(damped)
    inverse = second_factor(pos, later, later_other, first)
    weights, mixed = weights_product(pos, inverse, tests)
    scores = first_scores(pos, weights, (0, 1, 3), [own_row, *near_rows, *far_rows])
    scores, damped, damped_y2 = lax.optimization_barrier((scores, damped, damped_y2))
    factor = factor_product(damped, damped_y2, inverse)
    other_factor = SWAP_CORE(factor)
    columns = [own_column, *near_columns, *far_columns]
    scores, rows = second_scores(pos, mixed, factor, scores, (0, 1, 3), columns)
    rows, other_factor = lax.optimization_barrier((rows, other_factor))
    return scores, complete(pos, other_factor, rows)


def solution(mesh):
    in_specs = (P("train", "test"), P("test", "train"), P())
    out_specs = (P("test", "train"), P("test", None))
    return jax.shard_map(
        per_device, mesh=mesh, in_specs=in_specs, out_specs=out_specs, check_vma=False
    )
```

```python
import functools
import math

import jax
import jax.numpy as jnp
from jax import lax
from jax.experimental import pallas as pl
from jax.experimental.pallas import tpu as pltpu
from jax.sharding import PartitionSpec as P

P_SIZE = 1024
BLOCK = 128
SHARE = 64
F32 = jnp.float32
BF16 = jnp.bfloat16
VMEM = pl.BlockSpec(memory_space=pltpu.VMEM)
SMEM = pl.BlockSpec(memory_space=pltpu.SMEM)
ANY = pl.BlockSpec(memory_space=pl.ANY)
SPREAD = pltpu.VMEM((2, 64, BLOCK), F32)


def params(mebibytes):
    return pltpu.CompilerParams(vmem_limit_bytes=mebibytes * 1024 * 1024)


def dot(a, b, contract=(1, 0)):
    return lax.dot_general(a, b, ((contract[:1], contract[1:]), ((), ())), preferred_element_type=F32)


def split(value):
    high = value.astype(BF16)
    return high, (value - high.astype(F32)).astype(BF16)


def dot3(a, b, contract=(1, 0)):
    return dot(a[0], b[0], contract) + (dot(a[0], b[1], contract) + dot(a[1], b[0], contract))


def split3(value):
    high, rest = split(value)
    return high, rest, (value - high.astype(F32) - rest.astype(F32)).astype(BF16)


def dot6(a, b, contract=(1, 0)):
    ca, cb = contract
    wide = jnp.concatenate([jnp.concatenate(b[:2], axis=cb), jnp.concatenate(b[1::-1], axis=cb)], axis=1 - cb)
    both = dot(jnp.concatenate(a[:2], axis=ca), wide, contract)
    small = dot(jnp.concatenate(a[::2], axis=ca), jnp.concatenate(b[2::-2], axis=cb), contract)
    half = both.shape[1] // 2
    return both[:, :half] + (both[:, half:] + small)


def factor_block(tiles, work, spread_ref):
    tiles = list(tiles)
    count = len(tiles)
    lane = lax.broadcasted_iota(jnp.int32, (8, BLOCK), 1)
    row = lax.broadcasted_iota(jnp.int32, (8, BLOCK), 0)
    share = -(-len(work) // count)

    def spread(value):
        return jnp.broadcast_to(value, (8, BLOCK))

    for group in range(count):
        first = 8 * group
        own = tiles[group]
        below = range(group + 1, count)
        columns = [spread(own[:, first + j : first + j + 1]) for j in range(8)]
        for j in range(8):
            spread_ref[group % 2, 8 * j : 8 * (j + 1), :] = columns[j]
        pivots = [[spread(spread_ref[group % 2, 8 * j + i : 8 * j + i + 1, :]) for j in range(i + 1)] for i in range(8)]
        inside = (lane >= first) & (lane < first + 8)
        own = jnp.where(inside, (lane - first == row).astype(F32), own)
        lines = [spread(own[i : i + 1, :]) for i in range(8)]
        factors = {m: [spread(tiles[m][:, first + j : first + j + 1]) for j in range(8)] for m in below}
        for m in below:
            tiles[m] = jnp.where(inside, 0.0, tiles[m])
        done = None
        for k in range(8):
            scale = lax.rsqrt(pivots[k][k])
            line = lines[k] * scale
            ratios = {i: pivots[i][k] * scale for i in range(k + 1, 8)}
            for i in range(k + 1, 8):
                for j in range(k + 1, i + 1):
                    pivots[i][j] = pivots[i][j] - ratios[i] * ratios[j]
                lines[i] = lines[i] - ratios[i] * line
            done = line if done is None else jnp.where(row == k, line, done)
            for m in below:
                factor = factors[m][k] * scale
                tiles[m] = tiles[m] - factor * line
                for i in range(k + 1, 8):
                    factors[m][i] = factors[m][i] - factor * ratios[i]
        tiles[group] = done
        for step in work[share * group : share * (group + 1)]:
            step()
    return [jnp.where(lane < 8 * group + 8, tiles[group], 0.0) for group in range(count)]


def blocks_at(i):
    return slice(BLOCK * i, BLOCK * (i + 1))


def factor_in_place(x_ref, spread_ref, extra):
    size = x_ref.shape[0]
    blocks = size // BLOCK
    at = blocks_at

    inverses, panels, rows = {}, {}, {}

    def inverse(k):
        if k not in inverses:
            inverses[k] = split3(x_ref[at(k), at(k)])
        return inverses[k]

    def finish_rows(k):
        left = x_ref[at(k), : BLOCK * k]
        left = dot6(inverse(k), split3(left))
        x_ref[at(k), : BLOCK * k] = left
        rows[k] = tuple(jnp.concatenate(parts, axis=1) for parts in zip(split3(left), inverse(k)))

    def column_panel(i, k):
        panels[i, k] = split3(dot6(split3(x_ref[at(i), at(k)]), inverse(k), (1, 1)))

    def update_right(i, j, k):
        x_ref[at(i), at(j)] -= dot6(panels[i, k], panels[j, k], (1, 1))

    def update_left(i, k):
        change = dot6(panels[i, k], rows[k] if k else inverse(k))
        if k:
            x_ref[at(i), : BLOCK * k] -= change[:, : BLOCK * k]
        x_ref[at(i), at(k)] = -change[:, BLOCK * k :]

    def clear_right(k):
        x_ref[at(k), BLOCK * (k + 1) :] = jnp.zeros((BLOCK, size - BLOCK * (k + 1)), F32)

    def later(k):
        work = [functools.partial(finish_rows, k)] if k else []
        work += [functools.partial(column_panel, i, k) for i in range(k + 2, blocks)]
        work += [functools.partial(update_right, i, j, k) for j in range(k + 1, blocks) for i in range(max(j, k + 2), blocks)]
        work += [functools.partial(update_left, i, k) for i in range(k + 1, blocks)]
        return work + [functools.partial(clear_right, k)]

    for k in range(blocks):
        work = []
        if k:
            column_panel(k, k - 1)
            update_right(k, k, k - 1)
            work = later(k - 1)
        tiles = [x_ref[BLOCK * k + 8 * m : BLOCK * k + 8 * (m + 1), at(k)] for m in range(BLOCK // 8)]
        for m, tile in enumerate(factor_block(tiles, work + extra(k), spread_ref)):
            x_ref[BLOCK * k + 8 * m : BLOCK * k + 8 * (m + 1), at(k)] = tile
    finish_rows(blocks - 1)


def place_strips(pos_ref, mine_ref, other_ref, to_ref):
    for distance in range(mine_ref.shape[0]):
        x = (pos_ref[0] + distance) % 4
        for z in range(mine_ref.shape[1]):
            for source, core in ((mine_ref, pos_ref[2]), (other_ref, 1 - pos_ref[2])):
                start = pl.multiple_of((4 * z + x) * SHARE + core * (SHARE // 2), SHARE // 2)
                to_ref[pl.ds(start, SHARE // 2), :] = source[distance, z]


def first_factor_kernel(pos_ref, mine_ref, other_ref, x_ref, spread_ref):
    half, quarter = mine_ref.shape[1], mine_ref.shape[2] // 3
    for distance in range(4):
        x = (pos_ref[0] + distance) % 4
        for source, core in ((mine_ref, pos_ref[2]), (other_ref, 1 - pos_ref[2])):
            start = pl.multiple_of(x * SHARE + core * half, half)
            x_ref[pl.ds(start, half), :quarter] = source[distance, :, :quarter]
            x_ref[pl.ds(start + 4 * SHARE, half), :] = source[distance, :, quarter:]
    factor_in_place(x_ref, spread_ref, lambda k: [])


def second_factor_kernel(pos_ref, mine_ref, other_ref, first_ref, out_ref, a_ref, x_ref, spread_ref):
    size = first_ref.shape[0]
    blocks = size // BLOCK
    place_strips(pos_ref, mine_ref, other_ref, a_ref)
    at = blocks_at
    wide = 2 * BLOCK

    chunks = range(size // wide)
    lefts, products, columns, factors = {}, {}, {}, {}

    def left(i):
        parts = []
        for k in chunks:
            upto = slice(0, wide * (k + 1))
            if k not in factors:
                factors[k] = split3(first_ref[wide * k : wide * (k + 1), upto])
            parts.append(dot6(split3(a_ref[at(i), upto]), factors[k], (1, 1)))
        lefts[i] = split3(jnp.concatenate(parts, axis=1))

    def remainder(i, j):
        whole = a_ref[at(i), size + BLOCK * j : size + BLOCK * (j + 1)]
        x_ref[at(i), at(j)] = whole - dot6(lefts[i], lefts[j], (1, 1))

    def product(i):
        parts = []
        for k in chunks:
            after = slice(wide * k, size)
            if k not in columns:
                columns[k] = split(first_ref[after, wide * k : wide * (k + 1)])
            parts.append(dot3(tuple(part[:, after] for part in lefts[i][:2]), columns[k]))
        products[i] = split(jnp.concatenate(parts, axis=1))

    def lower_left(i):
        done = tuple(jnp.concatenate([products[j][part] for j in range(i + 1)], axis=0) for part in range(2))
        lower = dot3(split(x_ref[at(i), : BLOCK * (i + 1)]), done)
        out_ref[size + BLOCK * i : size + BLOCK * (i + 1), :size] = -lower

    def upper(i):
        out_ref[at(i), :size] = first_ref[at(i), :]
        out_ref[at(i), size:] = jnp.zeros((BLOCK, size), F32)

    def extra(k):
        work = []
        if k == 0:
            work += [functools.partial(left, i) for i in range(1, blocks)]
            work += [functools.partial(remainder, i, j) for j in range(blocks) for i in range(max(j, 1), blocks)]
        else:
            work += [functools.partial(lower_left, k - 1)]
        work += [functools.partial(product, k)]
        return work + [functools.partial(upper, k)]

    left(0)
    remainder(0, 0)
    factor_in_place(x_ref, spread_ref, extra)
    lower_left(blocks - 1)
    out_ref[size:, size:] = x_ref[...]


def first_factor(pos, mine, other):
    size = mine.shape[2] // 3 * 2
    return pl.pallas_call(
        first_factor_kernel,
        out_shape=jax.ShapeDtypeStruct((size, size), F32),
        in_specs=[SMEM, VMEM, VMEM],
        out_specs=VMEM,
        scratch_shapes=[SPREAD],
        compiler_params=params(16),
        cost_estimate=pl.CostEstimate(flops=size * size, bytes_accessed=8 * size * size, transcendentals=size),
    )(pos, mine, other)


def second_factor(pos, mine, other, first):
    size = first.shape[0]
    return pl.pallas_call(
        second_factor_kernel,
        out_shape=jax.ShapeDtypeStruct((2 * size, 2 * size), F32),
        in_specs=[SMEM, VMEM, VMEM, VMEM],
        out_specs=VMEM,
        scratch_shapes=[pltpu.VMEM((size, 2 * size), F32), pltpu.VMEM((size, size), F32), SPREAD],
        compiler_params=params(24),
        cost_estimate=pl.CostEstimate(flops=size * size, bytes_accessed=8 * size * size, transcendentals=size),
    )(pos, mine, other, first)


def arrange_kernel(axis, pos_ref, *refs):
    for distance in range(4):
        refs[4][(pos_ref[axis] + distance) % 4] = refs[distance][...]


def arrange(pos, axis, blocks):
    block = blocks[0]
    return pl.pallas_call(
        functools.partial(arrange_kernel, axis),
        out_shape=jax.ShapeDtypeStruct((4,) + block.shape, F32),
        in_specs=[SMEM] + [VMEM] * 4,
        out_specs=VMEM,
        compiler_params=params(4),
        cost_estimate=pl.CostEstimate(flops=0, bytes_accessed=32 * block.size, transcendentals=0),
    )(pos, *blocks)


def cut_kernel(first_ref, second_ref, upper_ref, lower_ref):
    half = upper_ref.shape[0]
    upper_ref[...] = first_ref[:half]
    lower_ref[...] = second_ref[half:]


def cut(first, second):
    half = jax.ShapeDtypeStruct((first.shape[0] // 2,) + first.shape[1:], F32)
    return pl.pallas_call(
        cut_kernel,
        out_shape=[half] * 2,
        in_specs=[VMEM] * 2,
        out_specs=[VMEM] * 2,
        compiler_params=params(4),
        cost_estimate=pl.CostEstimate(flops=0, bytes_accessed=8 * first.size, transcendentals=0),
    )(first, second)


def order_strips_kernel(pos_ref, *refs):
    left_ref, rest_ref = refs[4:]
    quarter = left_ref.shape[1] // 3
    for distance in range(4):
        z = (pos_ref[1] + distance) % 4

        @pl.when(z == 0)
        def _(distance=distance):
            left_ref[:, :quarter] = refs[distance][:, :quarter]

        @pl.when(z == 1)
        def _(distance=distance):
            left_ref[:, quarter:] = refs[distance][:, : 2 * quarter]

        @pl.when(z >= 2)
        def _(distance=distance, z=z):
            rest_ref[z % 2] = refs[distance][...]


def order_strips(pos, strips):
    rows, columns = strips[0].shape
    return pl.pallas_call(
        order_strips_kernel,
        out_shape=[
            jax.ShapeDtypeStruct((rows, columns // 4 * 3), F32),
            jax.ShapeDtypeStruct((2, rows, columns), F32),
        ],
        in_specs=[SMEM] + [VMEM] * 4,
        out_specs=[VMEM] * 2,
        compiler_params=params(4),
        cost_estimate=pl.CostEstimate(flops=0, bytes_accessed=32 * rows * columns, transcendentals=0),
    )(pos, *strips)


def piece_rows(ring, place, z):
    if ring == 0:
        return pl.ds(pl.multiple_of(place * 4 * SHARE, 4 * SHARE), 4 * SHARE)
    return pl.ds(pl.multiple_of((4 * z + place) * SHARE, SHARE), SHARE)


def add_product(ring, place, product, to_ref):
    if ring == 0:
        to_ref[piece_rows(0, place, 0), :] += product
    else:
        for z in range(4):
            to_ref[piece_rows(1, place, z), :] += product[SHARE * z : SHARE * (z + 1), :]


def early_gram_kernel(distances, first, pos_ref, f_ref, *refs):
    count = 2 * len(distances)
    pieces, refs = refs[:count], refs[count:]
    examples = f_ref.shape[0] // 2
    if first:
        out_ref = refs[0]
        out_ref[...] = jnp.zeros_like(out_ref)
    else:
        before_ref, out_ref, strip_ref = refs
        out_ref[...] = before_ref[...]
    for ring in range(2):
        features = split(f_ref[examples * ring : examples * (ring + 1), :])
        for n, distance in enumerate(distances):
            product = dot3(split(pieces[2 * n + ring][...].reshape(4 * SHARE, examples)), features)
            add_product(ring, (pos_ref[1 - ring] + distance) % 4, product, out_ref)
    if not first:
        for i in range(out_ref.shape[0] // BLOCK):
            at = slice(BLOCK * i, BLOCK * (i + 1))
            strip_ref[:, at] = out_ref[at, :BLOCK].T[:SHARE]


def early_gram(pos, features, distances, pieces, before=None):
    columns = features.shape[1]
    total = jax.ShapeDtypeStruct((P_SIZE, columns), F32)
    strip = jax.ShapeDtypeStruct((SHARE, P_SIZE), F32)
    extra = () if before is None else (before,)
    return pl.pallas_call(
        functools.partial(early_gram_kernel, distances, before is None),
        out_shape=total if before is None else [total, strip],
        in_specs=[SMEM] + [VMEM] * (1 + len(pieces) + len(extra)),
        out_specs=VMEM if before is None else [VMEM, VMEM],
        compiler_params=params(16),
        cost_estimate=pl.CostEstimate(
            flops=6 * features.size * 4 * SHARE * len(distances), bytes_accessed=4 * features.size, transcendentals=0
        ),
    )(pos, features, *pieces, *extra)


def strip_kernel(total, pos_ref, damping_ref, own_ref, early_ref, *refs):
    halves, (mine_ref, other_ref, strip_ref) = refs[:4], refs[4:]
    wide = 4 * SHARE
    examples = own_ref.shape[1] // 2
    strip_ref[...] = early_ref[...]
    for ring in range(2):
        own = split(own_ref[:, examples * ring : examples * (ring + 1)])
        parts = [half[...].reshape(wide // 2, examples) for half in halves[2 * ring : 2 * ring + 2]]
        product = jnp.concatenate([dot3(own, split(part), (1, 1)) for part in parts], axis=1)
        place = (pos_ref[1 - ring] + 2) % 4
        if ring == 0:
            strip_ref[:, piece_rows(0, place, 0)] += product
        else:
            lane = lax.broadcasted_iota(jnp.int32, (SHARE, wide), 1)
            for z in range(4):
                part = jnp.concatenate([product[:, SHARE * z : SHARE * (z + 1)]] * 4, axis=1)
                strip_ref[:, wide * z : wide * (z + 1)] += jnp.where(lane // SHARE == place, part, 0.0)
    half = mine_ref.shape[0]
    start = pl.multiple_of(pos_ref[2] * half, half)
    row = lax.broadcasted_iota(jnp.int32, mine_ref.shape, 0) + (4 * pos_ref[1] + pos_ref[0]) * SHARE + start
    column = lax.broadcasted_iota(jnp.int32, mine_ref.shape, 1)
    damping = jnp.where((row == column) & (pos_ref[3] < 2), damping_ref[...], 0.0)
    mine_ref[...] = strip_ref[pl.ds(start, half), :] * (1.0 / total) + damping
    other_ref[...] = strip_ref[pl.ds(half - start, half), :] * (1.0 / total)


def strip_product(total, pos, damping, own_t, early, halves):
    return pl.pallas_call(
        functools.partial(strip_kernel, total),
        out_shape=[jax.ShapeDtypeStruct((SHARE // 2, P_SIZE), F32)] * 2,
        in_specs=[SMEM] + [VMEM] * 7,
        out_specs=[VMEM] * 2,
        scratch_shapes=[pltpu.VMEM(early.shape, F32)],
        compiler_params=params(12),
        cost_estimate=pl.CostEstimate(flops=24 * own_t.size * 256, bytes_accessed=16 * own_t.size, transcendentals=0),
    )(pos, damping[None, :], own_t, early, *halves)


def add_kernel(a_ref, b_ref, sum_ref):
    sum_ref[...] = a_ref[...] + b_ref[...]


def add(a, b):
    return pl.pallas_call(
        add_kernel,
        out_shape=jax.ShapeDtypeStruct(a.shape, F32),
        in_specs=[VMEM] * 2,
        out_specs=VMEM,
        compiler_params=params(4),
        cost_estimate=pl.CostEstimate(flops=a.size, bytes_accessed=12 * a.size, transcendentals=0),
    )(a, b)


def sum_in_order_kernel(pos_ref, *refs):
    parts_ref = refs[5]
    for distance in range(4):
        parts_ref[(pos_ref[3] // 2 + distance) % 4] = refs[distance][...]
    refs[4][...] = (parts_ref[0] + parts_ref[1]) + (parts_ref[2] + parts_ref[3])


def sum_in_order(pos, parts):
    shape = parts[0].shape
    return pl.pallas_call(
        sum_in_order_kernel,
        out_shape=jax.ShapeDtypeStruct(shape, F32),
        in_specs=[SMEM] + [VMEM] * 4,
        out_specs=VMEM,
        scratch_shapes=[pltpu.VMEM((4,) + shape, F32)],
        compiler_params=params(4),
        cost_estimate=pl.CostEstimate(flops=3 * parts[0].size, bytes_accessed=20 * parts[0].size, transcendentals=0),
    )(pos, *parts)


def stack_kernel(*refs):
    for i, ref in enumerate(refs[:-1]):
        refs[-1][i] = ref[...]


def stack(arrays):
    return pl.pallas_call(
        stack_kernel,
        out_shape=jax.ShapeDtypeStruct((len(arrays),) + arrays[0].shape, F32),
        in_specs=[VMEM] * len(arrays),
        out_specs=VMEM,
        compiler_params=params(4),
        cost_estimate=pl.CostEstimate(flops=0, bytes_accessed=32 * arrays[0].size, transcendentals=0),
    )(*arrays)


def late_gram_kernel(total, pos_ref, damping_ref, early_ref, f_ref, *refs):
    halves, (mine_ref, other_ref, sum_ref) = refs[:4], refs[4:]
    wide = 4 * SHARE
    examples = f_ref.shape[0] // 2
    half = mine_ref.shape[0]
    sum_ref[...] = early_ref[...]
    for ring in range(2):
        parts = [part[...].reshape(wide // 2, examples) for part in halves[2 * ring : 2 * ring + 2]]
        features = split(f_ref[examples * ring : examples * (ring + 1), :])
        product = dot3(split(jnp.concatenate(parts, axis=0)), features)
        add_product(ring, (pos_ref[1 - ring] + 2) % 4, product, sum_ref)
    for to_ref, core in ((mine_ref, pos_ref[2]), (other_ref, 1 - pos_ref[2])):
        columns = pl.ds(pl.multiple_of(core * half, half), half)
        for i in range(sum_ref.shape[0] // BLOCK):
            at = slice(BLOCK * i, BLOCK * (i + 1))
            to_ref[:, at] = sum_ref[at, columns].T * (1.0 / total)

    @pl.when(pos_ref[3] == 0)
    def _():
        shape = (SHARE, mine_ref.shape[1])
        row = lax.broadcasted_iota(jnp.int32, shape, 0) + (4 * pos_ref[1] + pos_ref[0]) * SHARE
        column = lax.broadcasted_iota(jnp.int32, shape, 1)
        mine_ref[:SHARE, :] += jnp.where(row == column, damping_ref[...], 0.0)


def late_gram(total, pos, damping, early, features, halves):
    rows, columns = features.shape
    return pl.pallas_call(
        functools.partial(late_gram_kernel, total),
        out_shape=[jax.ShapeDtypeStruct((columns // 2, P_SIZE), F32)] * 2,
        in_specs=[SMEM] + [VMEM] * 7,
        out_specs=[VMEM] * 2,
        scratch_shapes=[pltpu.VMEM(early.shape, F32)],
        compiler_params=params(16),
        cost_estimate=pl.CostEstimate(flops=6 * features.size * 256, bytes_accessed=8 * features.size, transcendentals=0),
    )(pos, damping[None, :], early, features, *halves)


def factor_kernel(damped_ref, last_ref, inverse_ref, factor_ref):
    size = inverse_ref.shape[0]
    wide = 4 * SHARE
    damped = split(damped_ref[...] + last_ref[...])
    for k in range(size // wide):
        at, upto = slice(wide * k, wide * (k + 1)), slice(0, wide * (k + 1))
        factor_ref[:, at] = dot3(tuple(part[:, upto] for part in damped), split(inverse_ref[at, upto]), (1, 1))


def factor_product(damped, last, inverse):
    return pl.pallas_call(
        factor_kernel,
        out_shape=jax.ShapeDtypeStruct(damped.shape, F32),
        in_specs=[VMEM] * 3,
        out_specs=VMEM,
        compiler_params=params(16),
        cost_estimate=pl.CostEstimate(flops=4 * damped.size * P_SIZE, bytes_accessed=12 * damped.size, transcendentals=0),
    )(damped, last, inverse)


def weights_kernel(pos_ref, inverse_ref, *refs):
    tests, (weights_ref, mixed_ref, tests_ref, solved_ref) = refs[:4], refs[4:]
    size = inverse_ref.shape[0]
    wide = 4 * SHARE
    blocks = size // wide
    for distance, block in enumerate(tests):
        first = (pos_ref[3] + 2 * distance) % 8
        columns = block.shape[2]
        for i, place in enumerate((first, first + 1 - 2 * pos_ref[2])):
            tests_ref[:, pl.ds(pl.multiple_of(place * columns, columns), columns)] = block[i]
    for k in range(blocks):
        at, upto = slice(wide * k, wide * (k + 1)), slice(0, wide * (k + 1))
        solved_ref[:, at] = dot3(split(tests_ref[:, upto]), split(inverse_ref[at, upto]), (1, 1))
    for k in range(blocks):
        at, after = slice(wide * k, wide * (k + 1)), slice(wide * k, size)
        weights_ref[:, at] = dot3(split(solved_ref[:, after]), split(inverse_ref[after, at])) * (1.0 / math.sqrt(size))
    weights = weights_ref[...]
    for x in range(4):
        parts = [weights[:, wide * z + SHARE * x : wide * z + SHARE * (x + 1)] for z in range(4)]
        mixed_ref[:, wide * x : wide * (x + 1)] = jnp.concatenate(parts, axis=1)


def weights_product(pos, inverse, tests):
    size = inverse.shape[0]
    count = tests[0].shape[1]
    weights = jax.ShapeDtypeStruct((count, size), F32)
    return pl.pallas_call(
        weights_kernel,
        out_shape=[weights] * 2,
        in_specs=[SMEM] + [VMEM] * 5,
        out_specs=[VMEM] * 2,
        scratch_shapes=[pltpu.VMEM((count, size), F32)] * 2,
        compiler_params=params(16),
        cost_estimate=pl.CostEstimate(flops=6 * size * size * count, bytes_accessed=8 * size * size, transcendentals=0),
    )(pos, inverse, *tests)


def scores_columns(ring, distances, pos_ref, weights_ref, pieces, scores_ref, total_ref, sems):
    wide = 4 * SHARE
    examples = pieces[0].shape[2]
    whole = [piece[...].reshape(wide, examples) for piece in pieces[: len(distances)]]
    whole.append(jnp.concatenate([part[...] for part in pieces[len(distances) :]], axis=0).reshape(wide, examples))
    places = [pl.multiple_of((pos_ref[1 - ring] + distance) % 4 * wide, wide) for distance in distances + (2,)]
    weights = [split(weights_ref[:, pl.ds(place, wide)]) for place in places]
    copies = []
    for k in range(examples // wide):
        at = slice(wide * k, wide * (k + 1))
        total = None
        for weight, piece in zip(weights, whole):
            part = dot3(weight, split(piece[:, at]))
            total = part if total is None else total + part
        total_ref[:, at] = total
        target = scores_ref.at[:, examples * ring + wide * k : examples * ring + wide * (k + 1)]
        copies.append(pltpu.make_async_copy(total_ref.at[:, at], target, sems.at[k]))
        copies[-1].start()
    return copies


def first_scores_kernel(distances, pos_ref, weights_ref, *refs):
    pieces, (scores_ref, total_ref, sems) = refs[: len(distances) + 2], refs[len(distances) + 2 :]
    for copy in scores_columns(0, distances, pos_ref, weights_ref, pieces, scores_ref, total_ref, sems):
        copy.wait()


def copy_rows(pos_ref, source_ref, core, to_ref, sems):
    half, parts = source_ref.shape[0], sems.shape[0]
    size = half // parts
    copies = []
    for i in range(parts):
        target = to_ref.at[pl.ds(pl.multiple_of(core * half + size * i, size), size)]
        copies.append(pltpu.make_async_copy(source_ref.at[size * i : size * (i + 1)], target, sems.at[i]))
        copies[-1].start()
    return copies


def second_scores_kernel(distances, pos_ref, weights_ref, mine_ref, before_ref, *refs):
    del before_ref
    pieces, refs = refs[: len(distances) + 2], refs[len(distances) + 2 :]
    scores_ref, factor_ref, total_ref, sems, factor_sems = refs
    copies = copy_rows(pos_ref, mine_ref, pos_ref[2], factor_ref, factor_sems)
    copies += scores_columns(1, distances, pos_ref, weights_ref, pieces, scores_ref, total_ref, sems)
    for copy in copies:
        copy.wait()


def complete_kernel(pos_ref, other_ref, before_ref, factor_ref, sems):
    del before_ref
    for copy in copy_rows(pos_ref, other_ref, 1 - pos_ref[2], factor_ref, sems):
        copy.wait()


def complete(pos, other, before):
    return pl.pallas_call(
        complete_kernel,
        out_shape=jax.ShapeDtypeStruct(before.shape, F32),
        in_specs=[SMEM, VMEM, ANY],
        out_specs=ANY,
        input_output_aliases={2: 0},
        scratch_shapes=[pltpu.SemaphoreType.DMA((8,))],
        compiler_params=params(4),
        cost_estimate=pl.CostEstimate(flops=0, bytes_accessed=8 * other.size, transcendentals=0),
    )(pos, other, before)


def scores_scratch(weights, pieces):
    examples = pieces[0].shape[2]
    return [pltpu.VMEM((weights.shape[0], examples), F32), pltpu.SemaphoreType.DMA((examples // (4 * SHARE),))]


def first_scores(pos, weights, distances, pieces):
    return pl.pallas_call(
        functools.partial(first_scores_kernel, distances),
        out_shape=jax.ShapeDtypeStruct((weights.shape[0], 2 * pieces[0].shape[2]), F32),
        in_specs=[SMEM] + [VMEM] * (1 + len(pieces)),
        out_specs=ANY,
        scratch_shapes=scores_scratch(weights, pieces),
        compiler_params=params(16),
        cost_estimate=pl.CostEstimate(flops=6 * P_SIZE * P_SIZE * 256, bytes_accessed=4 * P_SIZE * P_SIZE, transcendentals=0),
    )(pos, weights, *pieces)


def second_scores(pos, weights, mine, before, distances, pieces):
    return pl.pallas_call(
        functools.partial(second_scores_kernel, distances),
        out_shape=[
            jax.ShapeDtypeStruct(before.shape, F32),
            jax.ShapeDtypeStruct((2 * mine.shape[0], mine.shape[1]), F32),
        ],
        in_specs=[SMEM] + [VMEM] * 2 + [ANY] + [VMEM] * len(pieces),
        out_specs=[ANY] * 2,
        input_output_aliases={3: 0},
        scratch_shapes=scores_scratch(weights, pieces) + [pltpu.SemaphoreType.DMA((2,))],
        compiler_params=params(16),
        cost_estimate=pl.CostEstimate(flops=6 * P_SIZE * P_SIZE * 256, bytes_accessed=4 * P_SIZE * P_SIZE, transcendentals=0),
    )(pos, weights, mine, before, *pieces)


def hop(axis, move):
    size = {"test": 16, "train": 8}[axis]
    return lambda value: lax.ppermute(value, axis, [(i, move(i)) for i in range(size)])


TO_X = {d: hop("test", lambda s, d=d: s // 4 * 4 + (s + d) % 4) for d in (1, 2, 3)}
TO_Z = {d: hop("test", lambda s, d=d: (s + 4 * d) % 16) for d in (1, 2, 3)}
TO_Y = {d: hop("train", lambda t, d=d: (t + 2 * d) % 8) for d in (1, 2, 3)}
SWAP_CORE = hop("train", lambda t: t ^ 1)
SWAP_Y1 = hop("train", lambda t: t ^ 2)
SWAP_Y2 = hop("train", lambda t: t ^ 4)


def ring(value, to):
    return [value, to[3](value), to[2](value), to[1](value)]


def relay(ahead, behind, to):
    upper, lower = cut(ahead, behind)
    return to[3](upper), to[1](lower)


def per_device(train_features, test_panel, damping):
    test, train = lax.axis_index("test"), lax.axis_index("train")
    pos = jnp.stack([test % 4, test // 4, train % 2, train]).astype(jnp.int32)
    rows_dev = train_features.shape[0]
    train_total = rows_dev * lax.axis_size("train")

    own_t = train_features[:, :SHARE].T
    first, second = own_t[:, : rows_dev // 2], own_t[:, rows_dev // 2 :]
    pos, first, second = lax.optimization_barrier((pos, first, second))
    own_row = arrange(pos, 0, ring(first, TO_X))
    own_column = arrange(pos, 1, ring(second, TO_Z))
    near_rows, near_columns = [TO_Z[3](own_row), TO_Z[1](own_row)], [TO_X[3](own_column), TO_X[1](own_column)]
    early = early_gram(pos, train_features, (0,), [own_row, own_column])
    early, test_panel = lax.optimization_barrier((early, test_panel))
    tests = ring(stack([test_panel, SWAP_CORE(test_panel)]), TO_Y)
    early, near_columns = lax.optimization_barrier((early, near_columns))
    far_rows, far_columns = relay(*near_rows, TO_Z), relay(*near_columns, TO_X)
    near = [near_rows[0], near_columns[0], near_rows[1], near_columns[1]]
    far = [*far_rows, *far_columns]
    early, strip = early_gram(pos, train_features, (1, 3), near, early)
    strip, tests = lax.optimization_barrier((strip, tests))

    strip, other_strip = strip_product(train_total, pos, damping, own_t, strip, far)
    strip = add(strip, SWAP_CORE(other_strip))
    strips = ring(strip, TO_Y)
    term, other_term = late_gram(train_total, pos, damping, early, train_features, far)
    strips, term, other_term = lax.optimization_barrier((strips, term, other_term))
    strip = sum_in_order(pos, strips)

    damped = add(term, SWAP_CORE(other_term))
    left, rest = order_strips(pos, ring(strip, TO_Z))
    left, damped = lax.optimization_barrier((left, damped))
    damped_y1 = SWAP_Y1(damped)
    mine = stack(ring(left, TO_X))
    mine, rest = lax.optimization_barrier((mine, rest))
    later = ring(rest, TO_X)
    first = first_factor(pos, mine, SWAP_CORE(mine))
    first, later, damped_y1 = lax.optimization_barrier((first, later, damped_y1))
    damped = add(damped, damped_y1)
    later = stack(later)
    later_other = SWAP_CORE(later)
    later, damped = lax.optimization_barrier((later, damped))
    damped_y2 = SWAP_Y2(damped)
    inverse = second_factor(pos, later, later_other, first)
    weights, mixed = weights_product(pos, inverse, tests)
    scores = first_scores(pos, weights, (0, 1, 3), [own_row, *near_rows, *far_rows])
    scores, damped, damped_y2 = lax.optimization_barrier((scores, damped, damped_y2))
    factor = factor_product(damped, damped_y2, inverse)
    other_factor = SWAP_CORE(factor)
    columns = [own_column, *near_columns, *far_columns]
    scores, rows = second_scores(pos, mixed, factor, scores, (0, 1, 3), columns)
    rows, other_factor = lax.optimization_barrier((rows, other_factor))
    return scores, complete(pos, other_factor, rows)


def solution(mesh):
    in_specs = (P("train", "test"), P("test", "train"), P())
    out_specs = (P("test", "train"), P("test", None))
    return jax.shard_map(
        per_device, mesh=mesh, in_specs=in_specs, out_specs=out_specs, check_vma=False
    )
```

```python
import functools
import math

import jax
import jax.numpy as jnp
from jax import lax
from jax.experimental import pallas as pl
from jax.experimental.pallas import tpu as pltpu
from jax.sharding import PartitionSpec as P

P_SIZE = 1024
BLOCK = 128
SHARE = 64
F32 = jnp.float32
BF16 = jnp.bfloat16
VMEM = pl.BlockSpec(memory_space=pltpu.VMEM)
SMEM = pl.BlockSpec(memory_space=pltpu.SMEM)
ANY = pl.BlockSpec(memory_space=pl.ANY)
SPREAD = pltpu.VMEM((2, 64, BLOCK), F32)


def params(mebibytes):
    return pltpu.CompilerParams(vmem_limit_bytes=mebibytes * 1024 * 1024)


def dot(a, b, contract=(1, 0)):
    return lax.dot_general(a, b, ((contract[:1], contract[1:]), ((), ())), preferred_element_type=F32)


def split(value):
    high = value.astype(BF16)
    return high, (value - high.astype(F32)).astype(BF16)


def dot3(a, b, contract=(1, 0)):
    return dot(a[0], b[0], contract) + (dot(a[0], b[1], contract) + dot(a[1], b[0], contract))


def split3(value):
    high, rest = split(value)
    return high, rest, (value - high.astype(F32) - rest.astype(F32)).astype(BF16)


def dot6(a, b, contract=(1, 0)):
    ca, cb = contract
    wide = jnp.concatenate([jnp.concatenate(b[:2], axis=cb), jnp.concatenate(b[1::-1], axis=cb)], axis=1 - cb)
    both = dot(jnp.concatenate(a[:2], axis=ca), wide, contract)
    small = dot(jnp.concatenate(a[::2], axis=ca), jnp.concatenate(b[2::-2], axis=cb), contract)
    half = both.shape[1] // 2
    return both[:, :half] + (both[:, half:] + small)


def factor_block(tiles, work, spread_ref):
    tiles = list(tiles)
    count = len(tiles)
    lane = lax.broadcasted_iota(jnp.int32, (8, BLOCK), 1)
    row = lax.broadcasted_iota(jnp.int32, (8, BLOCK), 0)
    share = -(-len(work) // count)

    def spread(value):
        return jnp.broadcast_to(value, (8, BLOCK))

    for group in range(count):
        first = 8 * group
        own = tiles[group]
        below = range(group + 1, count)
        columns = [spread(own[:, first + j : first + j + 1]) for j in range(8)]
        for j in range(8):
            spread_ref[group % 2, 8 * j : 8 * (j + 1), :] = columns[j]
        pivots = [[spread(spread_ref[group % 2, 8 * j + i : 8 * j + i + 1, :]) for j in range(i + 1)] for i in range(8)]
        inside = (lane >= first) & (lane < first + 8)
        own = jnp.where(inside, (lane - first == row).astype(F32), own)
        lines = [spread(own[i : i + 1, :]) for i in range(8)]
        factors = {m: [spread(tiles[m][:, first + j : first + j + 1]) for j in range(8)] for m in below}
        for m in below:
            tiles[m] = jnp.where(inside, 0.0, tiles[m])
        done = None
        for k in range(8):
            scale = lax.rsqrt(pivots[k][k])
            line = lines[k] * scale
            ratios = {i: pivots[i][k] * scale for i in range(k + 1, 8)}
            for i in range(k + 1, 8):
                for j in range(k + 1, i + 1):
                    pivots[i][j] = pivots[i][j] - ratios[i] * ratios[j]
                lines[i] = lines[i] - ratios[i] * line
            done = line if done is None else jnp.where(row == k, line, done)
            for m in below:
                factor = factors[m][k] * scale
                tiles[m] = tiles[m] - factor * line
                for i in range(k + 1, 8):
                    factors[m][i] = factors[m][i] - factor * ratios[i]
        tiles[group] = done
        for step in work[share * group : share * (group + 1)]:
            step()
    return [jnp.where(lane < 8 * group + 8, tiles[group], 0.0) for group in range(count)]


def blocks_at(i):
    return slice(BLOCK * i, BLOCK * (i + 1))


def factor_in_place(x_ref, spread_ref, extra):
    size = x_ref.shape[0]
    blocks = size // BLOCK
    at = blocks_at

    inverses, panels, rows = {}, {}, {}

    def inverse(k):
        if k not in inverses:
            inverses[k] = split3(x_ref[at(k), at(k)])
        return inverses[k]

    def finish_rows(k):
        left = x_ref[at(k), : BLOCK * k]
        left = dot6(inverse(k), split3(left))
        x_ref[at(k), : BLOCK * k] = left
        rows[k] = tuple(jnp.concatenate(parts, axis=1) for parts in zip(split3(left), inverse(k)))

    def column_panel(i, k):
        panels[i, k] = split3(dot6(split3(x_ref[at(i), at(k)]), inverse(k), (1, 1)))

    def update_right(i, j, k):
        x_ref[at(i), at(j)] -= dot6(panels[i, k], panels[j, k], (1, 1))

    def update_left(i, k):
        change = dot6(panels[i, k], rows[k] if k else inverse(k))
        if k:
            x_ref[at(i), : BLOCK * k] -= change[:, : BLOCK * k]
        x_ref[at(i), at(k)] = -change[:, BLOCK * k :]

    def clear_right(k):
        x_ref[at(k), BLOCK * (k + 1) :] = jnp.zeros((BLOCK, size - BLOCK * (k + 1)), F32)

    def later(k):
        work = [functools.partial(finish_rows, k)] if k else []
        work += [functools.partial(column_panel, i, k) for i in range(k + 2, blocks)]
        work += [functools.partial(update_right, i, j, k) for j in range(k + 1, blocks) for i in range(max(j, k + 2), blocks)]
        work += [functools.partial(update_left, i, k) for i in range(k + 1, blocks)]
        return work + [functools.partial(clear_right, k)]

    for k in range(blocks):
        work = []
        if k:
            column_panel(k, k - 1)
            update_right(k, k, k - 1)
            work = later(k - 1)
        tiles = [x_ref[BLOCK * k + 8 * m : BLOCK * k + 8 * (m + 1), at(k)] for m in range(BLOCK // 8)]
        for m, tile in enumerate(factor_block(tiles, work + extra(k), spread_ref)):
            x_ref[BLOCK * k + 8 * m : BLOCK * k + 8 * (m + 1), at(k)] = tile
    finish_rows(blocks - 1)


def place_strips(pos_ref, mine_ref, other_ref, to_ref):
    for distance in range(mine_ref.shape[0]):
        x = (pos_ref[0] + distance) % 4
        for z in range(mine_ref.shape[1]):
            for source, core in ((mine_ref, pos_ref[2]), (other_ref, 1 - pos_ref[2])):
                start = pl.multiple_of((4 * z + x) * SHARE + core * (SHARE // 2), SHARE // 2)
                to_ref[pl.ds(start, SHARE // 2), :] = source[distance, z]


def first_factor_kernel(pos_ref, mine_ref, other_ref, x_ref, spread_ref):
    half, quarter = mine_ref.shape[1], mine_ref.shape[2] // 3
    for distance in range(4):
        x = (pos_ref[0] + distance) % 4
        for source, core in ((mine_ref, pos_ref[2]), (other_ref, 1 - pos_ref[2])):
            start = pl.multiple_of(x * SHARE + core * half, half)
            x_ref[pl.ds(start, half), :quarter] = source[distance, :, :quarter]
            x_ref[pl.ds(start + 4 * SHARE, half), :] = source[distance, :, quarter:]
    factor_in_place(x_ref, spread_ref, lambda k: [])


def second_factor_kernel(pos_ref, mine_ref, other_ref, first_ref, out_ref, a_ref, x_ref, spread_ref):
    size = first_ref.shape[0]
    blocks = size // BLOCK
    place_strips(pos_ref, mine_ref, other_ref, a_ref)
    at = blocks_at
    wide = 2 * BLOCK

    chunks = range(size // wide)
    lefts, products, columns, factors = {}, {}, {}, {}

    def left(i):
        parts = []
        for k in chunks:
            upto = slice(0, wide * (k + 1))
            if k not in factors:
                factors[k] = split3(first_ref[wide * k : wide * (k + 1), upto])
            parts.append(dot6(split3(a_ref[at(i), upto]), factors[k], (1, 1)))
        lefts[i] = split3(jnp.concatenate(parts, axis=1))

    def remainder(i, j):
        whole = a_ref[at(i), size + BLOCK * j : size + BLOCK * (j + 1)]
        x_ref[at(i), at(j)] = whole - dot6(lefts[i], lefts[j], (1, 1))

    def product(i):
        parts = []
        for k in chunks:
            after = slice(wide * k, size)
            if k not in columns:
                columns[k] = split(first_ref[after, wide * k : wide * (k + 1)])
            parts.append(dot3(tuple(part[:, after] for part in lefts[i][:2]), columns[k]))
        products[i] = split(jnp.concatenate(parts, axis=1))

    def lower_left(i):
        done = tuple(jnp.concatenate([products[j][part] for j in range(i + 1)], axis=0) for part in range(2))
        lower = dot3(split(x_ref[at(i), : BLOCK * (i + 1)]), done)
        out_ref[size + BLOCK * i : size + BLOCK * (i + 1), :size] = -lower

    def upper(i):
        out_ref[at(i), :size] = first_ref[at(i), :]
        out_ref[at(i), size:] = jnp.zeros((BLOCK, size), F32)

    def extra(k):
        work = []
        if k == 0:
            work += [functools.partial(left, i) for i in range(1, blocks)]
            work += [functools.partial(remainder, i, j) for j in range(blocks) for i in range(max(j, 1), blocks)]
        else:
            work += [functools.partial(lower_left, k - 1)]
        work += [functools.partial(product, k)]
        return work + [functools.partial(upper, k)]

    left(0)
    remainder(0, 0)
    factor_in_place(x_ref, spread_ref, extra)
    lower_left(blocks - 1)
    out_ref[size:, size:] = x_ref[...]


def first_factor(pos, mine, other):
    size = mine.shape[2] // 3 * 2
    return pl.pallas_call(
        first_factor_kernel,
        out_shape=jax.ShapeDtypeStruct((size, size), F32),
        in_specs=[SMEM, VMEM, VMEM],
        out_specs=VMEM,
        scratch_shapes=[SPREAD],
        compiler_params=params(16),
        cost_estimate=pl.CostEstimate(flops=size * size, bytes_accessed=8 * size * size, transcendentals=size),
    )(pos, mine, other)


def second_factor(pos, mine, other, first):
    size = first.shape[0]
    return pl.pallas_call(
        second_factor_kernel,
        out_shape=jax.ShapeDtypeStruct((2 * size, 2 * size), F32),
        in_specs=[SMEM, VMEM, VMEM, VMEM],
        out_specs=VMEM,
        scratch_shapes=[pltpu.VMEM((size, 2 * size), F32), pltpu.VMEM((size, size), F32), SPREAD],
        compiler_params=params(24),
        cost_estimate=pl.CostEstimate(flops=size * size, bytes_accessed=8 * size * size, transcendentals=size),
    )(pos, mine, other, first)


def arrange_kernel(axis, pos_ref, *refs):
    for distance in range(4):
        refs[4][(pos_ref[axis] + distance) % 4] = refs[distance][...]


def arrange(pos, axis, blocks):
    block = blocks[0]
    return pl.pallas_call(
        functools.partial(arrange_kernel, axis),
        out_shape=jax.ShapeDtypeStruct((4,) + block.shape, F32),
        in_specs=[SMEM] + [VMEM] * 4,
        out_specs=VMEM,
        compiler_params=params(4),
        cost_estimate=pl.CostEstimate(flops=0, bytes_accessed=32 * block.size, transcendentals=0),
    )(pos, *blocks)


def cut_kernel(first_ref, second_ref, upper_ref, lower_ref):
    half = upper_ref.shape[0]
    upper_ref[...] = first_ref[:half]
    lower_ref[...] = second_ref[half:]


def cut(first, second):
    half = jax.ShapeDtypeStruct((first.shape[0] // 2,) + first.shape[1:], F32)
    return pl.pallas_call(
        cut_kernel,
        out_shape=[half] * 2,
        in_specs=[VMEM] * 2,
        out_specs=[VMEM] * 2,
        compiler_params=params(4),
        cost_estimate=pl.CostEstimate(flops=0, bytes_accessed=8 * first.size, transcendentals=0),
    )(first, second)


def order_strips_kernel(pos_ref, *refs):
    left_ref, rest_ref = refs[4:]
    quarter = left_ref.shape[1] // 3
    for distance in range(4):
        z = (pos_ref[1] + distance) % 4

        @pl.when(z == 0)
        def _(distance=distance):
            left_ref[:, :quarter] = refs[distance][:, :quarter]

        @pl.when(z == 1)
        def _(distance=distance):
            left_ref[:, quarter:] = refs[distance][:, : 2 * quarter]

        @pl.when(z >= 2)
        def _(distance=distance, z=z):
            rest_ref[z % 2] = refs[distance][...]


def order_strips(pos, strips):
    rows, columns = strips[0].shape
    return pl.pallas_call(
        order_strips_kernel,
        out_shape=[
            jax.ShapeDtypeStruct((rows, columns // 4 * 3), F32),
            jax.ShapeDtypeStruct((2, rows, columns), F32),
        ],
        in_specs=[SMEM] + [VMEM] * 4,
        out_specs=[VMEM] * 2,
        compiler_params=params(4),
        cost_estimate=pl.CostEstimate(flops=0, bytes_accessed=32 * rows * columns, transcendentals=0),
    )(pos, *strips)


def piece_rows(ring, place, z):
    if ring == 0:
        return pl.ds(pl.multiple_of(place * 4 * SHARE, 4 * SHARE), 4 * SHARE)
    return pl.ds(pl.multiple_of((4 * z + place) * SHARE, SHARE), SHARE)


def add_product(ring, place, product, to_ref):
    if ring == 0:
        to_ref[piece_rows(0, place, 0), :] += product
    else:
        for z in range(4):
            to_ref[piece_rows(1, place, z), :] += product[SHARE * z : SHARE * (z + 1), :]


def early_gram_kernel(distances, first, pos_ref, f_ref, *refs):
    count = 2 * len(distances)
    pieces, refs = refs[:count], refs[count:]
    examples = f_ref.shape[0] // 2
    if first:
        out_ref = refs[0]
        out_ref[...] = jnp.zeros_like(out_ref)
    else:
        before_ref, out_ref, strip_ref = refs
        out_ref[...] = before_ref[...]
    for ring in range(2):
        features = split(f_ref[examples * ring : examples * (ring + 1), :])
        for n, distance in enumerate(distances):
            product = dot3(split(pieces[2 * n + ring][...].reshape(4 * SHARE, examples)), features)
            add_product(ring, (pos_ref[1 - ring] + distance) % 4, product, out_ref)
    if not first:
        for i in range(out_ref.shape[0] // BLOCK):
            at = slice(BLOCK * i, BLOCK * (i + 1))
            strip_ref[:, at] = out_ref[at, :BLOCK].T[:SHARE]


def early_gram(pos, features, distances, pieces, before=None):
    columns = features.shape[1]
    total = jax.ShapeDtypeStruct((P_SIZE, columns), F32)
    strip = jax.ShapeDtypeStruct((SHARE, P_SIZE), F32)
    extra = () if before is None else (before,)
    return pl.pallas_call(
        functools.partial(early_gram_kernel, distances, before is None),
        out_shape=total if before is None else [total, strip],
        in_specs=[SMEM] + [VMEM] * (1 + len(pieces) + len(extra)),
        out_specs=VMEM if before is None else [VMEM, VMEM],
        compiler_params=params(16),
        cost_estimate=pl.CostEstimate(
            flops=6 * features.size * 4 * SHARE * len(distances), bytes_accessed=4 * features.size, transcendentals=0
        ),
    )(pos, features, *pieces, *extra)


def strip_kernel(total, pos_ref, damping_ref, own_ref, early_ref, *refs):
    halves, (mine_ref, other_ref, strip_ref) = refs[:4], refs[4:]
    wide = 4 * SHARE
    examples = own_ref.shape[1] // 2
    strip_ref[...] = early_ref[...]
    for ring in range(2):
        own = split(own_ref[:, examples * ring : examples * (ring + 1)])
        parts = [half[...].reshape(wide // 2, examples) for half in halves[2 * ring : 2 * ring + 2]]
        product = jnp.concatenate([dot3(own, split(part), (1, 1)) for part in parts], axis=1)
        place = (pos_ref[1 - ring] + 2) % 4
        if ring == 0:
            strip_ref[:, piece_rows(0, place, 0)] += product
        else:
            lane = lax.broadcasted_iota(jnp.int32, (SHARE, wide), 1)
            for z in range(4):
                part = jnp.concatenate([product[:, SHARE * z : SHARE * (z + 1)]] * 4, axis=1)
                strip_ref[:, wide * z : wide * (z + 1)] += jnp.where(lane // SHARE == place, part, 0.0)
    half = mine_ref.shape[0]
    start = pl.multiple_of(pos_ref[2] * half, half)
    row = lax.broadcasted_iota(jnp.int32, mine_ref.shape, 0) + (4 * pos_ref[1] + pos_ref[0]) * SHARE + start
    column = lax.broadcasted_iota(jnp.int32, mine_ref.shape, 1)
    damping = jnp.where((row == column) & (pos_ref[3] < 2), damping_ref[...], 0.0)
    mine_ref[...] = strip_ref[pl.ds(start, half), :] * (1.0 / total) + damping
    other_ref[...] = strip_ref[pl.ds(half - start, half), :] * (1.0 / total)


def strip_product(total, pos, damping, own_t, early, halves):
    return pl.pallas_call(
        functools.partial(strip_kernel, total),
        out_shape=[jax.ShapeDtypeStruct((SHARE // 2, P_SIZE), F32)] * 2,
        in_specs=[SMEM] + [VMEM] * 7,
        out_specs=[VMEM] * 2,
        scratch_shapes=[pltpu.VMEM(early.shape, F32)],
        compiler_params=params(12),
        cost_estimate=pl.CostEstimate(flops=24 * own_t.size * 256, bytes_accessed=16 * own_t.size, transcendentals=0),
    )(pos, damping[None, :], own_t, early, *halves)


def add_kernel(a_ref, b_ref, sum_ref):
    sum_ref[...] = a_ref[...] + b_ref[...]


def add(a, b):
    return pl.pallas_call(
        add_kernel,
        out_shape=jax.ShapeDtypeStruct(a.shape, F32),
        in_specs=[VMEM] * 2,
        out_specs=VMEM,
        compiler_params=params(4),
        cost_estimate=pl.CostEstimate(flops=a.size, bytes_accessed=12 * a.size, transcendentals=0),
    )(a, b)


def sum_in_order_kernel(pos_ref, *refs):
    parts_ref = refs[5]
    for distance in range(4):
        parts_ref[(pos_ref[3] // 2 + distance) % 4] = refs[distance][...]
    refs[4][...] = (parts_ref[0] + parts_ref[1]) + (parts_ref[2] + parts_ref[3])


def sum_in_order(pos, parts):
    shape = parts[0].shape
    return pl.pallas_call(
        sum_in_order_kernel,
        out_shape=jax.ShapeDtypeStruct(shape, F32),
        in_specs=[SMEM] + [VMEM] * 4,
        out_specs=VMEM,
        scratch_shapes=[pltpu.VMEM((4,) + shape, F32)],
        compiler_params=params(4),
        cost_estimate=pl.CostEstimate(flops=3 * parts[0].size, bytes_accessed=20 * parts[0].size, transcendentals=0),
    )(pos, *parts)


def stack_kernel(*refs):
    for i, ref in enumerate(refs[:-1]):
        refs[-1][i] = ref[...]


def stack(arrays):
    return pl.pallas_call(
        stack_kernel,
        out_shape=jax.ShapeDtypeStruct((len(arrays),) + arrays[0].shape, F32),
        in_specs=[VMEM] * len(arrays),
        out_specs=VMEM,
        compiler_params=params(4),
        cost_estimate=pl.CostEstimate(flops=0, bytes_accessed=32 * arrays[0].size, transcendentals=0),
    )(*arrays)


def late_gram_kernel(total, pos_ref, damping_ref, early_ref, f_ref, *refs):
    halves, (mine_ref, other_ref, sum_ref) = refs[:4], refs[4:]
    wide = 4 * SHARE
    examples = f_ref.shape[0] // 2
    half = mine_ref.shape[0]
    sum_ref[...] = early_ref[...]
    for ring in range(2):
        parts = [part[...].reshape(wide // 2, examples) for part in halves[2 * ring : 2 * ring + 2]]
        features = split(f_ref[examples * ring : examples * (ring + 1), :])
        product = dot3(split(jnp.concatenate(parts, axis=0)), features)
        add_product(ring, (pos_ref[1 - ring] + 2) % 4, product, sum_ref)
    for to_ref, core in ((mine_ref, pos_ref[2]), (other_ref, 1 - pos_ref[2])):
        columns = pl.ds(pl.multiple_of(core * half, half), half)
        for i in range(sum_ref.shape[0] // BLOCK):
            at = slice(BLOCK * i, BLOCK * (i + 1))
            to_ref[:, at] = sum_ref[at, columns].T * (1.0 / total)

    @pl.when(pos_ref[3] == 0)
    def _():
        shape = (SHARE, mine_ref.shape[1])
        row = lax.broadcasted_iota(jnp.int32, shape, 0) + (4 * pos_ref[1] + pos_ref[0]) * SHARE
        column = lax.broadcasted_iota(jnp.int32, shape, 1)
        mine_ref[:SHARE, :] += jnp.where(row == column, damping_ref[...], 0.0)


def late_gram(total, pos, damping, early, features, halves):
    rows, columns = features.shape
    return pl.pallas_call(
        functools.partial(late_gram_kernel, total),
        out_shape=[jax.ShapeDtypeStruct((columns // 2, P_SIZE), F32)] * 2,
        in_specs=[SMEM] + [VMEM] * 7,
        out_specs=[VMEM] * 2,
        scratch_shapes=[pltpu.VMEM(early.shape, F32)],
        compiler_params=params(16),
        cost_estimate=pl.CostEstimate(flops=6 * features.size * 256, bytes_accessed=8 * features.size, transcendentals=0),
    )(pos, damping[None, :], early, features, *halves)


def factor_kernel(damped_ref, last_ref, inverse_ref, factor_ref):
    size = inverse_ref.shape[0]
    wide = 4 * SHARE
    damped = split(damped_ref[...] + last_ref[...])
    for k in range(size // wide):
        at, upto = slice(wide * k, wide * (k + 1)), slice(0, wide * (k + 1))
        factor_ref[:, at] = dot3(tuple(part[:, upto] for part in damped), split(inverse_ref[at, upto]), (1, 1))


def factor_product(damped, last, inverse):
    return pl.pallas_call(
        factor_kernel,
        out_shape=jax.ShapeDtypeStruct(damped.shape, F32),
        in_specs=[VMEM] * 3,
        out_specs=VMEM,
        compiler_params=params(16),
        cost_estimate=pl.CostEstimate(flops=4 * damped.size * P_SIZE, bytes_accessed=12 * damped.size, transcendentals=0),
    )(damped, last, inverse)


def weights_kernel(pos_ref, inverse_ref, *refs):
    tests, (weights_ref, mixed_ref, tests_ref, solved_ref) = refs[:4], refs[4:]
    size = inverse_ref.shape[0]
    wide = 4 * SHARE
    blocks = size // wide
    for distance, block in enumerate(tests):
        first = (pos_ref[3] + 2 * distance) % 8
        columns = block.shape[2]
        for i, place in enumerate((first, first + 1 - 2 * pos_ref[2])):
            tests_ref[:, pl.ds(pl.multiple_of(place * columns, columns), columns)] = block[i]
    for k in range(blocks):
        at, upto = slice(wide * k, wide * (k + 1)), slice(0, wide * (k + 1))
        solved_ref[:, at] = dot3(split(tests_ref[:, upto]), split(inverse_ref[at, upto]), (1, 1))
    for k in range(blocks):
        at, after = slice(wide * k, wide * (k + 1)), slice(wide * k, size)
        weights_ref[:, at] = dot3(split(solved_ref[:, after]), split(inverse_ref[after, at])) * (1.0 / math.sqrt(size))
    weights = weights_ref[...]
    for x in range(4):
        parts = [weights[:, wide * z + SHARE * x : wide * z + SHARE * (x + 1)] for z in range(4)]
        mixed_ref[:, wide * x : wide * (x + 1)] = jnp.concatenate(parts, axis=1)


def weights_product(pos, inverse, tests):
    size = inverse.shape[0]
    count = tests[0].shape[1]
    weights = jax.ShapeDtypeStruct((count, size), F32)
    return pl.pallas_call(
        weights_kernel,
        out_shape=[weights] * 2,
        in_specs=[SMEM] + [VMEM] * 5,
        out_specs=[VMEM] * 2,
        scratch_shapes=[pltpu.VMEM((count, size), F32)] * 2,
        compiler_params=params(16),
        cost_estimate=pl.CostEstimate(flops=6 * size * size * count, bytes_accessed=8 * size * size, transcendentals=0),
    )(pos, inverse, *tests)


def scores_columns(ring, distances, pos_ref, weights_ref, pieces, scores_ref, total_ref, sems):
    wide = 4 * SHARE
    examples = pieces[0].shape[2]
    whole = [piece[...].reshape(wide, examples) for piece in pieces[: len(distances)]]
    whole.append(jnp.concatenate([part[...] for part in pieces[len(distances) :]], axis=0).reshape(wide, examples))
    places = [pl.multiple_of((pos_ref[1 - ring] + distance) % 4 * wide, wide) for distance in distances + (2,)]
    weights = split(jnp.concatenate([weights_ref[:, pl.ds(place, wide)] for place in places], axis=1))
    copies = []
    for k in range(examples // wide):
        at = slice(wide * k, wide * (k + 1))
        total_ref[:, at] = dot3(weights, split(jnp.concatenate([piece[:, at] for piece in whole], axis=0)))
        target = scores_ref.at[:, examples * ring + wide * k : examples * ring + wide * (k + 1)]
        copies.append(pltpu.make_async_copy(total_ref.at[:, at], target, sems.at[k]))
        copies[-1].start()
    return copies


def first_scores_kernel(distances, pos_ref, weights_ref, *refs):
    pieces, (scores_ref, total_ref, sems) = refs[: len(distances) + 2], refs[len(distances) + 2 :]
    for copy in scores_columns(0, distances, pos_ref, weights_ref, pieces, scores_ref, total_ref, sems):
        copy.wait()


def copy_rows(pos_ref, source_ref, core, to_ref, sems):
    half, parts = source_ref.shape[0], sems.shape[0]
    size = half // parts
    copies = []
    for i in range(parts):
        target = to_ref.at[pl.ds(pl.multiple_of(core * half + size * i, size), size)]
        copies.append(pltpu.make_async_copy(source_ref.at[size * i : size * (i + 1)], target, sems.at[i]))
        copies[-1].start()
    return copies


def second_scores_kernel(distances, pos_ref, weights_ref, mine_ref, before_ref, *refs):
    del before_ref
    pieces, refs = refs[: len(distances) + 2], refs[len(distances) + 2 :]
    scores_ref, factor_ref, total_ref, sems, factor_sems = refs
    copies = copy_rows(pos_ref, mine_ref, pos_ref[2], factor_ref, factor_sems)
    copies += scores_columns(1, distances, pos_ref, weights_ref, pieces, scores_ref, total_ref, sems)
    for copy in copies:
        copy.wait()


def complete_kernel(pos_ref, other_ref, before_ref, factor_ref, sems):
    del before_ref
    for copy in copy_rows(pos_ref, other_ref, 1 - pos_ref[2], factor_ref, sems):
        copy.wait()


def complete(pos, other, before):
    return pl.pallas_call(
        complete_kernel,
        out_shape=jax.ShapeDtypeStruct(before.shape, F32),
        in_specs=[SMEM, VMEM, ANY],
        out_specs=ANY,
        input_output_aliases={2: 0},
        scratch_shapes=[pltpu.SemaphoreType.DMA((8,))],
        compiler_params=params(4),
        cost_estimate=pl.CostEstimate(flops=0, bytes_accessed=8 * other.size, transcendentals=0),
    )(pos, other, before)


def scores_scratch(weights, pieces):
    examples = pieces[0].shape[2]
    return [pltpu.VMEM((weights.shape[0], examples), F32), pltpu.SemaphoreType.DMA((examples // (4 * SHARE),))]


def first_scores(pos, weights, distances, pieces):
    return pl.pallas_call(
        functools.partial(first_scores_kernel, distances),
        out_shape=jax.ShapeDtypeStruct((weights.shape[0], 2 * pieces[0].shape[2]), F32),
        in_specs=[SMEM] + [VMEM] * (1 + len(pieces)),
        out_specs=ANY,
        scratch_shapes=scores_scratch(weights, pieces),
        compiler_params=params(16),
        cost_estimate=pl.CostEstimate(flops=6 * P_SIZE * P_SIZE * 256, bytes_accessed=4 * P_SIZE * P_SIZE, transcendentals=0),
    )(pos, weights, *pieces)


def second_scores(pos, weights, mine, before, distances, pieces):
    return pl.pallas_call(
        functools.partial(second_scores_kernel, distances),
        out_shape=[
            jax.ShapeDtypeStruct(before.shape, F32),
            jax.ShapeDtypeStruct((2 * mine.shape[0], mine.shape[1]), F32),
        ],
        in_specs=[SMEM] + [VMEM] * 2 + [ANY] + [VMEM] * len(pieces),
        out_specs=[ANY] * 2,
        input_output_aliases={3: 0},
        scratch_shapes=scores_scratch(weights, pieces) + [pltpu.SemaphoreType.DMA((2,))],
        compiler_params=params(16),
        cost_estimate=pl.CostEstimate(flops=6 * P_SIZE * P_SIZE * 256, bytes_accessed=4 * P_SIZE * P_SIZE, transcendentals=0),
    )(pos, weights, mine, before, *pieces)


def hop(axis, move):
    size = {"test": 16, "train": 8}[axis]
    return lambda value: lax.ppermute(value, axis, [(i, move(i)) for i in range(size)])


TO_X = {d: hop("test", lambda s, d=d: s // 4 * 4 + (s + d) % 4) for d in (1, 2, 3)}
TO_Z = {d: hop("test", lambda s, d=d: (s + 4 * d) % 16) for d in (1, 2, 3)}
TO_Y = {d: hop("train", lambda t, d=d: (t + 2 * d) % 8) for d in (1, 2, 3)}
SWAP_CORE = hop("train", lambda t: t ^ 1)
SWAP_Y1 = hop("train", lambda t: t ^ 2)
SWAP_Y2 = hop("train", lambda t: t ^ 4)


def ring(value, to):
    return [value, to[3](value), to[2](value), to[1](value)]


def relay(ahead, behind, to):
    upper, lower = cut(ahead, behind)
    return to[3](upper), to[1](lower)


def per_device(train_features, test_panel, damping):
    test, train = lax.axis_index("test"), lax.axis_index("train")
    pos = jnp.stack([test % 4, test // 4, train % 2, train]).astype(jnp.int32)
    rows_dev = train_features.shape[0]
    train_total = rows_dev * lax.axis_size("train")

    own_t = train_features[:, :SHARE].T
    first, second = own_t[:, : rows_dev // 2], own_t[:, rows_dev // 2 :]
    pos, first, second = lax.optimization_barrier((pos, first, second))
    own_row = arrange(pos, 0, ring(first, TO_X))
    own_column = arrange(pos, 1, ring(second, TO_Z))
    near_rows, near_columns = [TO_Z[3](own_row), TO_Z[1](own_row)], [TO_X[3](own_column), TO_X[1](own_column)]
    early = early_gram(pos, train_features, (0,), [own_row, own_column])
    early, test_panel = lax.optimization_barrier((early, test_panel))
    tests = ring(stack([test_panel, SWAP_CORE(test_panel)]), TO_Y)
    early, near_columns = lax.optimization_barrier((early, near_columns))
    far_rows, far_columns = relay(*near_rows, TO_Z), relay(*near_columns, TO_X)
    near = [near_rows[0], near_columns[0], near_rows[1], near_columns[1]]
    far = [*far_rows, *far_columns]
    early, strip = early_gram(pos, train_features, (1, 3), near, early)
    strip, tests = lax.optimization_barrier((strip, tests))

    strip, other_strip = strip_product(train_total, pos, damping, own_t, strip, far)
    strip = add(strip, SWAP_CORE(other_strip))
    strips = ring(strip, TO_Y)
    term, other_term = late_gram(train_total, pos, damping, early, train_features, far)
    strips, term, other_term = lax.optimization_barrier((strips, term, other_term))
    strip = sum_in_order(pos, strips)

    damped = add(term, SWAP_CORE(other_term))
    left, rest = order_strips(pos, ring(strip, TO_Z))
    left, damped = lax.optimization_barrier((left, damped))
    damped_y1 = SWAP_Y1(damped)
    mine = stack(ring(left, TO_X))
    mine, rest = lax.optimization_barrier((mine, rest))
    later = ring(rest, TO_X)
    first = first_factor(pos, mine, SWAP_CORE(mine))
    first, later, damped_y1 = lax.optimization_barrier((first, later, damped_y1))
    damped = add(damped, damped_y1)
    later = stack(later)
    later_other = SWAP_CORE(later)
    later, damped = lax.optimization_barrier((later, damped))
    damped_y2 = SWAP_Y2(damped)
    inverse = second_factor(pos, later, later_other, first)
    weights, mixed = weights_product(pos, inverse, tests)
    scores = first_scores(pos, weights, (0, 1, 3), [own_row, *near_rows, *far_rows])
    scores, damped, damped_y2 = lax.optimization_barrier((scores, damped, damped_y2))
    factor = factor_product(damped, damped_y2, inverse)
    other_factor = SWAP_CORE(factor)
    columns = [own_column, *near_columns, *far_columns]
    scores, rows = second_scores(pos, mixed, factor, scores, (0, 1, 3), columns)
    rows, other_factor = lax.optimization_barrier((rows, other_factor))
    return scores, complete(pos, other_factor, rows)


def solution(mesh):
    in_specs = (P("train", "test"), P("test", "train"), P())
    out_specs = (P("test", "train"), P("test", None))
    return jax.shard_map(
        per_device, mesh=mesh, in_specs=in_specs, out_specs=out_specs, check_vma=False
    )
```
